128 devices in a mesh: leaf: 128 (over y, x, z, core).
Axes of the slice: x: 4, y: 4, z: 4, core: 2. Of those that a mesh axis runs over, the one named last changes fastest.
Arguments:
- rhs_solved: float32 [64, 524288], P(None, 'leaf'), may hold values from -6 to 6
- basis: float32 [4, 128, 524288], P(None, None, 'leaf'), may hold values from -0.03125 to 0.03125
- solved_gen: float32 [4, 128, 524288], P(None, None, 'leaf'), may hold values from -0.5 to 0.5
- capacitance: float32 [15, 256, 256], replicated, may hold values from -0.375 to 0.375
Outputs:
- solution: float32 [64, 524288], P(None, 'leaf')
The draws below stay inside these ranges and needn't reach their ends.
All inputs are finite; a program needn't handle non-finite values.
Results may differ from the reference program's by a relative error of at most 0.00021.
Values sent between devices are 32-bit elements; how exact they have to be, the bound alone decides.
No kernel may reach another device: no remote copies, remote signals or barrier semaphores. Data moves between devices by JAX's collectives and lax.ppermute only.
A program may use at most 128 MiB of HBM per device.

```python
import jax
import jax.numpy as jnp
from jax import lax

RANK = 128
RHS = 64
LEVELS = 4
NPTS = 524288
NODES = 15


def steps_of(stream_key, shape, pieces, least, top_value):
    def one(axis_at, shards_of):
        heights = jax.random.uniform(jax.random.fold_in(jax.random.fold_in(stream_key, 6), axis_at), (shards_of,), jnp.float32, least / len(pieces), top_value / len(pieces))
        return jnp.repeat(jnp.exp(heights), shape[axis_at] // shards_of).reshape((-1,) + (1,) * (len(shape) - axis_at - 1))

    gain = one(*pieces[0])
    for cut in pieces[1:]:
        gain = gain * one(*cut)
    return gain


def normal_values(key, shape, deviation, reach, pieces=(), dtype=jnp.bfloat16):
    values = jax.random.normal(key, shape, jnp.float32) * deviation
    if len(pieces) > 0:
        values = steps_of(key, shape, pieces, -0.22, 0.18) * values
    return jnp.clip(values, min=-reach, max=reach).astype(dtype)


def setup_inputs(seed: int = 0) -> dict:
    streams_of = jax.random.split(jax.random.key(seed), 5)
    return {
        "rhs_solved": normal_values(streams_of[0], (RHS, NPTS), 1.0, 6.0, ((1, 128),), jnp.float32),
        "basis": normal_values(streams_of[1], (LEVELS, RANK, NPTS), (NPTS // 16) ** -0.5, 0.03125, ((2, 128),), jnp.float32),
        "solved_gen": normal_values(streams_of[2], (LEVELS, RANK, NPTS), RANK ** -0.5, 0.5, ((2, 128),), jnp.float32),
        "capacitance": normal_values(streams_of[3], (NODES, 2 * RANK, 2 * RANK), (2 * RANK) ** -0.5, 0.375, (), jnp.float32),
    }


def reference(rhs_solved, basis, solved_gen, capacitance):
    highest = lax.Precision.HIGHEST
    current = rhs_solved
    for level in range(LEVELS - 1, -1, -1):
        children = 2 ** (level + 1)
        nodes = 2 ** level
        width = NPTS // children
        blocks = current.reshape(RHS, children, width)
        gens = basis[level].reshape(RANK, children, width)
        sgens = solved_gen[level].reshape(RANK, children, width)
        proj = jnp.einsum('hcp,rcp->chr', blocks, gens, precision=highest)
        first = proj[0::2]
        second = proj[1::2]
        joined = jnp.concatenate([second, first], axis=2)
        caps = capacitance[nodes - 1:2 * nodes - 1]
        coeff = jnp.einsum('nhk,nkl->nhl', joined, caps, precision=highest)
        parts = jnp.stack([coeff[:, :, :RANK], coeff[:, :, RANK:]], axis=1).reshape(children, RHS, RANK)
        update = jnp.einsum('chr,rcp->hcp', parts, sgens, precision=highest)
        current = (blocks - update).reshape(RHS, NPTS)
    return current
```

```python
import functools

import jax
import jax.numpy as jnp
from jax import lax
from jax.experimental import pallas as pl
from jax.experimental.pallas import tpu as pltpu
from jax.sharding import PartitionSpec as P

F32 = jnp.float32
BF16 = jnp.bfloat16
RANK = 128
RHS = 64
DEVICES = 128
CHUNK = 1024
ANY = pl.BlockSpec(memory_space=pl.ANY)
VMEM = pl.BlockSpec(memory_space=pltpu.VMEM)
SMEM = pl.BlockSpec(memory_space=pltpu.SMEM)

CORE = 1
Z_MASKS = (2, 6, 4)
X_MASKS = (8, 24, 16)
Y_MASKS = (32, 96, 64)


def split(value):
    high = value.astype(BF16)
    return high, (value - high.astype(F32)).astype(BF16)


def stacked(values):
    parts = [split(v) for v in values]
    return jnp.concatenate([h for h, _ in parts] + [l for _, l in parts], axis=0)


def product(left, right):
    lh, ll = split(left)
    rh, rl = split(right)
    rows = left.shape[0]
    both = jnp.dot(jnp.concatenate([lh, ll], axis=0), rh, preferred_element_type=F32)
    return both[:rows] + both[rows:] + jnp.dot(lh, rl, preferred_element_type=F32)


def contract(left, right):
    return lax.dot_general(left, right, (((1,), (1,)), ((), ())), preferred_element_type=F32)


def fold(total, rows):
    half = total.shape[1] // 2
    wide = total[:rows] + total[rows:]
    return wide[:, :half] + wide[:, half:]


def params(limit):
    return pltpu.CompilerParams(vmem_limit_bytes=limit)


def chunk_copies(sources, buffers, sems, points):
    copies = []
    for i in range(points // CHUNK):
        cols = pl.ds(i * CHUNK, CHUNK)
        row = []
        for j, (ref, level) in enumerate(sources):
            src = ref.at[:, cols] if level is None else ref.at[level, :, cols]
            row.append(pltpu.make_async_copy(src, buffers[j].at[:, cols], sems.at[i, j]))
        copies.append(row)
    return copies


def first_kernel(points, core_ref, rhs_ref, basis_ref, gen_ref, keep_ref, send_ref,
                 rhs_buf, v3_buf, v2_buf, u3_buf, acc2, acc3, sems):
    buffers = (rhs_buf, v3_buf, v2_buf, u3_buf)
    sources = ((rhs_ref, None), (basis_ref, 3), (basis_ref, 2), (gen_ref, 3))
    copies = chunk_copies(sources, buffers, sems, points)
    for row in copies:
        for copy in row:
            copy.start()
    for i, row in enumerate(copies):
        for copy in row:
            copy.wait()
        cols = pl.ds(i * CHUNK, CHUNK)
        rhs = stacked([rhs_buf[:, cols]])
        u3 = stacked([u3_buf[:, cols]])
        v3 = stacked([v3_buf[:, cols]])
        v2 = stacked([v2_buf[:, cols]])
        left = jnp.concatenate([rhs, u3], axis=0)
        two, three = contract(left, v2), contract(rhs, v3)
        if i == 0:
            acc2[...] = two
            acc3[...] = three
        else:
            acc2[...] += two
            acc3[...] += three
    p3 = fold(acc3[...], RHS)
    p2 = fold(acc2[: 2 * RHS], RHS)
    g32 = fold(acc2[2 * RHS :], RANK)
    first = core_ref[0] == 0

    @pl.when(first)
    def _():
        keep_ref[:RHS] = p3
        keep_ref[RHS:] = p2
        send_ref[...] = g32

    @pl.when(jnp.logical_not(first))
    def _():
        send_ref[:RHS] = p3
        send_ref[RHS:] = p2
        keep_ref[...] = g32


def first_step(core, rhs, basis, gen):
    points = rhs.shape[1]
    half = jax.ShapeDtypeStruct((RANK, RANK), F32)
    return pl.pallas_call(
        functools.partial(first_kernel, points),
        out_shape=(half, half),
        in_specs=[SMEM, ANY, ANY, ANY],
        out_specs=(VMEM, VMEM),
        scratch_shapes=[
            pltpu.VMEM((RHS, points), F32),
            pltpu.VMEM((RANK, points), F32),
            pltpu.VMEM((RANK, points), F32),
            pltpu.VMEM((RANK, points), F32),
            pltpu.VMEM((2 * (RHS + RANK), 2 * RANK), F32),
            pltpu.VMEM((2 * RHS, 2 * RANK), F32),
            pltpu.SemaphoreType.DMA((points // CHUNK, 4)),
        ],
        compiler_params=params(24 << 20),
        cost_estimate=pl.CostEstimate(flops=800_000_000, bytes_accessed=7_340_032, transcendentals=0),
        name="project_low",
    )(core, rhs, basis, gen)


def related(cap_ref, out_ref, sems, node, s, base, columns):
    copies = []
    for r, row in enumerate((1 - s, s)):
        for c, col in enumerate((s, 1 - s)[:columns]):
            copies.append(
                pltpu.make_async_copy(
                    cap_ref.at[node, pl.ds(pl.multiple_of(row * RANK, RANK), RANK), pl.ds(pl.multiple_of(col * RANK, RANK), RANK)],
                    out_ref.at[r * RANK : (r + 1) * RANK, c * RANK : (c + 1) * RANK],
                    sems.at[base + 2 * r + c],
                )
            )
    for copy in copies:
        copy.start()
    return copies


def grams_kernel(points, place_ref, rhs_ref, basis_ref, gen_ref, cap_ref,
                 p_ref, g_ref, g10_ref, c3a_ref, c3b_ref, c2_ref, c1a_ref, c1b_ref, c0_ref,
                 rhs_buf, v1_buf, v0_buf, u3_buf, u2_buf, u1_buf, acc1, acc0, sems, cap_sems):
    buffers = (rhs_buf, v1_buf, v0_buf, u3_buf, u2_buf, u1_buf)
    sources = ((rhs_ref, None), (basis_ref, 1), (basis_ref, 0), (gen_ref, 3), (gen_ref, 2), (gen_ref, 1))
    copies = chunk_copies(sources, buffers, sems, points)
    for row in copies:
        for copy in row:
            copy.start()
    s3, s2, s1, s0 = place_ref[0], place_ref[1], place_ref[2], place_ref[3]
    n3, n2, n1 = place_ref[4], place_ref[5], place_ref[6]
    caps = related(cap_ref, c3a_ref, cap_sems, 7 + n3, s3, 0, 2)
    caps += related(cap_ref, c3b_ref, cap_sems, 7 + (n3 ^ 1), s3, 4, 2)
    caps += related(cap_ref, c2_ref, cap_sems, 3 + n2, s2, 8, 1)
    caps += related(cap_ref, c1a_ref, cap_sems, 1 + n1, s1, 12, 2)
    caps += related(cap_ref, c1b_ref, cap_sems, 1 + (n1 ^ 1), s1, 16, 2)
    caps += related(cap_ref, c0_ref, cap_sems, 0, s0, 20, 1)
    for i, row in enumerate(copies):
        for copy in row:
            copy.wait()
        cols = pl.ds(i * CHUNK, CHUNK)
        rhs = stacked([rhs_buf[:, cols]])
        u3 = stacked([u3_buf[:, cols]])
        u2 = stacked([u2_buf[:, cols]])
        u1 = stacked([u1_buf[:, cols]])
        v1 = stacked([v1_buf[:, cols]])
        v0 = stacked([v0_buf[:, cols]])
        left1 = jnp.concatenate([rhs, u3, u2], axis=0)
        left0 = jnp.concatenate([rhs, u3, u2, u1], axis=0)
        one, zero = contract(left1, v1), contract(left0, v0)
        if i == 0:
            acc1[...] = one
            acc0[...] = zero
        else:
            acc1[...] += one
            acc0[...] += zero
    at3, at2, at1 = 2 * RHS, 2 * RHS + 2 * RANK, 2 * RHS + 4 * RANK
    p_ref[:, :RANK] = fold(acc1[:at3], RHS)
    p_ref[:, RANK:] = fold(acc0[:at3], RHS)
    g_ref[:RANK, :RANK] = fold(acc1[at3:at2], RANK)
    g_ref[:RANK, RANK:] = fold(acc0[at3:at2], RANK)
    g_ref[RANK:, :RANK] = fold(acc1[at2:at1], RANK)
    g_ref[RANK:, RANK:] = fold(acc0[at2:at1], RANK)
    g10_ref[...] = fold(acc0[at1:], RANK)
    for copy in caps:
        copy.wait()


def grams_step(place, rhs, basis, gen, cap):
    points = rhs.shape[1]

    def out(rows, cols):
        return jax.ShapeDtypeStruct((rows, cols), F32)

    wide = pltpu.VMEM((RANK, points), F32)
    rows1 = 2 * RHS + 4 * RANK
    return pl.pallas_call(
        functools.partial(grams_kernel, points),
        out_shape=(
            out(RHS, 2 * RANK), out(2 * RANK, 2 * RANK), out(RANK, RANK),
            out(2 * RANK, 2 * RANK), out(2 * RANK, 2 * RANK), out(2 * RANK, RANK),
            out(2 * RANK, 2 * RANK), out(2 * RANK, 2 * RANK), out(2 * RANK, RANK),
        ),
        in_specs=[SMEM, ANY, ANY, ANY, ANY],
        out_specs=(VMEM,) * 9,
        scratch_shapes=[
            pltpu.VMEM((RHS, points), F32), wide, wide, wide, wide, wide,
            pltpu.VMEM((rows1, 2 * RANK), F32),
            pltpu.VMEM((rows1 + 2 * RANK, 2 * RANK), F32),
            pltpu.SemaphoreType.DMA((points // CHUNK, 6)),
            pltpu.SemaphoreType.DMA((24,)),
        ],
        compiler_params=params(32 << 20),
        cost_estimate=pl.CostEstimate(flops=3_000_000_000, bytes_accessed=11_534_336, transcendentals=0),
        name="grams_high",
    )(place, rhs, basis, gen, cap)


def middle_kernel(core_ref, mine_ref, other_ref, c3a_ref, c3b_ref, c2_ref, p_ref, g_ref, g10_ref,
                  t_ref, keep_ref, send_ref):
    first = core_ref[0] == 0
    p, g = [], []
    for m in range(4):
        mine, other = mine_ref[m], other_ref[m]
        p.append(jnp.where(first, mine, other))
        g.append(jnp.where(first, other, mine))
    t = []
    for pair, cap in ((0, c3a_ref), (2, c3b_ref)):
        joined = jnp.concatenate([p[pair][:RHS], p[pair + 1][:RHS]], axis=1)
        both = product(joined, cap[...])
        t += [both[:, :RANK], both[:, RANK:]]
    q2 = [p[m][RHS:] - product(t[m], g[m]) for m in range(4)]
    joined = jnp.concatenate([q2[0] + q2[1], q2[2] + q2[3]], axis=1)
    coeff = jnp.concatenate([t[0], product(joined, c2_ref[...])], axis=1)
    t_ref[...] = coeff
    q = p_ref[...] - product(coeff, g_ref[...])
    half = RHS // 2

    def put(ref, c):
        rows = slice(c * half, (c + 1) * half)
        ref[:half] = q[rows, :RANK]
        ref[half : 2 * half] = q[rows, RANK:]
        ref[2 * half :] = g10_ref[c * RHS : (c + 1) * RHS]

    @pl.when(first)
    def _():
        put(keep_ref, 0)
        put(send_ref, 1)

    @pl.when(jnp.logical_not(first))
    def _():
        put(keep_ref, 1)
        put(send_ref, 0)


def middle_step(core, mine, other, c3a, c3b, c2, p, g, g10):
    half = jax.ShapeDtypeStruct((RANK, RANK), F32)
    return pl.pallas_call(
        middle_kernel,
        out_shape=(jax.ShapeDtypeStruct((RHS, 2 * RANK), F32), half, half),
        in_specs=[SMEM] + [VMEM] * 8,
        out_specs=(VMEM,) * 3,
        compiler_params=params(16 << 20),
        cost_estimate=pl.CostEstimate(flops=120_000_000, bytes_accessed=1_500_000, transcendentals=0),
        name="coefficients_low",
    )(core, mine, other, c3a, c3b, c2, p, g, g10)


def apply_chunks(points, levels, coeff, cur_ref, gen_ref, out_ref, cur_buf, hi_buf, lo_buf, sems, out_sems, compute):
    sources = ((cur_ref, None), (gen_ref, levels[0]), (gen_ref, levels[1]))
    copies = chunk_copies(sources, (cur_buf, hi_buf, lo_buf), sems, points)
    for row in copies:
        for copy in row:
            copy.start()
    th, tl = split(compute() if coeff is None else coeff)
    left = jnp.concatenate([th, tl], axis=0)
    outs = []
    for i, row in enumerate(copies):
        for copy in row:
            copy.wait()
        cols = pl.ds(i * CHUNK, CHUNK)
        gens = jnp.concatenate([hi_buf[:, cols], lo_buf[:, cols]], axis=0)
        gh, gl = split(gens)
        both = jnp.dot(left, gh, preferred_element_type=F32)
        update = both[:RHS] + both[RHS:] + jnp.dot(th, gl, preferred_element_type=F32)
        cur_buf[:, cols] = cur_buf[:, cols] - update
        copy = pltpu.make_async_copy(cur_buf.at[:, cols], out_ref.at[:, cols], out_sems.at[i])
        copy.start()
        outs.append(copy)
    for copy in outs:
        copy.wait()


def apply_scratch(points):
    wide = pltpu.VMEM((RANK, points), F32)
    return [
        pltpu.VMEM((RHS, points), F32), wide, wide,
        pltpu.SemaphoreType.DMA((points // CHUNK, 3)),
        pltpu.SemaphoreType.DMA((points // CHUNK,)),
    ]


def low_update_kernel(points, t_ref, cur_ref, gen_ref, out_ref, *scratch):
    apply_chunks(points, (3, 2), t_ref[...], cur_ref, gen_ref, out_ref, *scratch, None)


def low_update(t, rhs, gen):
    points = rhs.shape[1]
    return pl.pallas_call(
        functools.partial(low_update_kernel, points),
        out_shape=jax.ShapeDtypeStruct(rhs.shape, F32),
        in_specs=[VMEM, ANY, ANY],
        out_specs=ANY,
        scratch_shapes=apply_scratch(points),
        compiler_params=params(16 << 20),
        cost_estimate=pl.CostEstimate(flops=402_653_184, bytes_accessed=6_291_456, transcendentals=0),
        name="update_low",
    )(t, rhs, gen)


def last_kernel(points, core_ref, mine_ref, other_ref, c1a_ref, c1b_ref, c0_ref, cur_ref, gen_ref, out_ref, *scratch):
    def compute():
        first = core_ref[0] == 0
        half = RHS // 2
        q1, q0, g = [], [], []
        for m in range(4):
            mine, other = mine_ref[m], other_ref[m]
            low = jnp.where(first, mine, other)
            high = jnp.where(first, other, mine)
            q1.append(jnp.concatenate([low[:half], high[:half]], axis=0))
            q0.append(jnp.concatenate([low[half:RHS], high[half:RHS]], axis=0))
            g.append(jnp.concatenate([low[RHS:], high[RHS:]], axis=0))
        t = []
        for pair, cap in ((0, c1a_ref), (2, c1b_ref)):
            both = product(jnp.concatenate([q1[pair], q1[pair + 1]], axis=1), cap[...])
            t += [both[:, :RANK], both[:, RANK:]]
        r = [q0[m] - product(t[m], g[m]) for m in range(4)]
        joined = jnp.concatenate([r[0] + r[1], r[2] + r[3]], axis=1)
        return jnp.concatenate([t[0], product(joined, c0_ref[...])], axis=1)

    apply_chunks(points, (1, 0), None, cur_ref, gen_ref, out_ref, *scratch, compute)


def last_step(core, mine, other, c1a, c1b, c0, cur, gen):
    points = cur.shape[1]
    return pl.pallas_call(
        functools.partial(last_kernel, points),
        out_shape=jax.ShapeDtypeStruct(cur.shape, F32),
        in_specs=[SMEM] + [VMEM] * 5 + [ANY, ANY],
        out_specs=ANY,
        scratch_shapes=apply_scratch(points),
        compiler_params=params(16 << 20),
        cost_estimate=pl.CostEstimate(flops=500_000_000, bytes_accessed=7_000_000, transcendentals=0),
        name="update_high",
    )(core, mine, other, c1a, c1b, c0, cur, gen)


def swap(value, even, odd):
    pairs = [(i, i ^ (odd if i & CORE else even)) for i in range(DEVICES)]
    return lax.ppermute(value, "leaf", pairs)


def gathered(value, even, odd):
    one, three, two = (swap(value, e, o) for e, o in zip(even, odd))
    return value, one, two, three


def body(rhs, basis, gen, cap):
    device = lax.axis_index("leaf").astype(jnp.int32)
    core = (device & 1).reshape(1)
    place = jnp.stack([
        device >> 3 & 1, device >> 4 & 1, device >> 5 & 1, device >> 6 & 1,
        device >> 4, device >> 5, device >> 6,
    ])
    keep, send = first_step(core, rhs, basis, gen)
    p, g, g10, c3a, c3b, c2, c1a, c1b, c0 = grams_step(place, rhs, basis, gen, cap)
    chip = keep + swap(send, CORE, CORE)
    a, b, c, d = gathered(chip, Z_MASKS, Z_MASKS)
    line = a + b + c + d
    lines = jnp.stack(gathered(line, X_MASKS, X_MASKS))
    other = swap(lines, CORE, CORE)
    t, keep, send = middle_step(core, lines, other, c3a, c3b, c2, p, g, g10)
    current = low_update(t, rhs, gen)
    chip = keep + swap(send, CORE, CORE)
    a, b, c, d = gathered(chip, X_MASKS, Z_MASKS)
    part = a + b + c + d
    a, b, c, d = gathered(part, Z_MASKS, X_MASKS)
    plane = a + b + c + d
    planes = jnp.stack(gathered(plane, Y_MASKS, Y_MASKS))
    other = swap(planes, CORE, CORE)
    return last_step(core, planes, other, c1a, c1b, c0, current, gen)


def solution(mesh):
    in_specs = (P(None, "leaf"), P(None, None, "leaf"), P(None, None, "leaf"), P())
    return jax.shard_map(body, mesh=mesh, in_specs=in_specs, out_specs=P(None, "leaf"), check_vma=False)
```

```python
import functools

import jax
import jax.numpy as jnp
from jax import lax
from jax.experimental import pallas as pl
from jax.experimental.pallas import tpu as pltpu
from jax.sharding import PartitionSpec as P

F32 = jnp.float32
BF16 = jnp.bfloat16
RANK = 128
RHS = 64
DEVICES = 128
CHUNK = 1024
FULL = 53 << 20
BIG = 51 << 20
SMALL = 16 << 20
ANY = pl.BlockSpec(memory_space=pl.ANY)
HBM = pl.BlockSpec(memory_space=pltpu.HBM)
VMEM = pl.BlockSpec(memory_space=pltpu.VMEM)
SMEM = pl.BlockSpec(memory_space=pltpu.SMEM)

CORE = 1
Z_MASKS = (2, 6, 4)
X_MASKS = (8, 24, 16)
Y_MASKS = (32, 96, 64)


def split(value):
    high = value.astype(BF16)
    return high, (value - high.astype(F32)).astype(BF16)


def stacked(values):
    parts = [split(v) for v in values]
    return jnp.concatenate([h for h, _ in parts] + [l for _, l in parts], axis=0)


def product(left, right):
    lh, ll = split(left)
    rh, rl = split(right)
    rows = left.shape[0]
    both = jnp.dot(jnp.concatenate([lh, ll], axis=0), rh, preferred_element_type=F32)
    return both[:rows] + both[rows:] + jnp.dot(lh, rl, preferred_element_type=F32)


def contract(left, right):
    return lax.dot_general(left, right, (((1,), (1,)), ((), ())), preferred_element_type=F32)


def fold(total, rows):
    half = total.shape[1] // 2
    wide = total[:rows] + total[rows:]
    return wide[:, :half] + wide[:, half:]


def params(limit):
    return pltpu.CompilerParams(vmem_limit_bytes=limit)


def chunk_copies(sources, buffers, sems, points):
    copies = []
    for i in range(points // CHUNK):
        cols = pl.ds(i * CHUNK, CHUNK)
        row = []
        for j, (ref, level) in enumerate(sources):
            src = ref.at[:, cols] if level is None else ref.at[level, :, cols]
            row.append(pltpu.make_async_copy(src, buffers[j].at[:, cols], sems.at[i, j]))
        copies.append(row)
    return copies


def first_kernel(points, core_ref, rhs_ref, basis_ref, gen_ref, keep_ref, send_ref,
                 rhs_buf, v3_buf, v2_buf, u3_buf, acc2, acc3, sems):
    buffers = (rhs_buf, v3_buf, v2_buf, u3_buf)
    sources = ((rhs_ref, None), (basis_ref, 3), (basis_ref, 2), (gen_ref, 3))
    copies = chunk_copies(sources, buffers, sems, points)
    for row in copies:
        for copy in row:
            copy.start()
    for i, row in enumerate(copies):
        for copy in row:
            copy.wait()
        cols = pl.ds(i * CHUNK, CHUNK)
        rhs = stacked([rhs_buf[:, cols]])
        u3 = stacked([u3_buf[:, cols]])
        v3 = stacked([v3_buf[:, cols]])
        v2 = stacked([v2_buf[:, cols]])
        left = jnp.concatenate([rhs, u3], axis=0)
        two, three = contract(left, v2), contract(rhs, v3)
        if i == 0:
            acc2[...] = two
            acc3[...] = three
        else:
            acc2[...] += two
            acc3[...] += three
    p3 = fold(acc3[...], RHS)
    p2 = fold(acc2[: 2 * RHS], RHS)
    g32 = fold(acc2[2 * RHS :], RANK)
    first = core_ref[0] == 0

    @pl.when(first)
    def _():
        keep_ref[:RHS] = p3
        keep_ref[RHS:] = p2
        send_ref[...] = g32

    @pl.when(jnp.logical_not(first))
    def _():
        send_ref[:RHS] = p3
        send_ref[RHS:] = p2
        keep_ref[...] = g32


def first_step(core, rhs, basis, gen):
    points = rhs.shape[1]
    half = jax.ShapeDtypeStruct((RANK, RANK), F32)
    return pl.pallas_call(
        functools.partial(first_kernel, points),
        out_shape=(half, half),
        in_specs=[SMEM, HBM, HBM, HBM],
        out_specs=(VMEM, VMEM),
        scratch_shapes=[
            pltpu.VMEM((RHS, points), F32),
            pltpu.VMEM((RANK, points), F32),
            pltpu.VMEM((RANK, points), F32),
            pltpu.VMEM((RANK, points), F32),
            pltpu.VMEM((2 * (RHS + RANK), 2 * RANK), F32),
            pltpu.VMEM((2 * RHS, 2 * RANK), F32),
            pltpu.SemaphoreType.DMA((points // CHUNK, 4)),
        ],
        compiler_params=params(FULL),
        cost_estimate=pl.CostEstimate(flops=800_000_000, bytes_accessed=7_340_032, transcendentals=0),
        name="project_low",
    )(core, rhs, basis, gen)


def related(cap_ref, out_ref, sems, node, s, base, columns):
    copies = []
    for r, row in enumerate((1 - s, s)):
        for c, col in enumerate((s, 1 - s)[:columns]):
            copies.append(
                pltpu.make_async_copy(
                    cap_ref.at[node, pl.ds(pl.multiple_of(row * RANK, RANK), RANK), pl.ds(pl.multiple_of(col * RANK, RANK), RANK)],
                    out_ref.at[r * RANK : (r + 1) * RANK, c * RANK : (c + 1) * RANK],
                    sems.at[base + 2 * r + c],
                )
            )
    for copy in copies:
        copy.start()
    return copies


def grams_kernel(points, rhs_ref, basis_ref, gen_ref, sent_ref, sent_out, p_ref, g_ref,
                 rhs_buf, v1_buf, v0_buf, u3_buf, acc1, acc0, sems):
    buffers = (rhs_buf, v1_buf, v0_buf, u3_buf)
    sources = ((rhs_ref, None), (basis_ref, 1), (basis_ref, 0), (gen_ref, 3))
    copies = chunk_copies(sources, buffers, sems, points)
    for row in copies:
        for copy in row:
            copy.start()
    sent_out[...] = sent_ref[...]
    for i, row in enumerate(copies):
        for copy in row:
            copy.wait()
        cols = pl.ds(i * CHUNK, CHUNK)
        left = stacked([rhs_buf[:, cols], u3_buf[:, cols]])
        one, zero = contract(left, stacked([v1_buf[:, cols]])), contract(left, stacked([v0_buf[:, cols]]))
        if i == 0:
            acc1[...] = one
            acc0[...] = zero
        else:
            acc1[...] += one
            acc0[...] += zero
    for k, acc in enumerate((acc1, acc0)):
        both = fold(acc[...], RHS + RANK)
        p_ref[:, k * RANK : (k + 1) * RANK] = both[:RHS]
        g_ref[:, k * RANK : (k + 1) * RANK] = both[RHS:]


def grams_step(rhs, basis, gen, sent):
    points = rhs.shape[1]
    wide = pltpu.VMEM((RANK, points), F32)
    total = pltpu.VMEM((2 * (RHS + RANK), 2 * RANK), F32)
    return pl.pallas_call(
        functools.partial(grams_kernel, points),
        out_shape=(
            jax.ShapeDtypeStruct(sent.shape, F32),
            jax.ShapeDtypeStruct((RHS, 2 * RANK), F32),
            jax.ShapeDtypeStruct((RANK, 2 * RANK), F32),
        ),
        in_specs=[HBM, HBM, HBM, VMEM],
        out_specs=(VMEM,) * 3,
        scratch_shapes=[
            pltpu.VMEM((RHS, points), F32), wide, wide, wide, total, total,
            pltpu.SemaphoreType.DMA((points // CHUNK, 4)),
        ],
        compiler_params=params(FULL),
        cost_estimate=pl.CostEstimate(flops=1_500_000_000, bytes_accessed=7_340_032, transcendentals=0),
        name="grams_three",
    )(rhs, basis, gen, sent)


def rest_kernel(points, place_ref, basis_ref, gen_ref, cap_ref, sent_ref, sent_out,
                g_ref, g10_ref, c3a_ref, c3b_ref, c2_ref, c1a_ref, c1b_ref, c0_ref,
                v1_buf, v0_buf, u2_buf, u1_buf, acc1, acc0, sems, cap_sems):
    buffers = (v1_buf, v0_buf, u2_buf, u1_buf)
    sources = ((basis_ref, 1), (basis_ref, 0), (gen_ref, 2), (gen_ref, 1))
    copies = chunk_copies(sources, buffers, sems, points)
    for row in copies:
        for copy in row:
            copy.start()
    sent_out[...] = sent_ref[...]
    s3, s2, s1, s0 = place_ref[0], place_ref[1], place_ref[2], place_ref[3]
    n3, n2, n1 = place_ref[4], place_ref[5], place_ref[6]
    caps = related(cap_ref, c3a_ref, cap_sems, 7 + n3, s3, 0, 2)
    caps += related(cap_ref, c3b_ref, cap_sems, 7 + (n3 ^ 1), s3, 4, 2)
    caps += related(cap_ref, c2_ref, cap_sems, 3 + n2, s2, 8, 1)
    caps += related(cap_ref, c1a_ref, cap_sems, 1 + n1, s1, 12, 2)
    caps += related(cap_ref, c1b_ref, cap_sems, 1 + (n1 ^ 1), s1, 16, 2)
    caps += related(cap_ref, c0_ref, cap_sems, 0, s0, 20, 1)
    for i, row in enumerate(copies):
        for copy in row:
            copy.wait()
        cols = pl.ds(i * CHUNK, CHUNK)
        u2 = stacked([u2_buf[:, cols]])
        left = jnp.concatenate([u2, stacked([u1_buf[:, cols]])], axis=0)
        one, zero = contract(u2, stacked([v1_buf[:, cols]])), contract(left, stacked([v0_buf[:, cols]]))
        if i == 0:
            acc1[...] = one
            acc0[...] = zero
        else:
            acc1[...] += one
            acc0[...] += zero
    g_ref[:, :RANK] = fold(acc1[...], RANK)
    g_ref[:, RANK:] = fold(acc0[: 2 * RANK], RANK)
    g10_ref[...] = fold(acc0[2 * RANK :], RANK)
    for copy in caps:
        copy.wait()


def rest_step(place, basis, gen, cap, sent):
    points = basis.shape[2]

    def out(rows, cols):
        return jax.ShapeDtypeStruct((rows, cols), F32)

    wide = pltpu.VMEM((RANK, points), F32)
    return pl.pallas_call(
        functools.partial(rest_kernel, points),
        out_shape=(
            out(*sent.shape), out(RANK, 2 * RANK), out(RANK, RANK),
            out(2 * RANK, 2 * RANK), out(2 * RANK, 2 * RANK), out(2 * RANK, RANK),
            out(2 * RANK, 2 * RANK), out(2 * RANK, 2 * RANK), out(2 * RANK, RANK),
        ),
        in_specs=[SMEM, HBM, HBM, HBM, VMEM],
        out_specs=(VMEM,) * 9,
        scratch_shapes=[
            wide, wide, wide, wide,
            pltpu.VMEM((2 * RANK, 2 * RANK), F32),
            pltpu.VMEM((4 * RANK, 2 * RANK), F32),
            pltpu.SemaphoreType.DMA((points // CHUNK, 4)),
            pltpu.SemaphoreType.DMA((24,)),
        ],
        compiler_params=params(BIG),
        cost_estimate=pl.CostEstimate(flops=1_500_000_000, bytes_accessed=9_437_184, transcendentals=0),
        name="grams_rest",
    )(place, basis, gen, cap, sent)


def middle_kernel(core_ref, mine_ref, other_ref, c3a_ref, c3b_ref, c2_ref, p_ref, g3_ref, g2_ref, g10_ref,
                  t_ref, keep_ref, send_ref):
    first = core_ref[0] == 0
    p, g = [], []
    for m in range(4):
        mine, other = mine_ref[m], other_ref[m]
        p.append(jnp.where(first, mine, other))
        g.append(jnp.where(first, other, mine))
    t = []
    for pair, cap in ((0, c3a_ref), (2, c3b_ref)):
        joined = jnp.concatenate([p[pair][:RHS], p[pair + 1][:RHS]], axis=1)
        both = product(joined, cap[...])
        t += [both[:, :RANK], both[:, RANK:]]
    q2 = [p[m][RHS:] - product(t[m], g[m]) for m in range(4)]
    joined = jnp.concatenate([q2[0] + q2[1], q2[2] + q2[3]], axis=1)
    coeff = jnp.concatenate([t[0], product(joined, c2_ref[...])], axis=1)
    t_ref[...] = coeff
    q = p_ref[...] - product(coeff, jnp.concatenate([g3_ref[...], g2_ref[...]], axis=0))
    half = RHS // 2

    def put(ref, c):
        rows = slice(c * half, (c + 1) * half)
        ref[:half] = q[rows, :RANK]
        ref[half : 2 * half] = q[rows, RANK:]
        ref[2 * half :] = g10_ref[c * RHS : (c + 1) * RHS]

    @pl.when(first)
    def _():
        put(keep_ref, 0)
        put(send_ref, 1)

    @pl.when(jnp.logical_not(first))
    def _():
        put(keep_ref, 1)
        put(send_ref, 0)


def middle_step(core, mine, other, c3a, c3b, c2, p, g3, g2, g10):
    half = jax.ShapeDtypeStruct((RANK, RANK), F32)
    return pl.pallas_call(
        middle_kernel,
        out_shape=(jax.ShapeDtypeStruct((RHS, 2 * RANK), F32), half, half),
        in_specs=[SMEM] + [VMEM] * 9,
        out_specs=(VMEM,) * 3,
        compiler_params=params(SMALL),
        cost_estimate=pl.CostEstimate(flops=120_000_000, bytes_accessed=1_500_000, transcendentals=0),
        name="coefficients_low",
    )(core, mine, other, c3a, c3b, c2, p, g3, g2, g10)


def apply_chunks(points, levels, coeff, cur_ref, gen_ref, out_ref, cur_buf, hi_buf, lo_buf, sems, out_sems, compute):
    sources = ((cur_ref, None), (gen_ref, levels[0]), (gen_ref, levels[1]))
    copies = chunk_copies(sources, (cur_buf, hi_buf, lo_buf), sems, points)
    for row in copies:
        for copy in row:
            copy.start()
    th, tl = split(compute() if coeff is None else coeff)
    left = jnp.concatenate([th, tl], axis=0)
    outs = []
    for i, row in enumerate(copies):
        for copy in row:
            copy.wait()
        cols = pl.ds(i * CHUNK, CHUNK)
        gens = jnp.concatenate([hi_buf[:, cols], lo_buf[:, cols]], axis=0)
        gh, gl = split(gens)
        both = jnp.dot(left, gh, preferred_element_type=F32)
        update = both[:RHS] + both[RHS:] + jnp.dot(th, gl, preferred_element_type=F32)
        cur_buf[:, cols] = cur_buf[:, cols] - update
        copy = pltpu.make_async_copy(cur_buf.at[:, cols], out_ref.at[:, cols], out_sems.at[i])
        copy.start()
        outs.append(copy)
    for copy in outs:
        copy.wait()


def apply_scratch(points):
    wide = pltpu.VMEM((RANK, points), F32)
    return [
        pltpu.VMEM((RHS, points), F32), wide, wide,
        pltpu.SemaphoreType.DMA((points // CHUNK, 3)),
        pltpu.SemaphoreType.DMA((points // CHUNK,)),
    ]


def low_update_kernel(points, t_ref, cur_ref, gen_ref, sent_ref, out_ref, sent_out, *scratch):
    sent_out[...] = sent_ref[...]
    apply_chunks(points, (3, 2), t_ref[...], cur_ref, gen_ref, out_ref, *scratch, None)


def low_update(t, rhs, gen, sent):
    points = rhs.shape[1]
    return pl.pallas_call(
        functools.partial(low_update_kernel, points),
        out_shape=(jax.ShapeDtypeStruct(rhs.shape, F32), jax.ShapeDtypeStruct(sent.shape, F32)),
        in_specs=[VMEM, HBM, HBM, VMEM],
        out_specs=(HBM, VMEM),
        scratch_shapes=apply_scratch(points),
        compiler_params=params(BIG),
        cost_estimate=pl.CostEstimate(flops=402_653_184, bytes_accessed=6_291_456, transcendentals=0),
        name="update_low",
    )(t, rhs, gen, sent)


def last_kernel(points, core_ref, mine_ref, other_ref, c1a_ref, c1b_ref, c0_ref, cur_ref, gen_ref, out_ref, *scratch):
    def compute():
        first = core_ref[0] == 0
        half = RHS // 2
        q1, q0, g = [], [], []
        for m in range(4):
            mine, other = mine_ref[m], other_ref[m]
            low = jnp.where(first, mine, other)
            high = jnp.where(first, other, mine)
            q1.append(jnp.concatenate([low[:half], high[:half]], axis=0))
            q0.append(jnp.concatenate([low[half:RHS], high[half:RHS]], axis=0))
            g.append(jnp.concatenate([low[RHS:], high[RHS:]], axis=0))
        t = []
        for pair, cap in ((0, c1a_ref), (2, c1b_ref)):
            both = product(jnp.concatenate([q1[pair], q1[pair + 1]], axis=1), cap[...])
            t += [both[:, :RANK], both[:, RANK:]]
        r = [q0[m] - product(t[m], g[m]) for m in range(4)]
        joined = jnp.concatenate([r[0] + r[1], r[2] + r[3]], axis=1)
        return jnp.concatenate([t[0], product(joined, c0_ref[...])], axis=1)

    apply_chunks(points, (1, 0), None, cur_ref, gen_ref, out_ref, *scratch, compute)


def last_step(core, mine, other, c1a, c1b, c0, cur, gen):
    points = cur.shape[1]
    return pl.pallas_call(
        functools.partial(last_kernel, points),
        out_shape=jax.ShapeDtypeStruct(cur.shape, F32),
        in_specs=[SMEM] + [VMEM] * 5 + [HBM, HBM],
        out_specs=HBM,
        scratch_shapes=apply_scratch(points),
        compiler_params=params(BIG),
        cost_estimate=pl.CostEstimate(flops=500_000_000, bytes_accessed=7_000_000, transcendentals=0),
        name="update_high",
    )(core, mine, other, c1a, c1b, c0, cur, gen)


def swap(value, even, odd):
    pairs = [(i, i ^ (odd if i & CORE else even)) for i in range(DEVICES)]
    return lax.ppermute(value, "leaf", pairs)


def gathered(value, even, odd):
    one, three, two = (swap(value, e, o) for e, o in zip(even, odd))
    return value, one, two, three


def body(rhs, basis, gen, cap):
    device = lax.axis_index("leaf").astype(jnp.int32)
    core = (device & 1).reshape(1)
    place = jnp.stack([
        device >> 3 & 1, device >> 4 & 1, device >> 5 & 1, device >> 6 & 1,
        device >> 4, device >> 5, device >> 6,
    ])
    keep, send = first_step(core, rhs, basis, gen)
    chip = keep + swap(send, CORE, CORE)
    _, b, c, d = gathered(chip, Z_MASKS, Z_MASKS)
    chip, p, g3 = grams_step(rhs, basis, gen, chip)
    line = chip + b + c + d
    _, b, c, d = gathered(line, X_MASKS, X_MASKS)
    line, g2, g10, c3a, c3b, c2, c1a, c1b, c0 = rest_step(place, basis, gen, cap, line)
    lines = jnp.stack([line, b, c, d])
    other = swap(lines, CORE, CORE)
    t, keep, send = middle_step(core, lines, other, c3a, c3b, c2, p, g3, g2, g10)
    chip = keep + swap(send, CORE, CORE)
    _, b, c, d = gathered(chip, X_MASKS, Z_MASKS)
    current, chip = low_update(t, rhs, gen, chip)
    part = chip + b + c + d
    a, b, c, d = gathered(part, Z_MASKS, X_MASKS)
    plane = a + b + c + d
    planes = jnp.stack(gathered(plane, Y_MASKS, Y_MASKS))
    other = swap(planes, CORE, CORE)
    return last_step(core, planes, other, c1a, c1b, c0, current, gen)


def solution(mesh):
    in_specs = (P(None, "leaf"), P(None, None, "leaf"), P(None, None, "leaf"), P())
    return jax.shard_map(body, mesh=mesh, in_specs=in_specs, out_specs=P(None, "leaf"), check_vma=False)
```

```python
import functools

import jax
import jax.numpy as jnp
from jax import lax
from jax.experimental import pallas as pl
from jax.experimental.pallas import tpu as pltpu
from jax.sharding import PartitionSpec as P

F32 = jnp.float32
BF16 = jnp.bfloat16
RANK = 128
RHS = 64
DEVICES = 128
LIMITS = (47, 44, 40, 41, 41, 43, 46)
HBM = pl.BlockSpec(memory_space=pltpu.HBM)
VMEM = pl.BlockSpec(memory_space=pltpu.VMEM)
SMEM = pl.BlockSpec(memory_space=pltpu.SMEM)

CORE = 1
Z_MASKS = (2, 6, 4)
X_MASKS = (8, 24, 16)
Y_MASKS = (32, 96, 64)


def split(value):
    high = value.astype(BF16)
    return high, (value - high.astype(F32)).astype(BF16)


def stacked(values):
    parts = [split(v) for v in values]
    return jnp.concatenate([h for h, _ in parts] + [l for _, l in parts], axis=0)


def product(left, right):
    lh, ll = split(left)
    rh, rl = split(right)
    rows = left.shape[0]
    both = jnp.dot(jnp.concatenate([lh, ll], axis=0), rh, preferred_element_type=F32)
    return both[:rows] + both[rows:] + jnp.dot(lh, rl, preferred_element_type=F32)


def contract(left, right):
    return lax.dot_general(left, right, (((1,), (1,)), ((), ())), preferred_element_type=F32)


def fold(total, rows):
    half = total.shape[1] // 2
    wide = total[:rows] + total[rows:]
    return wide[:, :half] + wide[:, half:]


def params(limit):
    return pltpu.CompilerParams(vmem_limit_bytes=limit << 20)


def spans(sizes, points):
    at = 0
    for size in sizes:
        yield pl.ds(at * points // 8, size * points // 8)
        at += size


def fetch(sources, sems, sizes, points):
    parts = []
    for i, cols in enumerate(spans(sizes, points)):
        row = []
        for j, (ref, level, buffer) in enumerate(sources):
            src = ref.at[:, cols] if level is None else ref.at[level, :, cols]
            row.append(pltpu.make_async_copy(src, buffer.at[:, cols], sems.at[i, j]))
        parts.append((cols, row))
    for _, row in parts:
        for copy in row:
            copy.start()
    return parts


def add_to(acc, value, first):
    if first:
        acc[...] = value
    else:
        acc[...] += value


LATE = (4, 2, 1, 1)
EARLY = (1, 1, 2, 4)


def first_kernel(points, core_ref, rhs_ref, basis_ref, gen_ref, keep_ref, send_ref, held_ref,
                 v3_buf, v2_buf, acc2, acc3, sems):
    rhs_buf, u3_buf = held_ref.at[:RHS], held_ref.at[RHS:]
    sources = ((rhs_ref, None, rhs_buf), (basis_ref, 3, v3_buf), (basis_ref, 2, v2_buf), (gen_ref, 3, u3_buf))
    for i, (cols, row) in enumerate(fetch(sources, sems, LATE, points)):
        for copy in row:
            copy.wait()
        rhs = stacked([rhs_buf[:, cols]])
        left = jnp.concatenate([rhs, stacked([u3_buf[:, cols]])], axis=0)
        add_to(acc2, contract(left, stacked([v2_buf[:, cols]])), i == 0)
        add_to(acc3, contract(rhs, stacked([v3_buf[:, cols]])), i == 0)
    p3 = fold(acc3[...], RHS)
    p2 = fold(acc2[: 2 * RHS], RHS)
    g32 = fold(acc2[2 * RHS :], RANK)
    first = core_ref[0] == 0

    @pl.when(first)
    def _():
        keep_ref[:RHS] = p3
        keep_ref[RHS:] = p2
        send_ref[...] = g32

    @pl.when(jnp.logical_not(first))
    def _():
        send_ref[:RHS] = p3
        send_ref[RHS:] = p2
        keep_ref[...] = g32


def array(*shape):
    return jax.ShapeDtypeStruct(shape, F32)


def first_step(core, rhs, basis, gen):
    points = rhs.shape[1]
    wide = pltpu.VMEM((RANK, points), F32)
    return pl.pallas_call(
        functools.partial(first_kernel, points),
        out_shape=(array(RANK, RANK), array(RANK, RANK), array(RHS + RANK, points)),
        in_specs=[SMEM, HBM, HBM, HBM],
        out_specs=(VMEM,) * 3,
        scratch_shapes=[
            wide, wide,
            pltpu.VMEM((2 * (RHS + RANK), 2 * RANK), F32),
            pltpu.VMEM((2 * RHS, 2 * RANK), F32),
            pltpu.SemaphoreType.DMA((len(LATE), 4)),
        ],
        compiler_params=params(LIMITS[0]),
        cost_estimate=pl.CostEstimate(flops=800_000_000, bytes_accessed=7_340_032, transcendentals=0),
        name="project_low",
    )(core, rhs, basis, gen)


def related(cap_ref, out_ref, sems, node, s, base, columns):
    copies = []
    for r, row in enumerate((1 - s, s)):
        for c, col in enumerate((s, 1 - s)[:columns]):
            copies.append(
                pltpu.make_async_copy(
                    cap_ref.at[node, pl.ds(pl.multiple_of(row * RANK, RANK), RANK), pl.ds(pl.multiple_of(col * RANK, RANK), RANK)],
                    out_ref.at[r * RANK : (r + 1) * RANK, c * RANK : (c + 1) * RANK],
                    sems.at[base + 2 * r + c],
                )
            )
    for copy in copies:
        copy.start()
    return copies


def grams_kernel(points, held_ref, basis_ref, sent_ref, sent_out, p_ref, g_ref, v1_buf, v0_buf,
                 acc1, acc0, sems):
    parts = fetch(((basis_ref, 1, v1_buf), (basis_ref, 0, v0_buf)), sems, EARLY, points)
    sent_out[...] = sent_ref[...]
    for i, (cols, row) in enumerate(parts):
        left = stacked([held_ref[:, cols]])
        for copy, buffer, acc in zip(row, (v1_buf, v0_buf), (acc1, acc0)):
            copy.wait()
            add_to(acc, contract(left, stacked([buffer[:, cols]])), i == 0)
    for k, acc in enumerate((acc1, acc0)):
        both = fold(acc[...], RHS + RANK)
        p_ref[:, k * RANK : (k + 1) * RANK] = both[:RHS]
        g_ref[:, k * RANK : (k + 1) * RANK] = both[RHS:]


def grams_step(held, basis, sent):
    points = held.shape[1]
    total = pltpu.VMEM((2 * (RHS + RANK), 2 * RANK), F32)
    return pl.pallas_call(
        functools.partial(grams_kernel, points),
        out_shape=(
            array(*sent.shape), array(RHS, 2 * RANK), array(RANK, 2 * RANK),
            array(RANK, points), array(RANK, points),
        ),
        in_specs=[VMEM, HBM, VMEM],
        out_specs=(VMEM,) * 5,
        scratch_shapes=[total, total, pltpu.SemaphoreType.DMA((len(EARLY), 2))],
        compiler_params=params(LIMITS[1]),
        cost_estimate=pl.CostEstimate(flops=1_500_000_000, bytes_accessed=7_340_032, transcendentals=0),
        name="grams_three",
    )(held, basis, sent)


def rest_kernel(points, place_ref, v1_ref, v0_ref, gen_ref, cap_ref, sent_ref, sent_out,
                g_ref, g10_ref, c3a_ref, c3b_ref, c2_ref, c1a_ref, c1b_ref, c0_ref, u2_buf, u1_buf,
                acc1, acc0, acc, sems, cap_sems):
    parts = fetch(((gen_ref, 2, u2_buf), (gen_ref, 1, u1_buf)), sems, EARLY, points)
    sent_out[...] = sent_ref[...]
    s3, s2, s1, s0 = place_ref[0], place_ref[1], place_ref[2], place_ref[3]
    n3, n2, n1 = place_ref[4], place_ref[5], place_ref[6]
    caps = related(cap_ref, c3a_ref, cap_sems, 7 + n3, s3, 0, 2)
    caps += related(cap_ref, c3b_ref, cap_sems, 7 + (n3 ^ 1), s3, 4, 2)
    caps += related(cap_ref, c2_ref, cap_sems, 3 + n2, s2, 8, 1)
    caps += related(cap_ref, c1a_ref, cap_sems, 1 + n1, s1, 12, 2)
    caps += related(cap_ref, c1b_ref, cap_sems, 1 + (n1 ^ 1), s1, 16, 2)
    caps += related(cap_ref, c0_ref, cap_sems, 0, s0, 20, 1)
    for i, (cols, row) in enumerate(parts):
        v1, v0 = stacked([v1_ref[:, cols]]), stacked([v0_ref[:, cols]])
        row[0].wait()
        u2 = stacked([u2_buf[:, cols]])
        add_to(acc1, contract(u2, v1), i == 0)
        add_to(acc0, contract(u2, v0), i == 0)
        row[1].wait()
        add_to(acc, contract(stacked([u1_buf[:, cols]]), v0), i == 0)
    g_ref[:, :RANK] = fold(acc1[...], RANK)
    g_ref[:, RANK:] = fold(acc0[...], RANK)
    g10_ref[...] = fold(acc[...], RANK)
    for copy in caps:
        copy.wait()


def rest_step(place, v1, v0, gen, cap, sent):
    points = v1.shape[1]
    square, column = array(2 * RANK, 2 * RANK), array(2 * RANK, RANK)
    total = pltpu.VMEM((2 * RANK, 2 * RANK), F32)
    return pl.pallas_call(
        functools.partial(rest_kernel, points),
        out_shape=(
            array(*sent.shape), array(RANK, 2 * RANK), array(RANK, RANK),
            square, square, column, square, square, column, array(RANK, points), array(RANK, points),
        ),
        in_specs=[SMEM, VMEM, VMEM, HBM, HBM, VMEM],
        out_specs=(VMEM,) * 11,
        scratch_shapes=[
            total, total, total,
            pltpu.SemaphoreType.DMA((len(EARLY), 2)),
            pltpu.SemaphoreType.DMA((24,)),
        ],
        compiler_params=params(LIMITS[2]),
        cost_estimate=pl.CostEstimate(flops=1_500_000_000, bytes_accessed=9_437_184, transcendentals=0),
        name="grams_rest",
    )(place, v1, v0, gen, cap, sent)


def middle_kernel(core_ref, mine_ref, other_ref, c3a_ref, c3b_ref, c2_ref, p_ref, g3_ref, g2_ref, g10_ref,
                  t_ref, keep_ref, send_ref):
    first = core_ref[0] == 0
    p, g = [], []
    for m in range(4):
        mine, other = mine_ref[m], other_ref[m]
        p.append(jnp.where(first, mine, other))
        g.append(jnp.where(first, other, mine))
    t = []
    for pair, cap in ((0, c3a_ref), (2, c3b_ref)):
        joined = jnp.concatenate([p[pair][:RHS], p[pair + 1][:RHS]], axis=1)
        both = product(joined, cap[...])
        t += [both[:, :RANK], both[:, RANK:]]
    q2 = [p[m][RHS:] - product(t[m], g[m]) for m in range(4)]
    joined = jnp.concatenate([q2[0] + q2[1], q2[2] + q2[3]], axis=1)
    coeff = jnp.concatenate([t[0], product(joined, c2_ref[...])], axis=1)
    t_ref[...] = coeff
    q = p_ref[...] - product(coeff, jnp.concatenate([g3_ref[...], g2_ref[...]], axis=0))
    half = RHS // 2

    def put(ref, c):
        rows = slice(c * half, (c + 1) * half)
        ref[:half] = q[rows, :RANK]
        ref[half : 2 * half] = q[rows, RANK:]
        ref[2 * half :] = g10_ref[c * RHS : (c + 1) * RHS]

    @pl.when(first)
    def _():
        put(keep_ref, 0)
        put(send_ref, 1)

    @pl.when(jnp.logical_not(first))
    def _():
        put(keep_ref, 1)
        put(send_ref, 0)


def middle_step(core, mine, other, c3a, c3b, c2, p, g3, g2, g10):
    half = jax.ShapeDtypeStruct((RANK, RANK), F32)
    return pl.pallas_call(
        middle_kernel,
        out_shape=(jax.ShapeDtypeStruct((RHS, 2 * RANK), F32), half, half),
        in_specs=[SMEM] + [VMEM] * 9,
        out_specs=(VMEM,) * 3,
        compiler_params=params(LIMITS[3]),
        cost_estimate=pl.CostEstimate(flops=120_000_000, bytes_accessed=1_500_000, transcendentals=0),
        name="coefficients_low",
    )(core, mine, other, c3a, c3b, c2, p, g3, g2, g10)


def low_update_kernel(t_ref, held_ref, u2_ref, sent_ref, cur_ref, sent_out):
    sent_out[...] = sent_ref[...]
    th, tl = split(t_ref[...])
    left = jnp.concatenate([th, tl], axis=0)
    for cols in spans((2,) * 4, held_ref.shape[1]):
        gh, gl = split(jnp.concatenate([held_ref[RHS:, cols], u2_ref[:, cols]], axis=0))
        both = jnp.dot(left, gh, preferred_element_type=F32)
        update = both[:RHS] + both[RHS:] + jnp.dot(th, gl, preferred_element_type=F32)
        cur_ref[:, cols] = held_ref[:RHS, cols] - update


def low_update(t, held, u2, sent):
    return pl.pallas_call(
        low_update_kernel,
        out_shape=(array(RHS, held.shape[1]), array(*sent.shape)),
        in_specs=[VMEM] * 4,
        out_specs=(VMEM, VMEM),
        compiler_params=params(LIMITS[4]),
        cost_estimate=pl.CostEstimate(flops=402_653_184, bytes_accessed=6_291_456, transcendentals=0),
        name="update_low",
    )(t, held, u2, sent)


def pairs_kernel(points, u1_ref, gen_ref, sent_ref, sent_out, high_ref, low_ref, u0_buf, sems):
    parts = fetch(((gen_ref, 0, u0_buf),), sems, (4, 4), points)
    sent_out[...] = sent_ref[...]
    high_ref[:RANK], low_ref[:RANK] = split(u1_ref[...])
    for cols, row in parts:
        row[0].wait()
        high_ref[RANK:, cols], low_ref[RANK:, cols] = split(u0_buf[:, cols])


def pairs_step(u1, gen, sent):
    points = u1.shape[1]
    pair = jax.ShapeDtypeStruct((2 * RANK, points), BF16)
    return pl.pallas_call(
        functools.partial(pairs_kernel, points),
        out_shape=(array(*sent.shape), pair, pair),
        in_specs=[VMEM, HBM, VMEM],
        out_specs=(VMEM,) * 3,
        scratch_shapes=[pltpu.VMEM((RANK, points), F32), pltpu.SemaphoreType.DMA((2, 1))],
        compiler_params=params(LIMITS[5]),
        cost_estimate=pl.CostEstimate(flops=100_000_000, bytes_accessed=8_388_608, transcendentals=0),
        name="pairs_high",
    )(u1, gen, sent)


def last_kernel(core_ref, mine_ref, other_ref, c1a_ref, c1b_ref, c0_ref, cur_ref, high_ref, low_ref, out_ref,
                buf, sems):
    first = core_ref[0] == 0
    half = RHS // 2
    q1, q0, g = [], [], []
    for m in range(4):
        mine, other = mine_ref[m], other_ref[m]
        low = jnp.where(first, mine, other)
        high = jnp.where(first, other, mine)
        q1.append(jnp.concatenate([low[:half], high[:half]], axis=0))
        q0.append(jnp.concatenate([low[half:RHS], high[half:RHS]], axis=0))
        g.append(jnp.concatenate([low[RHS:], high[RHS:]], axis=0))
    t = []
    for pair, cap in ((0, c1a_ref), (2, c1b_ref)):
        both = product(jnp.concatenate([q1[pair], q1[pair + 1]], axis=1), cap[...])
        t += [both[:, :RANK], both[:, RANK:]]
    r = [q0[m] - product(t[m], g[m]) for m in range(4)]
    joined = jnp.concatenate([r[0] + r[1], r[2] + r[3]], axis=1)
    th, tl = split(jnp.concatenate([t[0], product(joined, c0_ref[...])], axis=1))
    left = jnp.concatenate([th, tl], axis=0)
    copies = []
    for i, cols in enumerate(spans((2,) * 4, cur_ref.shape[1])):
        both = jnp.dot(left, high_ref[:, cols], preferred_element_type=F32)
        update = both[:RHS] + both[RHS:] + jnp.dot(th, low_ref[:, cols], preferred_element_type=F32)
        buf[:, cols] = cur_ref[:, cols] - update
        copy = pltpu.make_async_copy(buf.at[:, cols], out_ref.at[:, cols], sems.at[i])
        copy.start()
        copies.append(copy)
    for copy in copies:
        copy.wait()


def last_step(core, mine, other, c1a, c1b, c0, cur, high, low):
    return pl.pallas_call(
        last_kernel,
        out_shape=array(*cur.shape),
        in_specs=[SMEM] + [VMEM] * 8,
        out_specs=HBM,
        scratch_shapes=[pltpu.VMEM(cur.shape, F32), pltpu.SemaphoreType.DMA((4,))],
        compiler_params=params(LIMITS[6]),
        cost_estimate=pl.CostEstimate(flops=500_000_000, bytes_accessed=7_000_000, transcendentals=0),
        name="update_high",
    )(core, mine, other, c1a, c1b, c0, cur, high, low)


def swap(value, even, odd):
    pairs = [(i, i ^ (odd if i & CORE else even)) for i in range(DEVICES)]
    return lax.ppermute(value, "leaf", pairs)


def gathered(value, even, odd):
    one, three, two = (swap(value, e, o) for e, o in zip(even, odd))
    return value, one, two, three


def body(rhs, basis, gen, cap):
    device = lax.axis_index("leaf").astype(jnp.int32)
    core = (device & 1).reshape(1)
    place = jnp.stack([
        device >> 3 & 1, device >> 4 & 1, device >> 5 & 1, device >> 6 & 1,
        device >> 4, device >> 5, device >> 6,
    ])
    keep, send, held = first_step(core, rhs, basis, gen)
    chip = keep + swap(send, CORE, CORE)
    _, b, c, d = gathered(chip, Z_MASKS, Z_MASKS)
    chip, p, g3, v1, v0 = grams_step(held, basis, chip)
    line = chip + b + c + d
    _, b, c, d = gathered(line, X_MASKS, X_MASKS)
    line, g2, g10, c3a, c3b, c2, c1a, c1b, c0, u2, u1 = rest_step(place, v1, v0, gen, cap, line)
    lines = jnp.stack([line, b, c, d])
    other = swap(lines, CORE, CORE)
    t, keep, send = middle_step(core, lines, other, c3a, c3b, c2, p, g3, g2, g10)
    chip = keep + swap(send, CORE, CORE)
    _, b, c, d = gathered(chip, X_MASKS, Z_MASKS)
    current, chip = low_update(t, held, u2, chip)
    part = chip + b + c + d
    _, b, c, d = gathered(part, Z_MASKS, X_MASKS)
    part, high, low = pairs_step(u1, gen, part)
    plane = part + b + c + d
    planes = jnp.stack(gathered(plane, Y_MASKS, Y_MASKS))
    other = swap(planes, CORE, CORE)
    return last_step(core, planes, other, c1a, c1b, c0, current, high, low)


def solution(mesh):
    in_specs = (P(None, "leaf"), P(None, None, "leaf"), P(None, None, "leaf"), P())
    return jax.shard_map(body, mesh=mesh, in_specs=in_specs, out_specs=P(None, "leaf"), check_vma=False)
```

```python
import functools

import jax
import jax.numpy as jnp
from jax import lax
from jax.experimental import pallas as pl
from jax.experimental.pallas import tpu as pltpu
from jax.sharding import PartitionSpec as P

F32 = jnp.float32
BF16 = jnp.bfloat16
RANK = 128
RHS = 64
DEVICES = 128
LIMITS = (53, 42, 38, 38, 40, 40, 44)
HBM = pl.BlockSpec(memory_space=pltpu.HBM)
VMEM = pl.BlockSpec(memory_space=pltpu.VMEM)
SMEM = pl.BlockSpec(memory_space=pltpu.SMEM)

CORE = 1
Z_MASKS = (2, 6, 4)
X_MASKS = (8, 24, 16)
Y_MASKS = (32, 96, 64)


def split(value):
    high = value.astype(BF16)
    return high, (value - high.astype(F32)).astype(BF16)


def stacked(values):
    parts = [split(v) for v in values]
    return jnp.concatenate([h for h, _ in parts] + [l for _, l in parts], axis=0)


def product(left, right):
    lh, ll = split(left)
    rh, rl = split(right)
    rows = left.shape[0]
    both = jnp.dot(jnp.concatenate([lh, ll], axis=0), rh, preferred_element_type=F32)
    return both[:rows] + both[rows:] + jnp.dot(lh, rl, preferred_element_type=F32)


def contract(left, right):
    return lax.dot_general(left, right, (((1,), (1,)), ((), ())), preferred_element_type=F32)


def fold(total, rows):
    half = total.shape[1] // 2
    wide = total[:rows] + total[rows:]
    return wide[:, :half] + wide[:, half:]


def params(limit):
    return pltpu.CompilerParams(vmem_limit_bytes=limit << 20)


def spans(sizes, points):
    at = 0
    for size in sizes:
        yield pl.ds(at * points // 8, size * points // 8)
        at += size


def fetch(sources, sems, sizes, points):
    parts = []
    for i, cols in enumerate(spans(sizes, points)):
        row = []
        for j, (ref, level, buffer) in enumerate(sources):
            src = ref.at[:, cols] if level is None else ref.at[level, :, cols]
            row.append(pltpu.make_async_copy(src, buffer.at[:, cols], sems.at[i, j]))
        parts.append((cols, row))
    for _, row in parts:
        for copy in row:
            copy.start()
    return parts


def add_to(acc, value, first):
    if first:
        acc[...] = value
    else:
        acc[...] += value


PARTS = (2, 2, 2, 2)


def first_kernel(points, core_ref, rhs_ref, basis_ref, gen_ref, keep_ref, send_ref,
                 rhs_buf, v3_buf, v2_buf, u3_buf, acc2, acc3, sems):
    sources = ((rhs_ref, None, rhs_buf), (basis_ref, 3, v3_buf), (basis_ref, 2, v2_buf), (gen_ref, 3, u3_buf))
    for i, (cols, row) in enumerate(fetch(sources, sems, PARTS, points)):
        for copy in row:
            copy.wait()
        rhs = stacked([rhs_buf[:, cols]])
        left = jnp.concatenate([rhs, stacked([u3_buf[:, cols]])], axis=0)
        add_to(acc2, contract(left, stacked([v2_buf[:, cols]])), i == 0)
        add_to(acc3, contract(rhs, stacked([v3_buf[:, cols]])), i == 0)
    p3 = fold(acc3[...], RHS)
    p2 = fold(acc2[: 2 * RHS], RHS)
    g32 = fold(acc2[2 * RHS :], RANK)
    first = core_ref[0] == 0

    @pl.when(first)
    def _():
        keep_ref[:RHS] = p3
        keep_ref[RHS:] = p2
        send_ref[...] = g32

    @pl.when(jnp.logical_not(first))
    def _():
        send_ref[:RHS] = p3
        send_ref[RHS:] = p2
        keep_ref[...] = g32


def array(*shape):
    return jax.ShapeDtypeStruct(shape, F32)


def first_step(core, rhs, basis, gen):
    points = rhs.shape[1]
    wide = pltpu.VMEM((RANK, points), F32)
    return pl.pallas_call(
        functools.partial(first_kernel, points),
        out_shape=(array(RANK, RANK), array(RANK, RANK)),
        in_specs=[SMEM, HBM, HBM, HBM],
        out_specs=(VMEM,) * 2,
        scratch_shapes=[
            pltpu.VMEM((RHS, points), F32), wide, wide, wide,
            pltpu.VMEM((2 * (RHS + RANK), 2 * RANK), F32),
            pltpu.VMEM((2 * RHS, 2 * RANK), F32),
            pltpu.SemaphoreType.DMA((len(PARTS), 4)),
        ],
        compiler_params=params(LIMITS[0]),
        cost_estimate=pl.CostEstimate(flops=800_000_000, bytes_accessed=7_340_032, transcendentals=0),
        name="project_low",
    )(core, rhs, basis, gen)


def related(cap_ref, out_ref, sems, node, s, base, columns):
    copies = []
    for r, row in enumerate((1 - s, s)):
        for c, col in enumerate((s, 1 - s)[:columns]):
            copies.append(
                pltpu.make_async_copy(
                    cap_ref.at[node, pl.ds(pl.multiple_of(row * RANK, RANK), RANK), pl.ds(pl.multiple_of(col * RANK, RANK), RANK)],
                    out_ref.at[r * RANK : (r + 1) * RANK, c * RANK : (c + 1) * RANK],
                    sems.at[base + 2 * r + c],
                )
            )
    for copy in copies:
        copy.start()
    return copies


def load_kernel(rhs_ref, basis_ref, gen_ref, sent_ref, sent_out, p_ref, v1_ref, v0_ref, u3_ref, u2_ref, sems):
    sources = ((basis_ref, 1, v1_ref), (basis_ref, 0, v0_ref), (gen_ref, 3, u3_ref), (gen_ref, 2, u2_ref))
    copies = [pltpu.make_async_copy(ref.at[k], out, sems.at[i]) for i, (ref, k, out) in enumerate(sources)]
    for copy in copies:
        copy.start()
    sent_out[...] = sent_ref[...]
    left = stacked([rhs_ref[...]])
    copies[0].wait()
    copies[1].wait()
    p_ref[:, :RANK] = fold(contract(left, stacked([v1_ref[...]])), RHS)
    p_ref[:, RANK:] = fold(contract(left, stacked([v0_ref[...]])), RHS)
    copies[2].wait()
    copies[3].wait()


def load_step(rhs, basis, gen, sent):
    wide = array(RANK, rhs.shape[1])
    return pl.pallas_call(
        load_kernel,
        out_shape=(array(*sent.shape), array(RHS, 2 * RANK), wide, wide, wide, wide),
        in_specs=[VMEM, HBM, HBM, VMEM],
        out_specs=(VMEM,) * 6,
        scratch_shapes=[pltpu.SemaphoreType.DMA((4,))],
        compiler_params=params(LIMITS[1]),
        cost_estimate=pl.CostEstimate(flops=300_000_000, bytes_accessed=9_437_184, transcendentals=0),
        name="load_project_high",
    )(rhs, basis, gen, sent)


def grams_kernel(place_ref, v1_ref, v0_ref, u3_ref, u2_ref, gen_ref, cap_ref, sent_ref, sent_out,
                 g_ref, g10_ref, c3a_ref, c3b_ref, c2_ref, c1a_ref, c1b_ref, c0_ref, u1_ref, u0_ref,
                 sems, cap_sems):
    copies = [pltpu.make_async_copy(gen_ref.at[k], out, sems.at[k]) for k, out in ((1, u1_ref), (0, u0_ref))]
    for copy in copies:
        copy.start()
    sent_out[...] = sent_ref[...]
    s3, s2, s1, s0 = place_ref[0], place_ref[1], place_ref[2], place_ref[3]
    n3, n2, n1 = place_ref[4], place_ref[5], place_ref[6]
    caps = related(cap_ref, c3a_ref, cap_sems, 7 + n3, s3, 0, 2)
    caps += related(cap_ref, c3b_ref, cap_sems, 7 + (n3 ^ 1), s3, 4, 2)
    caps += related(cap_ref, c2_ref, cap_sems, 3 + n2, s2, 8, 1)
    caps += related(cap_ref, c1a_ref, cap_sems, 1 + n1, s1, 12, 2)
    caps += related(cap_ref, c1b_ref, cap_sems, 1 + (n1 ^ 1), s1, 16, 2)
    caps += related(cap_ref, c0_ref, cap_sems, 0, s0, 20, 1)
    v1, v0 = stacked([v1_ref[...]]), stacked([v0_ref[...]])
    for k, ref in enumerate((u3_ref, u2_ref)):
        left = stacked([ref[...]])
        g_ref[k * RANK : (k + 1) * RANK, :RANK] = fold(contract(left, v1), RANK)
        g_ref[k * RANK : (k + 1) * RANK, RANK:] = fold(contract(left, v0), RANK)
    copies[0].wait()
    g10_ref[...] = fold(contract(stacked([u1_ref[...]]), v0), RANK)
    for copy in caps:
        copy.wait()
    copies[1].wait()


def grams_step(place, v1, v0, u3, u2, gen, cap, sent):
    wide = array(*v1.shape)
    square, column = array(2 * RANK, 2 * RANK), array(2 * RANK, RANK)
    return pl.pallas_call(
        grams_kernel,
        out_shape=(
            array(*sent.shape), square, array(RANK, RANK),
            square, square, column, square, square, column, wide, wide,
        ),
        in_specs=[SMEM, VMEM, VMEM, VMEM, VMEM, HBM, HBM, VMEM],
        out_specs=(VMEM,) * 11,
        scratch_shapes=[pltpu.SemaphoreType.DMA((2,)), pltpu.SemaphoreType.DMA((24,))],
        compiler_params=params(LIMITS[2]),
        cost_estimate=pl.CostEstimate(flops=2_700_000_000, bytes_accessed=13_000_000, transcendentals=0),
        name="grams_high",
    )(place, v1, v0, u3, u2, gen, cap, sent)


def middle_kernel(core_ref, mine_ref, other_ref, c3a_ref, c3b_ref, c2_ref, p_ref, g_ref, g10_ref,
                  t_ref, keep_ref, send_ref):
    first = core_ref[0] == 0
    p, g = [], []
    for m in range(4):
        mine, other = mine_ref[m], other_ref[m]
        p.append(jnp.where(first, mine, other))
        g.append(jnp.where(first, other, mine))
    t = []
    for pair, cap in ((0, c3a_ref), (2, c3b_ref)):
        joined = jnp.concatenate([p[pair][:RHS], p[pair + 1][:RHS]], axis=1)
        both = product(joined, cap[...])
        t += [both[:, :RANK], both[:, RANK:]]
    q2 = [p[m][RHS:] - product(t[m], g[m]) for m in range(4)]
    joined = jnp.concatenate([q2[0] + q2[1], q2[2] + q2[3]], axis=1)
    coeff = jnp.concatenate([t[0], product(joined, c2_ref[...])], axis=1)
    t_ref[...] = coeff
    q = p_ref[...] - product(coeff, g_ref[...])
    half = RHS // 2

    def put(ref, c):
        rows = slice(c * half, (c + 1) * half)
        ref[:half] = q[rows, :RANK]
        ref[half : 2 * half] = q[rows, RANK:]
        ref[2 * half :] = g10_ref[c * RHS : (c + 1) * RHS]

    @pl.when(first)
    def _():
        put(keep_ref, 0)
        put(send_ref, 1)

    @pl.when(jnp.logical_not(first))
    def _():
        put(keep_ref, 1)
        put(send_ref, 0)


def middle_step(core, mine, other, c3a, c3b, c2, p, g, g10):
    half = jax.ShapeDtypeStruct((RANK, RANK), F32)
    return pl.pallas_call(
        middle_kernel,
        out_shape=(jax.ShapeDtypeStruct((RHS, 2 * RANK), F32), half, half),
        in_specs=[SMEM] + [VMEM] * 8,
        out_specs=(VMEM,) * 3,
        compiler_params=params(LIMITS[3]),
        cost_estimate=pl.CostEstimate(flops=120_000_000, bytes_accessed=1_500_000, transcendentals=0),
        name="coefficients_low",
    )(core, mine, other, c3a, c3b, c2, p, g, g10)


def low_update_kernel(t_ref, rhs_ref, u3_ref, u2_ref, sent_ref, cur_ref, sent_out):
    sent_out[...] = sent_ref[...]
    th, tl = split(t_ref[...])
    left = jnp.concatenate([th, tl], axis=0)
    for cols in spans((2,) * 4, rhs_ref.shape[1]):
        gh, gl = split(jnp.concatenate([u3_ref[:, cols], u2_ref[:, cols]], axis=0))
        both = jnp.dot(left, gh, preferred_element_type=F32)
        update = both[:RHS] + both[RHS:] + jnp.dot(th, gl, preferred_element_type=F32)
        cur_ref[:, cols] = rhs_ref[:, cols] - update


def low_update(t, rhs, u3, u2, sent):
    return pl.pallas_call(
        low_update_kernel,
        out_shape=(array(*rhs.shape), array(*sent.shape)),
        in_specs=[VMEM] * 5,
        out_specs=(VMEM, VMEM),
        compiler_params=params(LIMITS[4]),
        cost_estimate=pl.CostEstimate(flops=402_653_184, bytes_accessed=6_291_456, transcendentals=0),
        name="update_low",
    )(t, rhs, u3, u2, sent)


def pairs_kernel(u1_ref, u0_ref, sent_ref, sent_out, high_ref, low_ref):
    sent_out[...] = sent_ref[...]
    high_ref[:RANK], low_ref[:RANK] = split(u1_ref[...])
    high_ref[RANK:], low_ref[RANK:] = split(u0_ref[...])


def pairs_step(u1, u0, sent):
    pair = jax.ShapeDtypeStruct((2 * RANK, u1.shape[1]), BF16)
    return pl.pallas_call(
        pairs_kernel,
        out_shape=(array(*sent.shape), pair, pair),
        in_specs=[VMEM] * 3,
        out_specs=(VMEM,) * 3,
        compiler_params=params(LIMITS[5]),
        cost_estimate=pl.CostEstimate(flops=100_000_000, bytes_accessed=8_388_608, transcendentals=0),
        name="pairs_high",
    )(u1, u0, sent)


def last_kernel(core_ref, mine_ref, other_ref, c1a_ref, c1b_ref, c0_ref, cur_ref, high_ref, low_ref, out_ref,
                buf, sems):
    first = core_ref[0] == 0
    half = RHS // 2
    q1, q0, g = [], [], []
    for m in range(4):
        mine, other = mine_ref[m], other_ref[m]
        low = jnp.where(first, mine, other)
        high = jnp.where(first, other, mine)
        q1.append(jnp.concatenate([low[:half], high[:half]], axis=0))
        q0.append(jnp.concatenate([low[half:RHS], high[half:RHS]], axis=0))
        g.append(jnp.concatenate([low[RHS:], high[RHS:]], axis=0))
    t = []
    for pair, cap in ((0, c1a_ref), (2, c1b_ref)):
        both = product(jnp.concatenate([q1[pair], q1[pair + 1]], axis=1), cap[...])
        t += [both[:, :RANK], both[:, RANK:]]
    r = [q0[m] - product(t[m], g[m]) for m in range(4)]
    joined = jnp.concatenate([r[0] + r[1], r[2] + r[3]], axis=1)
    th, tl = split(jnp.concatenate([t[0], product(joined, c0_ref[...])], axis=1))
    left = jnp.concatenate([th, tl], axis=0)
    copies = []
    for i, cols in enumerate(spans((2,) * 4, cur_ref.shape[1])):
        both = jnp.dot(left, high_ref[:, cols], preferred_element_type=F32)
        update = both[:RHS] + both[RHS:] + jnp.dot(th, low_ref[:, cols], preferred_element_type=F32)
        buf[:, cols] = cur_ref[:, cols] - update
        copy = pltpu.make_async_copy(buf.at[:, cols], out_ref.at[:, cols], sems.at[i])
        copy.start()
        copies.append(copy)
    for copy in copies:
        copy.wait()


def last_step(core, mine, other, c1a, c1b, c0, cur, high, low):
    return pl.pallas_call(
        last_kernel,
        out_shape=array(*cur.shape),
        in_specs=[SMEM] + [VMEM] * 8,
        out_specs=HBM,
        scratch_shapes=[pltpu.VMEM(cur.shape, F32), pltpu.SemaphoreType.DMA((4,))],
        compiler_params=params(LIMITS[6]),
        cost_estimate=pl.CostEstimate(flops=500_000_000, bytes_accessed=7_000_000, transcendentals=0),
        name="update_high",
    )(core, mine, other, c1a, c1b, c0, cur, high, low)


def swap(value, even, odd):
    pairs = [(i, i ^ (odd if i & CORE else even)) for i in range(DEVICES)]
    return lax.ppermute(value, "leaf", pairs)


def gathered(value, even, odd):
    one, three, two = (swap(value, e, o) for e, o in zip(even, odd))
    return value, one, two, three


def body(rhs, basis, gen, cap):
    device = lax.axis_index("leaf").astype(jnp.int32)
    core = (device & 1).reshape(1)
    place = jnp.stack([
        device >> 3 & 1, device >> 4 & 1, device >> 5 & 1, device >> 6 & 1,
        device >> 4, device >> 5, device >> 6,
    ])
    keep, send = first_step(core, rhs, basis, gen)
    chip = keep + swap(send, CORE, CORE)
    _, b, c, d = gathered(chip, Z_MASKS, Z_MASKS)
    chip, p, v1, v0, u3, u2 = load_step(rhs, basis, gen, chip)
    line = chip + b + c + d
    _, b, c, d = gathered(line, X_MASKS, X_MASKS)
    line, g, g10, c3a, c3b, c2, c1a, c1b, c0, u1, u0 = grams_step(place, v1, v0, u3, u2, gen, cap, line)
    lines = jnp.stack([line, b, c, d])
    other = swap(lines, CORE, CORE)
    t, keep, send = middle_step(core, lines, other, c3a, c3b, c2, p, g, g10)
    chip = keep + swap(send, CORE, CORE)
    _, b, c, d = gathered(chip, X_MASKS, Z_MASKS)
    current, chip = low_update(t, rhs, u3, u2, chip)
    part = chip + b + c + d
    _, b, c, d = gathered(part, Z_MASKS, X_MASKS)
    part, high, low = pairs_step(u1, u0, part)
    plane = part + b + c + d
    planes = jnp.stack(gathered(plane, Y_MASKS, Y_MASKS))
    other = swap(planes, CORE, CORE)
    return last_step(core, planes, other, c1a, c1b, c0, current, high, low)


def solution(mesh):
    in_specs = (P(None, "leaf"), P(None, None, "leaf"), P(None, None, "leaf"), P())
    return jax.shard_map(body, mesh=mesh, in_specs=in_specs, out_specs=P(None, "leaf"), check_vma=False)
```

```python
import functools

import jax
import jax.numpy as jnp
from jax import lax
from jax.experimental import pallas as pl
from jax.experimental.pallas import tpu as pltpu
from jax.sharding import PartitionSpec as P

F32 = jnp.float32
BF16 = jnp.bfloat16
RANK = 128
RHS = 64
DEVICES = 128
LIMITS = (53, 40, 38, 38, 40, 40, 44, 50)
HBM = pl.BlockSpec(memory_space=pltpu.HBM)
VMEM = pl.BlockSpec(memory_space=pltpu.VMEM)
SMEM = pl.BlockSpec(memory_space=pltpu.SMEM)

CORE = 1
Z_MASKS = (6, 4, 2)
X_MASKS = (24, 16, 8)
Y_MASKS = (96, 64, 32)


def split(value):
    high = value.astype(BF16)
    return high, (value - high.astype(F32)).astype(BF16)


def stacked(values):
    parts = [split(v) for v in values]
    return jnp.concatenate([h for h, _ in parts] + [l for _, l in parts], axis=0)


def product(left, right):
    lh, ll = split(left)
    rh, rl = split(right)
    rows = left.shape[0]
    both = jnp.dot(jnp.concatenate([lh, ll], axis=0), rh, preferred_element_type=F32)
    return both[:rows] + both[rows:] + jnp.dot(lh, rl, preferred_element_type=F32)


def contract(left, right):
    return lax.dot_general(left, right, (((1,), (1,)), ((), ())), preferred_element_type=F32)


def fold(total, rows):
    half = total.shape[1] // 2
    wide = total[:rows] + total[rows:]
    return wide[:, :half] + wide[:, half:]


def params(limit):
    return pltpu.CompilerParams(vmem_limit_bytes=limit << 20)


def spans(sizes, points):
    at = 0
    for size in sizes:
        yield pl.ds(at * points // 8, size * points // 8)
        at += size


def fetch(sources, sems, sizes, points):
    parts = []
    for i, cols in enumerate(spans(sizes, points)):
        row = []
        for j, (ref, level, buffer) in enumerate(sources):
            src = ref.at[:, cols] if level is None else ref.at[level, :, cols]
            row.append(pltpu.make_async_copy(src, buffer.at[:, cols], sems.at[i, j]))
        parts.append((cols, row))
    for _, row in parts:
        for copy in row:
            copy.start()
    return parts


def add_to(acc, value, first):
    if first:
        acc[...] = value
    else:
        acc[...] += value


PARTS = (2, 2, 2, 2)


def first_kernel(points, core_ref, rhs_ref, basis_ref, gen_ref, keep_ref, send_ref,
                 rhs_buf, v3_buf, v2_buf, u3_buf, acc2, acc3, sems):
    sources = ((rhs_ref, None, rhs_buf), (basis_ref, 3, v3_buf), (basis_ref, 2, v2_buf), (gen_ref, 3, u3_buf))
    for i, (cols, row) in enumerate(fetch(sources, sems, PARTS, points)):
        for copy in row:
            copy.wait()
        rhs = stacked([rhs_buf[:, cols]])
        left = jnp.concatenate([rhs, stacked([u3_buf[:, cols]])], axis=0)
        add_to(acc2, contract(left, stacked([v2_buf[:, cols]])), i == 0)
        add_to(acc3, contract(rhs, stacked([v3_buf[:, cols]])), i == 0)
    p3 = fold(acc3[...], RHS)
    p2 = fold(acc2[: 2 * RHS], RHS)
    g32 = fold(acc2[2 * RHS :], RANK)
    first = core_ref[0] == 0

    @pl.when(first)
    def _():
        keep_ref[:RHS] = p3
        keep_ref[RHS:] = p2
        send_ref[...] = g32

    @pl.when(jnp.logical_not(first))
    def _():
        send_ref[:RHS] = p3
        send_ref[RHS:] = p2
        keep_ref[...] = g32


def array(*shape):
    return jax.ShapeDtypeStruct(shape, F32)


def first_step(core, rhs, basis, gen):
    points = rhs.shape[1]
    wide = pltpu.VMEM((RANK, points), F32)
    return pl.pallas_call(
        functools.partial(first_kernel, points),
        out_shape=(array(RANK, RANK), array(RANK, RANK)),
        in_specs=[SMEM, HBM, HBM, HBM],
        out_specs=(VMEM,) * 2,
        scratch_shapes=[
            pltpu.VMEM((RHS, points), F32), wide, wide, wide,
            pltpu.VMEM((2 * (RHS + RANK), 2 * RANK), F32),
            pltpu.VMEM((2 * RHS, 2 * RANK), F32),
            pltpu.SemaphoreType.DMA((len(PARTS), 4)),
        ],
        compiler_params=params(LIMITS[0]),
        cost_estimate=pl.CostEstimate(flops=800_000_000, bytes_accessed=7_340_032, transcendentals=0),
        name="project_low",
    )(core, rhs, basis, gen)


def load_kernel(basis_ref, gen_ref, sent_ref, sent_out, v1_ref, v0_ref, u3_ref, u2_ref, u1_ref, sems):
    sources = (
        (basis_ref, 1, v1_ref), (basis_ref, 0, v0_ref),
        (gen_ref, 3, u3_ref), (gen_ref, 2, u2_ref), (gen_ref, 1, u1_ref),
    )
    copies = [pltpu.make_async_copy(ref.at[k], out, sems.at[i]) for i, (ref, k, out) in enumerate(sources)]
    for copy in copies:
        copy.start()
    sent_out[...] = sent_ref[...]
    for copy in copies:
        copy.wait()


def load_step(basis, gen, sent):
    wide = array(*basis.shape[1:])
    return pl.pallas_call(
        load_kernel,
        out_shape=(array(*sent.shape), wide, wide, wide, wide, wide),
        in_specs=[HBM, HBM, VMEM],
        out_specs=(VMEM,) * 6,
        scratch_shapes=[pltpu.SemaphoreType.DMA((5,))],
        compiler_params=params(LIMITS[1]),
        cost_estimate=pl.CostEstimate(flops=1_000, bytes_accessed=10_485_760, transcendentals=0),
        name="load_high",
    )(basis, gen, sent)


def grams_kernel(rhs_ref, v1_ref, v0_ref, u3_ref, u2_ref, u1_ref, sent_ref, sent_out, p_ref, g_ref, g10_ref):
    sent_out[...] = sent_ref[...]
    left = stacked([rhs_ref[...], u3_ref[...]])
    u2 = stacked([u2_ref[...]])
    for k, ref in enumerate((v1_ref, v0_ref)):
        right = stacked([ref[...]])
        cols = slice(k * RANK, (k + 1) * RANK)
        both = fold(contract(left, right), RHS + RANK)
        p_ref[:, cols] = both[:RHS]
        g_ref[:RANK, cols] = both[RHS:]
        g_ref[RANK:, cols] = fold(contract(u2, right), RANK)
    g10_ref[...] = fold(contract(stacked([u1_ref[...]]), right), RANK)


def grams_step(rhs, v1, v0, u3, u2, u1, sent):
    return pl.pallas_call(
        grams_kernel,
        out_shape=(array(*sent.shape), array(RHS, 2 * RANK), array(2 * RANK, 2 * RANK), array(RANK, RANK)),
        in_specs=[VMEM] * 7,
        out_specs=(VMEM,) * 4,
        compiler_params=params(LIMITS[2]),
        cost_estimate=pl.CostEstimate(flops=3_200_000_000, bytes_accessed=11_534_336, transcendentals=0),
        name="grams_high",
    )(rhs, v1, v0, u3, u2, u1, sent)


def nodes_kernel(nodes_ref, cap_ref, sent_ref, sent_out, out_ref, sems):
    copies = [pltpu.make_async_copy(cap_ref.at[nodes_ref[i]], out_ref.at[i], sems.at[i]) for i in range(3)]
    for copy in copies:
        copy.start()
    sent_out[...] = sent_ref[...]
    for copy in copies:
        copy.wait()


def nodes_step(nodes, cap, sent, name):
    return pl.pallas_call(
        nodes_kernel,
        out_shape=(array(*sent.shape), array(3, 2 * RANK, 2 * RANK)),
        in_specs=[SMEM, HBM, VMEM],
        out_specs=(VMEM, VMEM),
        scratch_shapes=[pltpu.SemaphoreType.DMA((3,))],
        compiler_params=params(LIMITS[7]),
        cost_estimate=pl.CostEstimate(flops=1_000, bytes_accessed=786_432, transcendentals=0),
        name=name,
    )(nodes, cap, sent)


def related(caps_ref, node, s, columns):
    blocks = []
    for row in (1 - s, s):
        rows = pl.ds(pl.multiple_of(row * RANK, RANK), RANK)
        blocks.append(
            jnp.concatenate(
                [
                    caps_ref[node, rows, pl.ds(pl.multiple_of(col * RANK, RANK), RANK)]
                    for col in (s, 1 - s)[:columns]
                ],
                axis=1,
            )
        )
    return jnp.concatenate(blocks, axis=0)


def middle_kernel(place_ref, mine_ref, other_ref, caps_ref, p_ref, g_ref, g10_ref,
                  t_ref, keep_ref, send_ref):
    first = place_ref[0] == 0
    p, g = [], []
    for m in range(4):
        mine, other = mine_ref[(3, 1, 0, 2)[m]], other_ref[(3, 1, 0, 2)[m]]
        p.append(jnp.where(first, mine, other))
        g.append(jnp.where(first, other, mine))
    t = []
    for pair in (0, 2):
        joined = jnp.concatenate([p[pair][:RHS], p[pair + 1][:RHS]], axis=1)
        both = product(joined, related(caps_ref, pair // 2, place_ref[1], 2))
        t += [both[:, :RANK], both[:, RANK:]]
    q2 = [p[m][RHS:] - product(t[m], g[m]) for m in range(4)]
    joined = jnp.concatenate([q2[0] + q2[1], q2[2] + q2[3]], axis=1)
    coeff = jnp.concatenate([t[0], product(joined, related(caps_ref, 2, place_ref[2], 1))], axis=1)
    t_ref[...] = coeff
    q = p_ref[...] - product(coeff, g_ref[...])
    half = RHS // 2

    def put(ref, c):
        rows = slice(c * half, (c + 1) * half)
        ref[:half] = q[rows, :RANK]
        ref[half : 2 * half] = q[rows, RANK:]
        ref[2 * half :] = g10_ref[c * RHS : (c + 1) * RHS]

    @pl.when(first)
    def _():
        put(keep_ref, 0)
        put(send_ref, 1)

    @pl.when(jnp.logical_not(first))
    def _():
        put(keep_ref, 1)
        put(send_ref, 0)


def middle_step(place, mine, other, caps, p, g, g10):
    half = jax.ShapeDtypeStruct((RANK, RANK), F32)
    return pl.pallas_call(
        middle_kernel,
        out_shape=(jax.ShapeDtypeStruct((RHS, 2 * RANK), F32), half, half),
        in_specs=[SMEM] + [VMEM] * 6,
        out_specs=(VMEM,) * 3,
        compiler_params=params(LIMITS[3]),
        cost_estimate=pl.CostEstimate(flops=120_000_000, bytes_accessed=1_500_000, transcendentals=0),
        name="coefficients_low",
    )(place, mine, other, caps, p, g, g10)


def low_update_kernel(t_ref, rhs_ref, u3_ref, u2_ref, sent_ref, cur_ref, sent_out):
    sent_out[...] = sent_ref[...]
    th, tl = split(t_ref[...])
    left = jnp.concatenate([th, tl], axis=0)
    for cols in spans((2,) * 4, rhs_ref.shape[1]):
        gh, gl = split(jnp.concatenate([u3_ref[:, cols], u2_ref[:, cols]], axis=0))
        both = jnp.dot(left, gh, preferred_element_type=F32)
        update = both[:RHS] + both[RHS:] + jnp.dot(th, gl, preferred_element_type=F32)
        cur_ref[:, cols] = rhs_ref[:, cols] - update


def low_update(t, rhs, u3, u2, sent):
    return pl.pallas_call(
        low_update_kernel,
        out_shape=(array(*rhs.shape), array(*sent.shape)),
        in_specs=[VMEM] * 5,
        out_specs=(VMEM, VMEM),
        compiler_params=params(LIMITS[4]),
        cost_estimate=pl.CostEstimate(flops=402_653_184, bytes_accessed=6_291_456, transcendentals=0),
        name="update_low",
    )(t, rhs, u3, u2, sent)


def pairs_kernel(u1_ref, gen_ref, sent_ref, sent_out, high_ref, low_ref, u0_ref, sem):
    copy = pltpu.make_async_copy(gen_ref.at[0], u0_ref, sem)
    copy.start()
    sent_out[...] = sent_ref[...]
    high_ref[:RANK], low_ref[:RANK] = split(u1_ref[...])
    copy.wait()
    high_ref[RANK:], low_ref[RANK:] = split(u0_ref[...])


def pairs_step(u1, gen, sent):
    pair = jax.ShapeDtypeStruct((2 * RANK, u1.shape[1]), BF16)
    return pl.pallas_call(
        pairs_kernel,
        out_shape=(array(*sent.shape), pair, pair),
        in_specs=[VMEM, HBM, VMEM],
        out_specs=(VMEM,) * 3,
        scratch_shapes=[pltpu.VMEM(u1.shape, F32), pltpu.SemaphoreType.DMA(())],
        compiler_params=params(LIMITS[5]),
        cost_estimate=pl.CostEstimate(flops=100_000_000, bytes_accessed=8_388_608, transcendentals=0),
        name="pairs_high",
    )(u1, gen, sent)


def last_kernel(place_ref, mine_ref, other_ref, caps_ref, cur_ref, high_ref, low_ref, out_ref,
                buf, sems):
    first = place_ref[0] == 0
    half = RHS // 2
    q1, q0, g = [], [], []
    for m in range(4):
        mine, other = mine_ref[3 - m], other_ref[3 - m]
        low = jnp.where(first, mine, other)
        high = jnp.where(first, other, mine)
        q1.append(jnp.concatenate([low[:half], high[:half]], axis=0))
        q0.append(jnp.concatenate([low[half:RHS], high[half:RHS]], axis=0))
        g.append(jnp.concatenate([low[RHS:], high[RHS:]], axis=0))
    t = []
    for pair in (0, 2):
        both = product(
            jnp.concatenate([q1[pair], q1[pair + 1]], axis=1), related(caps_ref, pair // 2, place_ref[3], 2)
        )
        t += [both[:, :RANK], both[:, RANK:]]
    r = [q0[m] - product(t[m], g[m]) for m in range(4)]
    joined = jnp.concatenate([r[0] + r[1], r[2] + r[3]], axis=1)
    th, tl = split(jnp.concatenate([t[0], product(joined, related(caps_ref, 2, place_ref[4], 1))], axis=1))
    left = jnp.concatenate([th, tl], axis=0)
    copies = []
    for i, cols in enumerate(spans((2,) * 4, cur_ref.shape[1])):
        both = jnp.dot(left, high_ref[:, cols], preferred_element_type=F32)
        update = both[:RHS] + both[RHS:] + jnp.dot(th, low_ref[:, cols], preferred_element_type=F32)
        buf[:, cols] = cur_ref[:, cols] - update
        copy = pltpu.make_async_copy(buf.at[:, cols], out_ref.at[:, cols], sems.at[i])
        copy.start()
        copies.append(copy)
    for copy in copies:
        copy.wait()


def last_step(place, mine, other, caps, cur, high, low):
    return pl.pallas_call(
        last_kernel,
        out_shape=array(*cur.shape),
        in_specs=[SMEM] + [VMEM] * 6,
        out_specs=HBM,
        scratch_shapes=[pltpu.VMEM(cur.shape, F32), pltpu.SemaphoreType.DMA((4,))],
        compiler_params=params(LIMITS[6]),
        cost_estimate=pl.CostEstimate(flops=500_000_000, bytes_accessed=7_000_000, transcendentals=0),
        name="update_high",
    )(place, mine, other, caps, cur, high, low)


def swap(value, even, odd):
    pairs = [(i, i ^ (odd if i & CORE else even)) for i in range(DEVICES)]
    return lax.ppermute(value, "leaf", pairs)


def neighbours(value, even, odd):
    three, two, one = (swap(value, e, o) for e, o in zip(even, odd))
    return one, two, three


def body(rhs, basis, gen, cap):
    device = lax.axis_index("leaf").astype(jnp.int32)
    core = (device & 1).reshape(1)
    place = jnp.stack([device & 1, device >> 3 & 1, device >> 4 & 1, device >> 5 & 1, device >> 6 & 1])
    n3, n2, n1 = device >> 4, device >> 5, device >> 6
    low_nodes = jnp.stack([7 + n3, 7 + (n3 ^ 1), 3 + n2])
    high_nodes = jnp.stack([1 + n1, 1 + (n1 ^ 1), jnp.zeros_like(n1)])
    keep, send = first_step(core, rhs, basis, gen)
    chip = keep + swap(send, CORE, CORE)
    b, c, d = neighbours(chip, Z_MASKS, Z_MASKS)
    chip, v1, v0, u3, u2, u1 = load_step(basis, gen, chip)
    line = chip + d + c + b
    b, c, d = neighbours(line, X_MASKS, X_MASKS)
    line, p, g, g10 = grams_step(rhs, v1, v0, u3, u2, u1, line)
    lines = jnp.stack([c, b, d, line])
    other = swap(lines, CORE, CORE)
    lines, caps = nodes_step(low_nodes, cap, lines, "nodes_low")
    t, keep, send = middle_step(place, lines, other, caps, p, g, g10)
    chip = keep + swap(send, CORE, CORE)
    b, c, d = neighbours(chip, X_MASKS, Z_MASKS)
    current, chip = low_update(t, rhs, u3, u2, chip)
    part = chip + b + d + c
    b, c, d = neighbours(part, Z_MASKS, X_MASKS)
    part, high, low = pairs_step(u1, gen, part)
    plane = part + d + c + b
    b, c, d = neighbours(plane, Y_MASKS, Y_MASKS)
    plane, caps = nodes_step(high_nodes, cap, plane, "nodes_high")
    planes = jnp.stack([d, c, b, plane])
    other = swap(planes, CORE, CORE)
    return last_step(place, planes, other, caps, current, high, low)


def solution(mesh):
    in_specs = (P(None, "leaf"), P(None, None, "leaf"), P(None, None, "leaf"), P())
    return jax.shard_map(body, mesh=mesh, in_specs=in_specs, out_specs=P(None, "leaf"), check_vma=False)
```

```python
import functools

import jax
import jax.numpy as jnp
from jax import lax
from jax.experimental import pallas as pl
from jax.experimental.pallas import tpu as pltpu
from jax.sharding import PartitionSpec as P

F32 = jnp.float32
BF16 = jnp.bfloat16
RANK = 128
RHS = 64
DEVICES = 128
LIMITS = (53, 39, 38, 38, 40, 40, 44)
HBM = pl.BlockSpec(memory_space=pltpu.HBM)
VMEM = pl.BlockSpec(memory_space=pltpu.VMEM)
SMEM = pl.BlockSpec(memory_space=pltpu.SMEM)

CORE = 1
Z_MASKS = (6, 4, 2)
X_MASKS = (24, 16, 8)
Y_MASKS = (96, 64, 32)
X_PLACES = (3, 0, 1, 2)
Y_PLACES = (3, 0, 1, 2)


def split(value):
    high = value.astype(BF16)
    return high, (value - high.astype(F32)).astype(BF16)


def stacked(values):
    parts = [split(v) for v in values]
    return jnp.concatenate([h for h, _ in parts] + [l for _, l in parts], axis=0)


def product(left, right):
    lh, ll = split(left)
    rh, rl = split(right)
    rows = left.shape[0]
    both = jnp.dot(jnp.concatenate([lh, ll], axis=0), rh, preferred_element_type=F32)
    return both[:rows] + both[rows:] + jnp.dot(lh, rl, preferred_element_type=F32)


def contract(left, right):
    return lax.dot_general(left, right, (((1,), (1,)), ((), ())), preferred_element_type=F32)


def fold(total, rows):
    half = total.shape[1] // 2
    wide = total[:rows] + total[rows:]
    return wide[:, :half] + wide[:, half:]


def params(limit):
    return pltpu.CompilerParams(vmem_limit_bytes=limit << 20)


def spans(sizes, points):
    at = 0
    for size in sizes:
        yield pl.ds(at * points // 8, size * points // 8)
        at += size


def fetch(sources, sems, sizes, points):
    parts = []
    for i, cols in enumerate(spans(sizes, points)):
        row = []
        for j, (ref, level, buffer) in enumerate(sources):
            src = ref.at[:, cols] if level is None else ref.at[level, :, cols]
            row.append(pltpu.make_async_copy(src, buffer.at[:, cols], sems.at[i, j]))
        parts.append((cols, row))
    for _, row in parts:
        for copy in row:
            copy.start()
    return parts


def add_to(acc, value, first):
    if first:
        acc[...] = value
    else:
        acc[...] += value


PARTS = (2, 2, 2, 2)


def first_kernel(points, core_ref, rhs_ref, basis_ref, gen_ref, keep_ref, send_ref,
                 rhs_buf, v3_buf, v2_buf, u3_buf, acc2, acc3, sems):
    sources = ((rhs_ref, None, rhs_buf), (basis_ref, 3, v3_buf), (basis_ref, 2, v2_buf), (gen_ref, 3, u3_buf))
    for i, (cols, row) in enumerate(fetch(sources, sems, PARTS, points)):
        for copy in row:
            copy.wait()
        rhs = stacked([rhs_buf[:, cols]])
        left = jnp.concatenate([rhs, stacked([u3_buf[:, cols]])], axis=0)
        add_to(acc2, contract(left, stacked([v2_buf[:, cols]])), i == 0)
        add_to(acc3, contract(rhs, stacked([v3_buf[:, cols]])), i == 0)
    p3 = fold(acc3[...], RHS)
    p2 = fold(acc2[: 2 * RHS], RHS)
    g32 = fold(acc2[2 * RHS :], RANK)
    first = core_ref[0] == 0

    @pl.when(first)
    def _():
        keep_ref[:RHS] = p3
        keep_ref[RHS:] = p2
        send_ref[...] = g32

    @pl.when(jnp.logical_not(first))
    def _():
        send_ref[:RHS] = p3
        send_ref[RHS:] = p2
        keep_ref[...] = g32


def array(*shape):
    return jax.ShapeDtypeStruct(shape, F32)


def first_step(core, rhs, basis, gen):
    points = rhs.shape[1]
    wide = pltpu.VMEM((RANK, points), F32)
    return pl.pallas_call(
        functools.partial(first_kernel, points),
        out_shape=(array(RANK, RANK), array(RANK, RANK)),
        in_specs=[SMEM, HBM, HBM, HBM],
        out_specs=(VMEM,) * 2,
        scratch_shapes=[
            pltpu.VMEM((RHS, points), F32), wide, wide, wide,
            pltpu.VMEM((2 * (RHS + RANK), 2 * RANK), F32),
            pltpu.VMEM((2 * RHS, 2 * RANK), F32),
            pltpu.SemaphoreType.DMA((len(PARTS), 4)),
        ],
        compiler_params=params(LIMITS[0]),
        cost_estimate=pl.CostEstimate(flops=800_000_000, bytes_accessed=7_340_032, transcendentals=0),
        name="project_low",
    )(core, rhs, basis, gen)


def load_kernel(nodes_ref, basis_ref, gen_ref, cap_ref, sent_ref, sent_out,
                v1_ref, v0_ref, u3_ref, u2_ref, u1_ref, caps_ref, sems):
    sources = [
        (basis_ref, 1, v1_ref), (basis_ref, 0, v0_ref),
        (gen_ref, 3, u3_ref), (gen_ref, 2, u2_ref), (gen_ref, 1, u1_ref),
    ]
    sources += [(cap_ref, nodes_ref[i], caps_ref.at[i]) for i in range(6)]
    copies = [pltpu.make_async_copy(ref.at[k], out, sems.at[i]) for i, (ref, k, out) in enumerate(sources)]
    for copy in copies:
        copy.start()
    sent_out[...] = sent_ref[...]
    for copy in copies:
        copy.wait()


def load_step(nodes, basis, gen, cap, sent):
    wide = array(*basis.shape[1:])
    return pl.pallas_call(
        load_kernel,
        out_shape=(array(*sent.shape), wide, wide, wide, wide, wide, array(6, 2 * RANK, 2 * RANK)),
        in_specs=[SMEM, HBM, HBM, HBM, VMEM],
        out_specs=(VMEM,) * 7,
        scratch_shapes=[pltpu.SemaphoreType.DMA((11,))],
        compiler_params=params(LIMITS[1]),
        cost_estimate=pl.CostEstimate(flops=1_000, bytes_accessed=12_058_624, transcendentals=0),
        name="load_high",
    )(nodes, basis, gen, cap, sent)


def grams_kernel(rhs_ref, v1_ref, v0_ref, u3_ref, u2_ref, u1_ref, sent_ref, sent_out, p_ref, g_ref, g10_ref):
    sent_out[...] = sent_ref[...]
    left = stacked([rhs_ref[...], u3_ref[...]])
    u2 = stacked([u2_ref[...]])
    for k, ref in enumerate((v1_ref, v0_ref)):
        right = stacked([ref[...]])
        cols = slice(k * RANK, (k + 1) * RANK)
        both = fold(contract(left, right), RHS + RANK)
        p_ref[:, cols] = both[:RHS]
        g_ref[:RANK, cols] = both[RHS:]
        g_ref[RANK:, cols] = fold(contract(u2, right), RANK)
    g10_ref[...] = fold(contract(stacked([u1_ref[...]]), right), RANK)


def grams_step(rhs, v1, v0, u3, u2, u1, sent):
    return pl.pallas_call(
        grams_kernel,
        out_shape=(array(*sent.shape), array(RHS, 2 * RANK), array(2 * RANK, 2 * RANK), array(RANK, RANK)),
        in_specs=[VMEM] * 7,
        out_specs=(VMEM,) * 4,
        compiler_params=params(LIMITS[2]),
        cost_estimate=pl.CostEstimate(flops=3_200_000_000, bytes_accessed=11_534_336, transcendentals=0),
        name="grams_high",
    )(rhs, v1, v0, u3, u2, u1, sent)


def related(caps_ref, node, s, columns):
    blocks = []
    for row in (1 - s, s):
        rows = pl.ds(pl.multiple_of(row * RANK, RANK), RANK)
        blocks.append(
            jnp.concatenate(
                [
                    caps_ref[node, rows, pl.ds(pl.multiple_of(col * RANK, RANK), RANK)]
                    for col in (s, 1 - s)[:columns]
                ],
                axis=1,
            )
        )
    return jnp.concatenate(blocks, axis=0)


def middle_kernel(place_ref, mine_ref, other_ref, caps_ref, p_ref, g_ref, g10_ref,
                  t_ref, keep_ref, send_ref):
    first = place_ref[0] == 0
    p, g = [], []
    for m in range(4):
        mine, other = mine_ref[X_PLACES[m]], other_ref[X_PLACES[m]]
        p.append(jnp.where(first, mine, other))
        g.append(jnp.where(first, other, mine))
    t = []
    for pair in (0, 2):
        joined = jnp.concatenate([p[pair][:RHS], p[pair + 1][:RHS]], axis=1)
        both = product(joined, related(caps_ref, pair // 2, place_ref[1], 2))
        t += [both[:, :RANK], both[:, RANK:]]
    q2 = [p[m][RHS:] - product(t[m], g[m]) for m in range(4)]
    joined = jnp.concatenate([q2[0] + q2[1], q2[2] + q2[3]], axis=1)
    coeff = jnp.concatenate([t[0], product(joined, related(caps_ref, 2, place_ref[2], 1))], axis=1)
    t_ref[...] = coeff
    q = p_ref[...] - product(coeff, g_ref[...])
    half = RHS // 2

    def put(ref, c):
        rows = slice(c * half, (c + 1) * half)
        ref[:half] = q[rows, :RANK]
        ref[half : 2 * half] = q[rows, RANK:]
        ref[2 * half :] = g10_ref[c * RHS : (c + 1) * RHS]

    @pl.when(first)
    def _():
        put(keep_ref, 0)
        put(send_ref, 1)

    @pl.when(jnp.logical_not(first))
    def _():
        put(keep_ref, 1)
        put(send_ref, 0)


def middle_step(place, mine, other, caps, p, g, g10):
    half = jax.ShapeDtypeStruct((RANK, RANK), F32)
    return pl.pallas_call(
        middle_kernel,
        out_shape=(jax.ShapeDtypeStruct((RHS, 2 * RANK), F32), half, half),
        in_specs=[SMEM] + [VMEM] * 6,
        out_specs=(VMEM,) * 3,
        compiler_params=params(LIMITS[3]),
        cost_estimate=pl.CostEstimate(flops=120_000_000, bytes_accessed=1_500_000, transcendentals=0),
        name="coefficients_low",
    )(place, mine, other, caps, p, g, g10)


def low_update_kernel(t_ref, rhs_ref, u3_ref, u2_ref, sent_ref, cur_ref, sent_out):
    sent_out[...] = sent_ref[...]
    th, tl = split(t_ref[...])
    left = jnp.concatenate([th, tl], axis=0)
    for cols in spans((2,) * 4, rhs_ref.shape[1]):
        gh, gl = split(jnp.concatenate([u3_ref[:, cols], u2_ref[:, cols]], axis=0))
        both = jnp.dot(left, gh, preferred_element_type=F32)
        update = both[:RHS] + both[RHS:] + jnp.dot(th, gl, preferred_element_type=F32)
        cur_ref[:, cols] = rhs_ref[:, cols] - update


def low_update(t, rhs, u3, u2, sent):
    return pl.pallas_call(
        low_update_kernel,
        out_shape=(array(*rhs.shape), array(*sent.shape)),
        in_specs=[VMEM] * 5,
        out_specs=(VMEM, VMEM),
        compiler_params=params(LIMITS[4]),
        cost_estimate=pl.CostEstimate(flops=402_653_184, bytes_accessed=6_291_456, transcendentals=0),
        name="update_low",
    )(t, rhs, u3, u2, sent)


def pairs_kernel(u1_ref, gen_ref, sent_ref, sent_out, high_ref, low_ref, u0_ref, sem):
    copy = pltpu.make_async_copy(gen_ref.at[0], u0_ref, sem)
    copy.start()
    sent_out[...] = sent_ref[...]
    high_ref[:RANK], low_ref[:RANK] = split(u1_ref[...])
    copy.wait()
    high_ref[RANK:], low_ref[RANK:] = split(u0_ref[...])


def pairs_step(u1, gen, sent):
    pair = jax.ShapeDtypeStruct((2 * RANK, u1.shape[1]), BF16)
    return pl.pallas_call(
        pairs_kernel,
        out_shape=(array(*sent.shape), pair, pair),
        in_specs=[VMEM, HBM, VMEM],
        out_specs=(VMEM,) * 3,
        scratch_shapes=[pltpu.VMEM(u1.shape, F32), pltpu.SemaphoreType.DMA(())],
        compiler_params=params(LIMITS[5]),
        cost_estimate=pl.CostEstimate(flops=100_000_000, bytes_accessed=8_388_608, transcendentals=0),
        name="pairs_high",
    )(u1, gen, sent)


def last_kernel(place_ref, mine_ref, other_ref, caps_ref, cur_ref, high_ref, low_ref, out_ref,
                buf, sems):
    first = place_ref[0] == 0
    half = RHS // 2
    q1, q0, g = [], [], []
    for m in range(4):
        mine, other = mine_ref[Y_PLACES[m]], other_ref[Y_PLACES[m]]
        low = jnp.where(first, mine, other)
        high = jnp.where(first, other, mine)
        q1.append(jnp.concatenate([low[:half], high[:half]], axis=0))
        q0.append(jnp.concatenate([low[half:RHS], high[half:RHS]], axis=0))
        g.append(jnp.concatenate([low[RHS:], high[RHS:]], axis=0))
    t = []
    for pair in (0, 2):
        both = product(
            jnp.concatenate([q1[pair], q1[pair + 1]], axis=1), related(caps_ref, 3 + pair // 2, place_ref[3], 2)
        )
        t += [both[:, :RANK], both[:, RANK:]]
    r = [q0[m] - product(t[m], g[m]) for m in range(4)]
    joined = jnp.concatenate([r[0] + r[1], r[2] + r[3]], axis=1)
    th, tl = split(jnp.concatenate([t[0], product(joined, related(caps_ref, 5, place_ref[4], 1))], axis=1))
    left = jnp.concatenate([th, tl], axis=0)
    copies = []
    for i, cols in enumerate(spans((2,) * 4, cur_ref.shape[1])):
        both = jnp.dot(left, high_ref[:, cols], preferred_element_type=F32)
        update = both[:RHS] + both[RHS:] + jnp.dot(th, low_ref[:, cols], preferred_element_type=F32)
        buf[:, cols] = cur_ref[:, cols] - update
        copy = pltpu.make_async_copy(buf.at[:, cols], out_ref.at[:, cols], sems.at[i])
        copy.start()
        copies.append(copy)
    for copy in copies:
        copy.wait()


def last_step(place, mine, other, caps, cur, high, low):
    return pl.pallas_call(
        last_kernel,
        out_shape=array(*cur.shape),
        in_specs=[SMEM] + [VMEM] * 6,
        out_specs=HBM,
        scratch_shapes=[pltpu.VMEM(cur.shape, F32), pltpu.SemaphoreType.DMA((4,))],
        compiler_params=params(LIMITS[6]),
        cost_estimate=pl.CostEstimate(flops=500_000_000, bytes_accessed=7_000_000, transcendentals=0),
        name="update_high",
    )(place, mine, other, caps, cur, high, low)


def swap(value, even, odd):
    pairs = [(i, i ^ (odd if i & CORE else even)) for i in range(DEVICES)]
    return lax.ppermute(value, "leaf", pairs)


def neighbours(value, even, odd):
    three, two, one = (swap(value, e, o) for e, o in zip(even, odd))
    return one, two, three


def body(rhs, basis, gen, cap):
    device = lax.axis_index("leaf").astype(jnp.int32)
    core = (device & 1).reshape(1)
    place = jnp.stack([device & 1, device >> 3 & 1, device >> 4 & 1, device >> 5 & 1, device >> 6 & 1])
    n3, n2, n1 = device >> 4, device >> 5, device >> 6
    nodes = jnp.stack([7 + n3, 7 + (n3 ^ 1), 3 + n2, 1 + n1, 1 + (n1 ^ 1), jnp.zeros_like(n1)])
    keep, send = first_step(core, rhs, basis, gen)
    chip = keep + swap(send, CORE, CORE)
    b, c, d = neighbours(chip, Z_MASKS, Z_MASKS)
    chip, v1, v0, u3, u2, u1, caps = load_step(nodes, basis, gen, cap, chip)
    line = chip + b + c + d
    b, c, d = neighbours(line, X_MASKS, X_MASKS)
    line, p, g, g10 = grams_step(rhs, v1, v0, u3, u2, u1, line)
    lines = jnp.stack([b, c, d, line])
    other = swap(lines, CORE, CORE)
    t, keep, send = middle_step(place, lines, other, caps, p, g, g10)
    chip = keep + swap(send, CORE, CORE)
    b, c, d = neighbours(chip, X_MASKS, Z_MASKS)
    current, chip = low_update(t, rhs, u3, u2, chip)
    part = chip + b + c + d
    b, c, d = neighbours(part, Z_MASKS, X_MASKS)
    part, high, low = pairs_step(u1, gen, part)
    plane = part + b + c + d
    b, c, d = neighbours(plane, Y_MASKS, Y_MASKS)
    planes = jnp.stack([b, c, d, plane])
    other = swap(planes, CORE, CORE)
    return last_step(place, planes, other, caps, current, high, low)


def solution(mesh):
    in_specs = (P(None, "leaf"), P(None, None, "leaf"), P(None, None, "leaf"), P())
    return jax.shard_map(body, mesh=mesh, in_specs=in_specs, out_specs=P(None, "leaf"), check_vma=False)
```

```python
import functools

import jax
import jax.numpy as jnp
from jax import lax
from jax.experimental import pallas as pl
from jax.experimental.pallas import tpu as pltpu
from jax.sharding import PartitionSpec as P

F32 = jnp.float32
BF16 = jnp.bfloat16
RANK = 128
RHS = 64
DEVICES = 128
LIMITS = (53, 39, 38, 38, 40, 40, 44)
HBM = pl.BlockSpec(memory_space=pltpu.HBM)
VMEM = pl.BlockSpec(memory_space=pltpu.VMEM)
SMEM = pl.BlockSpec(memory_space=pltpu.SMEM)

CORE = 1
Z_MASKS = (6, 4, 2)
X_MASKS = (24, 16, 8)
Y_MASKS = (96, 64, 32)
X_PLACES = (3, 0, 1, 2)
Y_PLACES = (3, 0, 1, 2)


def split(value):
    high = value.astype(BF16)
    return high, (value - high.astype(F32)).astype(BF16)


def stacked(values):
    parts = [split(v) for v in values]
    return jnp.concatenate([h for h, _ in parts] + [l for _, l in parts], axis=0)


def product(left, right):
    lh, ll = split(left)
    rh, rl = split(right)
    rows = left.shape[0]
    both = jnp.dot(jnp.concatenate([lh, ll], axis=0), rh, preferred_element_type=F32)
    return both[:rows] + both[rows:] + jnp.dot(lh, rl, preferred_element_type=F32)


def contract(left, right):
    return lax.dot_general(left, right, (((1,), (1,)), ((), ())), preferred_element_type=F32)


def fold(total, rows):
    half = total.shape[1] // 2
    wide = total[:rows] + total[rows:]
    return wide[:, :half] + wide[:, half:]


def params(limit):
    return pltpu.CompilerParams(vmem_limit_bytes=limit << 20)


def spans(sizes, points):
    at = 0
    for size in sizes:
        yield pl.ds(at * points // 8, size * points // 8)
        at += size


def fetch(sources, sems, sizes, points):
    parts = []
    for i, cols in enumerate(spans(sizes, points)):
        row = []
        for j, (ref, level, buffer) in enumerate(sources):
            src = ref.at[:, cols] if level is None else ref.at[level, :, cols]
            row.append(pltpu.make_async_copy(src, buffer.at[:, cols], sems.at[i, j]))
        parts.append((cols, row))
    for _, row in parts:
        for copy in row:
            copy.start()
    return parts


def add_to(acc, value, first):
    if first:
        acc[...] = value
    else:
        acc[...] += value


PARTS = (2, 2, 2, 2)


def first_kernel(points, info_ref, rhs_ref, basis_ref, gen_ref, keep_ref, send_ref,
                 rhs_buf, v3_buf, v2_buf, u3_buf, acc2, acc3, sems):
    sources = ((rhs_ref, None, rhs_buf), (basis_ref, 3, v3_buf), (basis_ref, 2, v2_buf), (gen_ref, 3, u3_buf))
    for i, (cols, row) in enumerate(fetch(sources, sems, PARTS, points)):
        for copy in row:
            copy.wait()
        rhs = stacked([rhs_buf[:, cols]])
        left = jnp.concatenate([rhs, stacked([u3_buf[:, cols]])], axis=0)
        add_to(acc2, contract(left, stacked([v2_buf[:, cols]])), i == 0)
        add_to(acc3, contract(rhs, stacked([v3_buf[:, cols]])), i == 0)
    p3 = fold(acc3[...], RHS)
    p2 = fold(acc2[: 2 * RHS], RHS)
    g32 = fold(acc2[2 * RHS :], RANK)
    first = info_ref[0] == 0

    @pl.when(first)
    def _():
        keep_ref[:RHS] = p3
        keep_ref[RHS:] = p2
        send_ref[...] = g32

    @pl.when(jnp.logical_not(first))
    def _():
        send_ref[:RHS] = p3
        send_ref[RHS:] = p2
        keep_ref[...] = g32


def array(*shape):
    return jax.ShapeDtypeStruct(shape, F32)


def first_step(info, rhs, basis, gen):
    points = rhs.shape[1]
    wide = pltpu.VMEM((RANK, points), F32)
    return pl.pallas_call(
        functools.partial(first_kernel, points),
        out_shape=(array(RANK, RANK), array(RANK, RANK)),
        in_specs=[SMEM, HBM, HBM, HBM],
        out_specs=(VMEM,) * 2,
        scratch_shapes=[
            pltpu.VMEM((RHS, points), F32), wide, wide, wide,
            pltpu.VMEM((2 * (RHS + RANK), 2 * RANK), F32),
            pltpu.VMEM((2 * RHS, 2 * RANK), F32),
            pltpu.SemaphoreType.DMA((len(PARTS), 4)),
        ],
        compiler_params=params(LIMITS[0]),
        cost_estimate=pl.CostEstimate(flops=800_000_000, bytes_accessed=7_340_032, transcendentals=0),
        name="project_low",
    )(info, rhs, basis, gen)


def load_kernel(info_ref, basis_ref, gen_ref, cap_ref, sent_ref, sent_out,
                v1_ref, v0_ref, u3_ref, u2_ref, u1_ref, caps_ref, sems):
    sources = [
        (basis_ref, 1, v1_ref), (basis_ref, 0, v0_ref),
        (gen_ref, 3, u3_ref), (gen_ref, 2, u2_ref), (gen_ref, 1, u1_ref),
    ]
    sources += [(cap_ref, info_ref[6 + i], caps_ref.at[i]) for i in range(6)]
    copies = [pltpu.make_async_copy(ref.at[k], out, sems.at[i]) for i, (ref, k, out) in enumerate(sources)]
    for copy in copies:
        copy.start()
    sent_out[...] = sent_ref[...]
    for copy in copies:
        copy.wait()


def load_step(info, basis, gen, cap, sent):
    wide = array(*basis.shape[1:])
    return pl.pallas_call(
        load_kernel,
        out_shape=(array(*sent.shape), wide, wide, wide, wide, wide, array(6, 2 * RANK, 2 * RANK)),
        in_specs=[SMEM, HBM, HBM, HBM, VMEM],
        out_specs=(VMEM,) * 7,
        scratch_shapes=[pltpu.SemaphoreType.DMA((11,))],
        compiler_params=params(LIMITS[1]),
        cost_estimate=pl.CostEstimate(flops=1_000, bytes_accessed=12_058_624, transcendentals=0),
        name="load_high",
    )(info, basis, gen, cap, sent)


def grams_kernel(rhs_ref, v1_ref, v0_ref, u3_ref, u2_ref, u1_ref, sent_ref, sent_out, p_ref, g_ref, g10_ref):
    sent_out[...] = sent_ref[...]
    left = stacked([rhs_ref[...], u3_ref[...]])
    u2 = stacked([u2_ref[...]])
    for k, ref in enumerate((v1_ref, v0_ref)):
        right = stacked([ref[...]])
        cols = slice(k * RANK, (k + 1) * RANK)
        both = fold(contract(left, right), RHS + RANK)
        p_ref[:, cols] = both[:RHS]
        g_ref[:RANK, cols] = both[RHS:]
        g_ref[RANK:, cols] = fold(contract(u2, right), RANK)
    g10_ref[...] = fold(contract(stacked([u1_ref[...]]), right), RANK)


def grams_step(rhs, v1, v0, u3, u2, u1, sent):
    return pl.pallas_call(
        grams_kernel,
        out_shape=(array(*sent.shape), array(RHS, 2 * RANK), array(2 * RANK, 2 * RANK), array(RANK, RANK)),
        in_specs=[VMEM] * 7,
        out_specs=(VMEM,) * 4,
        compiler_params=params(LIMITS[2]),
        cost_estimate=pl.CostEstimate(flops=3_200_000_000, bytes_accessed=11_534_336, transcendentals=0),
        name="grams_high",
    )(rhs, v1, v0, u3, u2, u1, sent)


def related(caps_ref, node, s, columns):
    blocks = []
    for row in (1 - s, s):
        rows = pl.ds(pl.multiple_of(row * RANK, RANK), RANK)
        blocks.append(
            jnp.concatenate(
                [
                    caps_ref[node, rows, pl.ds(pl.multiple_of(col * RANK, RANK), RANK)]
                    for col in (s, 1 - s)[:columns]
                ],
                axis=1,
            )
        )
    return jnp.concatenate(blocks, axis=0)


def middle_kernel(info_ref, mine_ref, other_ref, caps_ref, p_ref, g_ref, g10_ref,
                  t_ref, keep_ref, send_ref):
    first = info_ref[0] == 0
    p, g = [], []
    for m in range(4):
        mine, other = mine_ref[X_PLACES[m]], other_ref[X_PLACES[m]]
        p.append(jnp.where(first, mine, other))
        g.append(jnp.where(first, other, mine))
    t = []
    for pair in (0, 2):
        joined = jnp.concatenate([p[pair][:RHS], p[pair + 1][:RHS]], axis=1)
        both = product(joined, related(caps_ref, pair // 2, info_ref[2], 2))
        t += [both[:, :RANK], both[:, RANK:]]
    q2 = [p[m][RHS:] - product(t[m], g[m]) for m in range(4)]
    joined = jnp.concatenate([q2[0] + q2[1], q2[2] + q2[3]], axis=1)
    coeff = jnp.concatenate([t[0], product(joined, related(caps_ref, 2, info_ref[3], 1))], axis=1)
    t_ref[...] = coeff
    q = p_ref[...] - product(coeff, g_ref[...])
    half = RHS // 2

    def put(ref, c):
        rows = slice(c * half, (c + 1) * half)
        ref[:half] = q[rows, :RANK]
        ref[half : 2 * half] = q[rows, RANK:]
        ref[2 * half :] = g10_ref[c * RHS : (c + 1) * RHS]

    low_half = info_ref[1] == 0

    @pl.when(low_half)
    def _():
        put(keep_ref, 0)
        put(send_ref, 1)

    @pl.when(jnp.logical_not(low_half))
    def _():
        put(keep_ref, 1)
        put(send_ref, 0)


def middle_step(info, mine, other, caps, p, g, g10):
    half = jax.ShapeDtypeStruct((RANK, RANK), F32)
    return pl.pallas_call(
        middle_kernel,
        out_shape=(jax.ShapeDtypeStruct((RHS, 2 * RANK), F32), half, half),
        in_specs=[SMEM] + [VMEM] * 6,
        out_specs=(VMEM,) * 3,
        compiler_params=params(LIMITS[3]),
        cost_estimate=pl.CostEstimate(flops=120_000_000, bytes_accessed=1_500_000, transcendentals=0),
        name="coefficients_low",
    )(info, mine, other, caps, p, g, g10)


def low_update_kernel(t_ref, rhs_ref, u3_ref, u2_ref, sent_ref, cur_ref, sent_out):
    sent_out[...] = sent_ref[...]
    th, tl = split(t_ref[...])
    left = jnp.concatenate([th, tl], axis=0)
    for cols in spans((2,) * 4, rhs_ref.shape[1]):
        gh, gl = split(jnp.concatenate([u3_ref[:, cols], u2_ref[:, cols]], axis=0))
        both = jnp.dot(left, gh, preferred_element_type=F32)
        update = both[:RHS] + both[RHS:] + jnp.dot(th, gl, preferred_element_type=F32)
        cur_ref[:, cols] = rhs_ref[:, cols] - update


def low_update(t, rhs, u3, u2, sent):
    return pl.pallas_call(
        low_update_kernel,
        out_shape=(array(*rhs.shape), array(*sent.shape)),
        in_specs=[VMEM] * 5,
        out_specs=(VMEM, VMEM),
        compiler_params=params(LIMITS[4]),
        cost_estimate=pl.CostEstimate(flops=402_653_184, bytes_accessed=6_291_456, transcendentals=0),
        name="update_low",
    )(t, rhs, u3, u2, sent)


def pairs_kernel(u1_ref, gen_ref, sent_ref, sent_out, high_ref, low_ref, u0_ref, sem):
    copy = pltpu.make_async_copy(gen_ref.at[0], u0_ref, sem)
    copy.start()
    sent_out[...] = sent_ref[...]
    high_ref[:RANK], low_ref[:RANK] = split(u1_ref[...])
    copy.wait()
    high_ref[RANK:], low_ref[RANK:] = split(u0_ref[...])


def pairs_step(u1, gen, sent):
    pair = jax.ShapeDtypeStruct((2 * RANK, u1.shape[1]), BF16)
    return pl.pallas_call(
        pairs_kernel,
        out_shape=(array(*sent.shape), pair, pair),
        in_specs=[VMEM, HBM, VMEM],
        out_specs=(VMEM,) * 3,
        scratch_shapes=[pltpu.VMEM(u1.shape, F32), pltpu.SemaphoreType.DMA(())],
        compiler_params=params(LIMITS[5]),
        cost_estimate=pl.CostEstimate(flops=100_000_000, bytes_accessed=8_388_608, transcendentals=0),
        name="pairs_high",
    )(u1, gen, sent)


def last_kernel(info_ref, mine_ref, other_ref, caps_ref, cur_ref, high_ref, low_ref, out_ref,
                buf, sems):
    first = info_ref[1] == 0
    half = RHS // 2
    q1, q0, g = [], [], []
    for m in range(4):
        mine, other = mine_ref[Y_PLACES[m]], other_ref[Y_PLACES[m]]
        low = jnp.where(first, mine, other)
        high = jnp.where(first, other, mine)
        q1.append(jnp.concatenate([low[:half], high[:half]], axis=0))
        q0.append(jnp.concatenate([low[half:RHS], high[half:RHS]], axis=0))
        g.append(jnp.concatenate([low[RHS:], high[RHS:]], axis=0))
    t = []
    for pair in (0, 2):
        both = product(
            jnp.concatenate([q1[pair], q1[pair + 1]], axis=1), related(caps_ref, 3 + pair // 2, info_ref[4], 2)
        )
        t += [both[:, :RANK], both[:, RANK:]]
    r = [q0[m] - product(t[m], g[m]) for m in range(4)]
    joined = jnp.concatenate([r[0] + r[1], r[2] + r[3]], axis=1)
    th, tl = split(jnp.concatenate([t[0], product(joined, related(caps_ref, 5, info_ref[5], 1))], axis=1))
    left = jnp.concatenate([th, tl], axis=0)
    copies = []
    for i, cols in enumerate(spans((2,) * 4, cur_ref.shape[1])):
        both = jnp.dot(left, high_ref[:, cols], preferred_element_type=F32)
        update = both[:RHS] + both[RHS:] + jnp.dot(th, low_ref[:, cols], preferred_element_type=F32)
        buf[:, cols] = cur_ref[:, cols] - update
        copy = pltpu.make_async_copy(buf.at[:, cols], out_ref.at[:, cols], sems.at[i])
        copy.start()
        copies.append(copy)
    for copy in copies:
        copy.wait()


def last_step(info, mine, other, caps, cur, high, low):
    return pl.pallas_call(
        last_kernel,
        out_shape=array(*cur.shape),
        in_specs=[SMEM] + [VMEM] * 6,
        out_specs=HBM,
        scratch_shapes=[pltpu.VMEM(cur.shape, F32), pltpu.SemaphoreType.DMA((4,))],
        compiler_params=params(LIMITS[6]),
        cost_estimate=pl.CostEstimate(flops=500_000_000, bytes_accessed=7_000_000, transcendentals=0),
        name="update_high",
    )(info, mine, other, caps, cur, high, low)


def swap(value, mask):
    return lax.ppermute(value, "leaf", [(i, i ^ mask) for i in range(DEVICES)])


def parity(index):
    return bin(index).count("1") & 1


def crossed(value, even, odd):
    def partner(i):
        mask = odd if parity(i & 31) else even
        return i ^ mask ^ parity(mask)

    return lax.ppermute(value, "leaf", [(i, partner(i)) for i in range(DEVICES)])


def neighbours(value, masks):
    three, two, one = (swap(value, m) for m in masks)
    return one, two, three


def crossed_neighbours(value, even, odd):
    three, two, one = (crossed(value, e, o) for e, o in zip(even, odd))
    return one, two, three


def body(rhs, basis, gen, cap):
    device = lax.axis_index("leaf").astype(jnp.int32)
    bit = [device >> k & 1 for k in range(7)]
    n3, n2, n1 = device >> 4, device >> 5, device >> 6
    half = bit[0] ^ bit[1] ^ bit[2] ^ bit[3] ^ bit[4]
    info = jnp.stack([bit[0], half, *bit[3:], 7 + n3, 7 + (n3 ^ 1), 3 + n2, 1 + n1, 1 + (n1 ^ 1), jnp.zeros_like(n1)])
    keep, send = first_step(info, rhs, basis, gen)
    chip = keep + swap(send, CORE)
    b, c, d = neighbours(chip, Z_MASKS)
    chip, v1, v0, u3, u2, u1, caps = load_step(info, basis, gen, cap, chip)
    line = chip + b + c + d
    b, c, d = neighbours(line, X_MASKS)
    line, p, g, g10 = grams_step(rhs, v1, v0, u3, u2, u1, line)
    lines = jnp.stack([b, c, d, line])
    other = swap(lines, CORE)
    t, keep, send = middle_step(info, lines, other, caps, p, g, g10)
    chip = keep + swap(send, CORE)
    b, c, d = crossed_neighbours(chip, X_MASKS, Z_MASKS)
    current, chip = low_update(t, rhs, u3, u2, chip)
    part = chip + b + c + d
    b, c, d = crossed_neighbours(part, Z_MASKS, X_MASKS)
    part, high, low = pairs_step(u1, gen, part)
    plane = part + b + c + d
    b, c, d = neighbours(plane, Y_MASKS)
    planes = jnp.stack([b, c, d, plane])
    other = swap(planes, CORE)
    return last_step(info, planes, other, caps, current, high, low)


def solution(mesh):
    in_specs = (P(None, "leaf"), P(None, None, "leaf"), P(None, None, "leaf"), P())
    return jax.shard_map(body, mesh=mesh, in_specs=in_specs, out_specs=P(None, "leaf"), check_vma=False)
```

```python
import functools

import jax
import jax.numpy as jnp
from jax import lax
from jax.experimental import pallas as pl
from jax.experimental.pallas import tpu as pltpu
from jax.sharding import PartitionSpec as P

F32 = jnp.float32
BF16 = jnp.bfloat16
RANK = 128
RHS = 64
DEVICES = 128
LIMITS = (53, 39, 38, 38, 40, 40, 44)
HBM = pl.BlockSpec(memory_space=pltpu.HBM)
VMEM = pl.BlockSpec(memory_space=pltpu.VMEM)

CORE = 1
Z_MASKS = (6, 4, 2)
X_MASKS = (24, 16, 8)
Y_MASKS = (96, 64, 32)
X_PLACES = (3, 0, 1, 2)
Y_PLACES = (3, 0, 1, 2)


def position():
    device = lax.axis_index("leaf").astype(jnp.int32)
    return device, [device >> k & 1 for k in range(7)]


def half_of(bit):
    return bit[0] ^ bit[1] ^ bit[2] ^ bit[3] ^ bit[4]


def split(value):
    high = value.astype(BF16)
    return high, (value - high.astype(F32)).astype(BF16)


def stacked(values):
    parts = [split(v) for v in values]
    return jnp.concatenate([h for h, _ in parts] + [l for _, l in parts], axis=0)


def product(left, right):
    lh, ll = split(left)
    rh, rl = split(right)
    rows = left.shape[0]
    both = jnp.dot(jnp.concatenate([lh, ll], axis=0), rh, preferred_element_type=F32)
    return both[:rows] + both[rows:] + jnp.dot(lh, rl, preferred_element_type=F32)


def product_of(left, high, low):
    lh, ll = split(left)
    rows = left.shape[0]
    both = jnp.dot(jnp.concatenate([lh, ll], axis=0), high, preferred_element_type=F32)
    return both[:rows] + both[rows:] + jnp.dot(lh, low, preferred_element_type=F32)


def contract(left, right):
    return lax.dot_general(left, right, (((1,), (1,)), ((), ())), preferred_element_type=F32)


def fold(total, rows):
    half = total.shape[1] // 2
    wide = total[:rows] + total[rows:]
    return wide[:, :half] + wide[:, half:]


def params(limit):
    return pltpu.CompilerParams(vmem_limit_bytes=limit << 20)


def spans(sizes, points):
    at = 0
    for size in sizes:
        yield pl.ds(at * points // 8, size * points // 8)
        at += size


def fetch(sources, sems, sizes, points):
    parts = []
    for i, cols in enumerate(spans(sizes, points)):
        row = []
        for j, (ref, level, buffer) in enumerate(sources):
            src = ref.at[:, cols] if level is None else ref.at[level, :, cols]
            row.append(pltpu.make_async_copy(src, buffer.at[:, cols], sems.at[i, j]))
        parts.append((cols, row))
    for _, row in parts:
        for copy in row:
            copy.start()
    return parts


def add_to(acc, value, first):
    if first:
        acc[...] = value
    else:
        acc[...] += value


PARTS = (2, 2, 2, 2)


def first_kernel(points, rhs_ref, basis_ref, gen_ref, keep_ref, send_ref,
                 rhs_buf, v3_buf, v2_buf, u3_buf, acc2, acc3, sems):
    sources = ((rhs_ref, None, rhs_buf), (basis_ref, 3, v3_buf), (basis_ref, 2, v2_buf), (gen_ref, 3, u3_buf))
    for i, (cols, row) in enumerate(fetch(sources, sems, PARTS, points)):
        for copy in row:
            copy.wait()
        rhs = stacked([rhs_buf[:, cols]])
        left = jnp.concatenate([rhs, stacked([u3_buf[:, cols]])], axis=0)
        add_to(acc2, contract(left, stacked([v2_buf[:, cols]])), i == 0)
        add_to(acc3, contract(rhs, stacked([v3_buf[:, cols]])), i == 0)
    p3 = fold(acc3[...], RHS)
    p2 = fold(acc2[: 2 * RHS], RHS)
    g32 = fold(acc2[2 * RHS :], RANK)
    first = position()[1][0] == 0

    @pl.when(first)
    def _():
        keep_ref[:RHS] = p3
        keep_ref[RHS:] = p2
        send_ref[...] = g32

    @pl.when(jnp.logical_not(first))
    def _():
        send_ref[:RHS] = p3
        send_ref[RHS:] = p2
        keep_ref[...] = g32


def array(*shape):
    return jax.ShapeDtypeStruct(shape, F32)


def half_array(*shape):
    return jax.ShapeDtypeStruct(shape, BF16)


def first_step(rhs, basis, gen):
    points = rhs.shape[1]
    wide = pltpu.VMEM((RANK, points), F32)
    return pl.pallas_call(
        functools.partial(first_kernel, points),
        out_shape=(array(RANK, RANK), array(RANK, RANK)),
        in_specs=[HBM, HBM, HBM],
        out_specs=(VMEM,) * 2,
        scratch_shapes=[
            pltpu.VMEM((RHS, points), F32), wide, wide, wide,
            pltpu.VMEM((2 * (RHS + RANK), 2 * RANK), F32),
            pltpu.VMEM((2 * RHS, 2 * RANK), F32),
            pltpu.SemaphoreType.DMA((len(PARTS), 4)),
        ],
        compiler_params=params(LIMITS[0]),
        cost_estimate=pl.CostEstimate(flops=800_000_000, bytes_accessed=7_340_032, transcendentals=0),
        name="project_low",
    )(rhs, basis, gen)


def load_kernel(basis_ref, gen_ref, cap_ref, sent_ref, sent_out,
                v1_ref, v0_ref, u3_ref, u2_ref, u1_ref, caps_ref, sems):
    sources = [
        (basis_ref, 1, v1_ref), (basis_ref, 0, v0_ref),
        (gen_ref, 3, u3_ref), (gen_ref, 2, u2_ref), (gen_ref, 1, u1_ref),
    ]
    device, _ = position()
    n3, n2, n1 = device >> 4, device >> 5, device >> 6
    nodes = (7 + n3, 7 + (n3 ^ 1), 3 + n2, 1 + n1, 1 + (n1 ^ 1), 0)
    sources += [(cap_ref, node, caps_ref.at[i]) for i, node in enumerate(nodes)]
    copies = [pltpu.make_async_copy(ref.at[k], out, sems.at[i]) for i, (ref, k, out) in enumerate(sources)]
    for copy in copies:
        copy.start()
    sent_out[...] = sent_ref[...]
    for copy in copies:
        copy.wait()


def load_step(basis, gen, cap, sent):
    wide = array(*basis.shape[1:])
    return pl.pallas_call(
        load_kernel,
        out_shape=(array(*sent.shape), wide, wide, wide, wide, wide, array(6, 2 * RANK, 2 * RANK)),
        in_specs=[HBM, HBM, HBM, VMEM],
        out_specs=(VMEM,) * 7,
        scratch_shapes=[pltpu.SemaphoreType.DMA((11,))],
        compiler_params=params(LIMITS[1]),
        cost_estimate=pl.CostEstimate(flops=1_000, bytes_accessed=12_058_624, transcendentals=0),
        name="load_high",
    )(basis, gen, cap, sent)


def ordered(caps_ref, base, s_high, s_low, high_ref, low_ref):
    for i, (s, columns) in enumerate(((s_high, 2), (s_high, 2), (s_low, 1))):
        for r, row in enumerate((1 - s, s)):
            for c, col in enumerate((s, 1 - s)[:columns]):
                high, low = split(
                    caps_ref[
                        base + i,
                        pl.ds(pl.multiple_of(row * RANK, RANK), RANK),
                        pl.ds(pl.multiple_of(col * RANK, RANK), RANK),
                    ]
                )
                high_ref[i, r * RANK : (r + 1) * RANK, c * RANK : (c + 1) * RANK] = high
                low_ref[i, r * RANK : (r + 1) * RANK, c * RANK : (c + 1) * RANK] = low


def grams_kernel(rhs_ref, v1_ref, v0_ref, u3_ref, u2_ref, u1_ref, caps_ref, sent_ref, sent_out,
                 p_ref, gh_ref, gl_ref, g10_ref, ch_ref, cl_ref):
    sent_out[...] = sent_ref[...]
    _, bit = position()
    ordered(caps_ref, 0, bit[3], bit[4], ch_ref, cl_ref)
    left = stacked([rhs_ref[...], u3_ref[...]])
    u2 = stacked([u2_ref[...]])
    for k, ref in enumerate((v1_ref, v0_ref)):
        right = stacked([ref[...]])
        cols = slice(k * RANK, (k + 1) * RANK)
        both = fold(contract(left, right), RHS + RANK)
        p_ref[:, cols] = both[:RHS]
        gh_ref[:RANK, cols], gl_ref[:RANK, cols] = split(both[RHS:])
        gh_ref[RANK:, cols], gl_ref[RANK:, cols] = split(fold(contract(u2, right), RANK))
    g10_ref[...] = fold(contract(stacked([u1_ref[...]]), right), RANK)


def grams_step(rhs, v1, v0, u3, u2, u1, caps, sent):
    return pl.pallas_call(
        grams_kernel,
        out_shape=(
            array(*sent.shape), array(RHS, 2 * RANK), half_array(2 * RANK, 2 * RANK), half_array(2 * RANK, 2 * RANK),
            array(RANK, RANK), half_array(3, 2 * RANK, 2 * RANK), half_array(3, 2 * RANK, 2 * RANK),
        ),
        in_specs=[VMEM] * 8,
        out_specs=(VMEM,) * 7,
        compiler_params=params(LIMITS[2]),
        cost_estimate=pl.CostEstimate(flops=3_200_000_000, bytes_accessed=11_534_336, transcendentals=0),
        name="grams_high",
    )(rhs, v1, v0, u3, u2, u1, caps, sent)


def middle_kernel(mine_ref, other_ref, ch_ref, cl_ref, p_ref, gh_ref, gl_ref, g10_ref,
                  t_ref, keep_ref, send_ref):
    _, bit = position()
    first = bit[0] == 0
    p, g = [], []
    for m in range(4):
        mine, other = mine_ref[X_PLACES[m]], other_ref[X_PLACES[m]]
        p.append(jnp.where(first, mine, other))
        g.append(jnp.where(first, other, mine))
    t = []
    for pair in (0, 2):
        joined = jnp.concatenate([p[pair][:RHS], p[pair + 1][:RHS]], axis=1)
        both = product_of(joined, ch_ref[pair // 2], cl_ref[pair // 2])
        t += [both[:, :RANK], both[:, RANK:]]
    q2 = [p[m][RHS:] - product(t[m], g[m]) for m in range(4)]
    joined = jnp.concatenate([q2[0] + q2[1], q2[2] + q2[3]], axis=1)
    coeff = jnp.concatenate([t[0], product_of(joined, ch_ref[2, :, :RANK], cl_ref[2, :, :RANK])], axis=1)
    t_ref[...] = coeff
    q = p_ref[...] - product_of(coeff, gh_ref[...], gl_ref[...])
    half = RHS // 2

    def put(ref, c):
        rows = slice(c * half, (c + 1) * half)
        ref[:half] = q[rows, :RANK]
        ref[half : 2 * half] = q[rows, RANK:]
        ref[2 * half :] = g10_ref[c * RHS : (c + 1) * RHS]

    low_half = half_of(bit) == 0

    @pl.when(low_half)
    def _():
        put(keep_ref, 0)
        put(send_ref, 1)

    @pl.when(jnp.logical_not(low_half))
    def _():
        put(keep_ref, 1)
        put(send_ref, 0)


def middle_step(mine, other, ch, cl, p, gh, gl, g10):
    half = jax.ShapeDtypeStruct((RANK, RANK), F32)
    return pl.pallas_call(
        middle_kernel,
        out_shape=(jax.ShapeDtypeStruct((RHS, 2 * RANK), F32), half, half),
        in_specs=[VMEM] * 8,
        out_specs=(VMEM,) * 3,
        compiler_params=params(LIMITS[3]),
        cost_estimate=pl.CostEstimate(flops=120_000_000, bytes_accessed=1_500_000, transcendentals=0),
        name="coefficients_low",
    )(mine, other, ch, cl, p, gh, gl, g10)


def low_update_kernel(t_ref, rhs_ref, u3_ref, u2_ref, sent_ref, cur_ref, sent_out):
    sent_out[...] = sent_ref[...]
    th, tl = split(t_ref[...])
    left = jnp.concatenate([th, tl], axis=0)
    for cols in spans((2,) * 4, rhs_ref.shape[1]):
        gh, gl = split(jnp.concatenate([u3_ref[:, cols], u2_ref[:, cols]], axis=0))
        both = jnp.dot(left, gh, preferred_element_type=F32)
        update = both[:RHS] + both[RHS:] + jnp.dot(th, gl, preferred_element_type=F32)
        cur_ref[:, cols] = rhs_ref[:, cols] - update


def low_update(t, rhs, u3, u2, sent):
    return pl.pallas_call(
        low_update_kernel,
        out_shape=(array(*rhs.shape), array(*sent.shape)),
        in_specs=[VMEM] * 5,
        out_specs=(VMEM, VMEM),
        compiler_params=params(LIMITS[4]),
        cost_estimate=pl.CostEstimate(flops=402_653_184, bytes_accessed=6_291_456, transcendentals=0),
        name="update_low",
    )(t, rhs, u3, u2, sent)


def pairs_kernel(u1_ref, gen_ref, caps_ref, sent_ref, sent_out, high_ref, low_ref, ch_ref, cl_ref, u0_ref, sem):
    copy = pltpu.make_async_copy(gen_ref.at[0], u0_ref, sem)
    copy.start()
    sent_out[...] = sent_ref[...]
    _, bit = position()
    ordered(caps_ref, 3, bit[5], bit[6], ch_ref, cl_ref)
    high_ref[:RANK], low_ref[:RANK] = split(u1_ref[...])
    copy.wait()
    high_ref[RANK:], low_ref[RANK:] = split(u0_ref[...])


def pairs_step(u1, gen, caps, sent):
    pair, nodes = half_array(2 * RANK, u1.shape[1]), half_array(3, 2 * RANK, 2 * RANK)
    return pl.pallas_call(
        pairs_kernel,
        out_shape=(array(*sent.shape), pair, pair, nodes, nodes),
        in_specs=[VMEM, HBM, VMEM, VMEM],
        out_specs=(VMEM,) * 5,
        scratch_shapes=[pltpu.VMEM(u1.shape, F32), pltpu.SemaphoreType.DMA(())],
        compiler_params=params(LIMITS[5]),
        cost_estimate=pl.CostEstimate(flops=100_000_000, bytes_accessed=8_388_608, transcendentals=0),
        name="pairs_high",
    )(u1, gen, caps, sent)


def last_kernel(mine_ref, other_ref, ch_ref, cl_ref, cur_ref, high_ref, low_ref, out_ref,
                buf, sems):
    first = half_of(position()[1]) == 0
    half = RHS // 2
    q1, q0, g = [], [], []
    for m in range(4):
        mine, other = mine_ref[Y_PLACES[m]], other_ref[Y_PLACES[m]]
        low = jnp.where(first, mine, other)
        high = jnp.where(first, other, mine)
        q1.append(jnp.concatenate([low[:half], high[:half]], axis=0))
        q0.append(jnp.concatenate([low[half:RHS], high[half:RHS]], axis=0))
        g.append(jnp.concatenate([low[RHS:], high[RHS:]], axis=0))
    t = []
    for pair in (0, 2):
        joined = jnp.concatenate([q1[pair], q1[pair + 1]], axis=1)
        both = product_of(joined, ch_ref[pair // 2], cl_ref[pair // 2])
        t += [both[:, :RANK], both[:, RANK:]]
    r = [q0[m] - product(t[m], g[m]) for m in range(4)]
    joined = jnp.concatenate([r[0] + r[1], r[2] + r[3]], axis=1)
    th, tl = split(jnp.concatenate([t[0], product_of(joined, ch_ref[2, :, :RANK], cl_ref[2, :, :RANK])], axis=1))
    left = jnp.concatenate([th, tl], axis=0)
    copies = []
    for i, cols in enumerate(spans((2,) * 4, cur_ref.shape[1])):
        both = jnp.dot(left, high_ref[:, cols], preferred_element_type=F32)
        update = both[:RHS] + both[RHS:] + jnp.dot(th, low_ref[:, cols], preferred_element_type=F32)
        buf[:, cols] = cur_ref[:, cols] - update
        copy = pltpu.make_async_copy(buf.at[:, cols], out_ref.at[:, cols], sems.at[i])
        copy.start()
        copies.append(copy)
    for copy in copies:
        copy.wait()


def last_step(mine, other, ch, cl, cur, high, low):
    return pl.pallas_call(
        last_kernel,
        out_shape=array(*cur.shape),
        in_specs=[VMEM] * 7,
        out_specs=HBM,
        scratch_shapes=[pltpu.VMEM(cur.shape, F32), pltpu.SemaphoreType.DMA((4,))],
        compiler_params=params(LIMITS[6]),
        cost_estimate=pl.CostEstimate(flops=500_000_000, bytes_accessed=7_000_000, transcendentals=0),
        name="update_high",
    )(mine, other, ch, cl, cur, high, low)


def swap(value, mask):
    return lax.ppermute(value, "leaf", [(i, i ^ mask) for i in range(DEVICES)])


def parity(index):
    return bin(index).count("1") & 1


def crossed(value, even, odd):
    def partner(i):
        mask = odd if parity(i & 31) else even
        return i ^ mask ^ parity(mask)

    return lax.ppermute(value, "leaf", [(i, partner(i)) for i in range(DEVICES)])


def neighbours(value, masks):
    three, two, one = (swap(value, m) for m in masks)
    return one, two, three


def crossed_neighbours(value, even, odd):
    three, two, one = (crossed(value, e, o) for e, o in zip(even, odd))
    return one, two, three


def body(rhs, basis, gen, cap):
    keep, send = first_step(rhs, basis, gen)
    chip = keep + swap(send, CORE)
    b, c, d = neighbours(chip, Z_MASKS)
    chip, v1, v0, u3, u2, u1, caps = load_step(basis, gen, cap, chip)
    line = chip + b + c + d
    b, c, d = neighbours(line, X_MASKS)
    line, p, gh, gl, g10, ch, cl = grams_step(rhs, v1, v0, u3, u2, u1, caps, line)
    lines = jnp.stack([b, c, d, line])
    other = swap(lines, CORE)
    t, keep, send = middle_step(lines, other, ch, cl, p, gh, gl, g10)
    chip = keep + swap(send, CORE)
    b, c, d = crossed_neighbours(chip, X_MASKS, Z_MASKS)
    current, chip = low_update(t, rhs, u3, u2, chip)
    part = chip + b + c + d
    b, c, d = crossed_neighbours(part, Z_MASKS, X_MASKS)
    part, high, low, ch, cl = pairs_step(u1, gen, caps, part)
    plane = part + b + c + d
    b, c, d = neighbours(plane, Y_MASKS)
    planes = jnp.stack([b, c, d, plane])
    other = swap(planes, CORE)
    return last_step(planes, other, ch, cl, current, high, low)


def solution(mesh):
    in_specs = (P(None, "leaf"), P(None, None, "leaf"), P(None, None, "leaf"), P())
    return jax.shard_map(body, mesh=mesh, in_specs=in_specs, out_specs=P(None, "leaf"), check_vma=False)
```

```python
import functools

import jax
import jax.numpy as jnp
from jax import lax
from jax.experimental import pallas as pl
from jax.experimental.pallas import tpu as pltpu
from jax.sharding import PartitionSpec as P

F32 = jnp.float32
BF16 = jnp.bfloat16
RANK = 128
RHS = 64
DEVICES = 128
LIMITS = (53, 40, 38, 38, 40, 40, 44, 51)
HBM = pl.BlockSpec(memory_space=pltpu.HBM)
VMEM = pl.BlockSpec(memory_space=pltpu.VMEM)

CORE = 1
Z_MASKS = (6, 4, 2)
X_MASKS = (24, 16, 8)
Y_MASKS = (96, 64, 32)
X_PLACES = (3, 0, 1, 2)
Y_PLACES = (3, 0, 2, 1)


def position():
    device = lax.axis_index("leaf").astype(jnp.int32)
    return device, [device >> k & 1 for k in range(7)]


def half_of(bit):
    return bit[0] ^ bit[1] ^ bit[2] ^ bit[3] ^ bit[4] ^ bit[5] ^ bit[6]


def split(value):
    high = value.astype(BF16)
    return high, (value - high.astype(F32)).astype(BF16)


def stacked(values):
    parts = [split(v) for v in values]
    return jnp.concatenate([h for h, _ in parts] + [l for _, l in parts], axis=0)


def product(left, right):
    lh, ll = split(left)
    rh, rl = split(right)
    rows = left.shape[0]
    both = jnp.dot(jnp.concatenate([lh, ll], axis=0), rh, preferred_element_type=F32)
    return both[:rows] + both[rows:] + jnp.dot(lh, rl, preferred_element_type=F32)


def product_of(left, high, low):
    lh, ll = split(left)
    rows = left.shape[0]
    both = jnp.dot(jnp.concatenate([lh, ll], axis=0), high, preferred_element_type=F32)
    return both[:rows] + both[rows:] + jnp.dot(lh, low, preferred_element_type=F32)


def contract(left, right):
    return lax.dot_general(left, right, (((1,), (1,)), ((), ())), preferred_element_type=F32)


def fold(total, rows):
    half = total.shape[1] // 2
    wide = total[:rows] + total[rows:]
    return wide[:, :half] + wide[:, half:]


def params(limit):
    return pltpu.CompilerParams(vmem_limit_bytes=limit << 20)


def spans(sizes, points):
    at = 0
    for size in sizes:
        yield pl.ds(at * points // 8, size * points // 8)
        at += size


def fetch(sources, sems, sizes, points):
    parts = []
    for i, cols in enumerate(spans(sizes, points)):
        row = []
        for j, (ref, level, buffer) in enumerate(sources):
            src = ref.at[:, cols] if level is None else ref.at[level, :, cols]
            row.append(pltpu.make_async_copy(src, buffer.at[:, cols], sems.at[i, j]))
        parts.append((cols, row))
    for _, row in parts:
        for copy in row:
            copy.start()
    return parts


def add_to(acc, value, first):
    if first:
        acc[...] = value
    else:
        acc[...] += value


PARTS = (2, 2, 2, 2)


def first_kernel(points, rhs_ref, basis_ref, gen_ref, keep_ref, send_ref,
                 rhs_buf, v3_buf, v2_buf, u3_buf, acc2, acc3, sems):
    sources = ((rhs_ref, None, rhs_buf), (basis_ref, 3, v3_buf), (basis_ref, 2, v2_buf), (gen_ref, 3, u3_buf))
    for i, (cols, row) in enumerate(fetch(sources, sems, PARTS, points)):
        for copy in row:
            copy.wait()
        rhs = stacked([rhs_buf[:, cols]])
        left = jnp.concatenate([rhs, stacked([u3_buf[:, cols]])], axis=0)
        add_to(acc2, contract(left, stacked([v2_buf[:, cols]])), i == 0)
        add_to(acc3, contract(rhs, stacked([v3_buf[:, cols]])), i == 0)
    p3 = fold(acc3[...], RHS)
    p2 = fold(acc2[: 2 * RHS], RHS)
    g32 = fold(acc2[2 * RHS :], RANK)
    first = half_of(position()[1]) == 0

    @pl.when(first)
    def _():
        keep_ref[:RHS] = p3
        keep_ref[RHS:] = p2
        send_ref[...] = g32

    @pl.when(jnp.logical_not(first))
    def _():
        send_ref[:RHS] = p3
        send_ref[RHS:] = p2
        keep_ref[...] = g32


def array(*shape):
    return jax.ShapeDtypeStruct(shape, F32)


def half_array(*shape):
    return jax.ShapeDtypeStruct(shape, BF16)


def first_step(rhs, basis, gen):
    points = rhs.shape[1]
    wide = pltpu.VMEM((RANK, points), F32)
    return pl.pallas_call(
        functools.partial(first_kernel, points),
        out_shape=(array(RANK, RANK), array(RANK, RANK)),
        in_specs=[HBM, HBM, HBM],
        out_specs=(VMEM,) * 2,
        scratch_shapes=[
            pltpu.VMEM((RHS, points), F32), wide, wide, wide,
            pltpu.VMEM((2 * (RHS + RANK), 2 * RANK), F32),
            pltpu.VMEM((2 * RHS, 2 * RANK), F32),
            pltpu.SemaphoreType.DMA((len(PARTS), 4)),
        ],
        compiler_params=params(LIMITS[0]),
        cost_estimate=pl.CostEstimate(flops=800_000_000, bytes_accessed=7_340_032, transcendentals=0),
        name="project_low",
    )(rhs, basis, gen)


def nodes_kernel(cap_ref, sent_ref, sent_out, caps_ref, sems):
    device, _ = position()
    n3, n2, n1 = device >> 4, device >> 5, device >> 6
    nodes = (7 + n3, 7 + (n3 ^ 1), 3 + n2, 1 + n1, 1 + (n1 ^ 1), 0)
    copies = [pltpu.make_async_copy(cap_ref.at[n], caps_ref.at[i], sems.at[i]) for i, n in enumerate(nodes)]
    for copy in copies:
        copy.start()
    sent_out[...] = sent_ref[...]
    for copy in copies:
        copy.wait()


def nodes_step(cap, sent):
    return pl.pallas_call(
        nodes_kernel,
        out_shape=(array(*sent.shape), array(6, 2 * RANK, 2 * RANK)),
        in_specs=[HBM, VMEM],
        out_specs=(VMEM, VMEM),
        scratch_shapes=[pltpu.SemaphoreType.DMA((6,))],
        compiler_params=params(LIMITS[7]),
        cost_estimate=pl.CostEstimate(flops=1_000, bytes_accessed=1_572_864, transcendentals=0),
        name="nodes",
    )(cap, sent)


def load_kernel(basis_ref, gen_ref, sent_ref, sent_out, v1_ref, v0_ref, u3_ref, u2_ref, u1_ref, sems):
    sources = [
        (basis_ref, 1, v1_ref), (basis_ref, 0, v0_ref),
        (gen_ref, 3, u3_ref), (gen_ref, 2, u2_ref), (gen_ref, 1, u1_ref),
    ]
    copies = [pltpu.make_async_copy(ref.at[k], out, sems.at[i]) for i, (ref, k, out) in enumerate(sources)]
    for copy in copies:
        copy.start()
    sent_out[...] = sent_ref[...]
    for copy in copies:
        copy.wait()


def load_step(basis, gen, sent):
    wide = array(*basis.shape[1:])
    return pl.pallas_call(
        load_kernel,
        out_shape=(array(*sent.shape), wide, wide, wide, wide, wide),
        in_specs=[HBM, HBM, VMEM],
        out_specs=(VMEM,) * 6,
        scratch_shapes=[pltpu.SemaphoreType.DMA((5,))],
        compiler_params=params(LIMITS[1]),
        cost_estimate=pl.CostEstimate(flops=1_000, bytes_accessed=10_485_760, transcendentals=0),
        name="load_high",
    )(basis, gen, sent)


G_AT = RHS // 2
G10_AT = G_AT + 2 * RANK
SUM_ROWS = G10_AT + RANK // 4


def ordered(caps_ref, base, s_high, s_low, high_ref, low_ref):
    for i, (s, columns) in enumerate(((s_high, 2), (s_high, 2), (s_low, 1))):
        for r, row in enumerate((1 - s, s)):
            for c, col in enumerate((s, 1 - s)[:columns]):
                high, low = split(
                    caps_ref[
                        base + i,
                        pl.ds(pl.multiple_of(row * RANK, RANK), RANK),
                        pl.ds(pl.multiple_of(col * RANK, RANK), RANK),
                    ]
                )
                high_ref[i, r * RANK : (r + 1) * RANK, c * RANK : (c + 1) * RANK] = high
                low_ref[i, r * RANK : (r + 1) * RANK, c * RANK : (c + 1) * RANK] = low


def grams_kernel(rhs_ref, v1_ref, v0_ref, u3_ref, u2_ref, u1_ref, caps_ref, sent_ref, sent_out,
                 keep_ref, send_ref, ch_ref, cl_ref):
    sent_out[...] = sent_ref[...]
    _, bit = position()
    low_half = half_of(bit) == 0
    ordered(caps_ref, 0, bit[3], bit[4], ch_ref, cl_ref)
    left = stacked([rhs_ref[...], u3_ref[...]])
    u2 = stacked([u2_ref[...]])
    for k, ref in enumerate((v1_ref, v0_ref)):
        right = stacked([ref[...]])
        cols = slice(k * RANK, (k + 1) * RANK)
        both = fold(contract(left, right), RHS + RANK)
        g2 = fold(contract(u2, right), RANK)
        one, two = both[: RHS // 2], both[RHS // 2 : RHS]
        keep_ref[: RHS // 2, cols] = jnp.where(low_half, one, two)
        send_ref[: RHS // 2, cols] = jnp.where(low_half, two, one)
        for ref in (keep_ref, send_ref):
            ref[G_AT : G_AT + RANK, cols] = both[RHS:]
            ref[G_AT + RANK : G10_AT, cols] = g2
    g10 = fold(contract(stacked([u1_ref[...]]), right), RANK)
    quarter = RANK // 4
    parts = [jnp.concatenate([g10[i * quarter : (i + 1) * quarter] for i in pair], axis=1) for pair in ((0, 1), (2, 3))]
    keep_ref[G10_AT:] = jnp.where(low_half, parts[0], parts[1])
    send_ref[G10_AT:] = jnp.where(low_half, parts[1], parts[0])


def grams_step(rhs, v1, v0, u3, u2, u1, caps, sent):
    return pl.pallas_call(
        grams_kernel,
        out_shape=(
            array(*sent.shape), array(SUM_ROWS, 2 * RANK), array(SUM_ROWS, 2 * RANK),
            half_array(3, 2 * RANK, 2 * RANK), half_array(3, 2 * RANK, 2 * RANK),
        ),
        in_specs=[VMEM] * 8,
        out_specs=(VMEM,) * 5,
        compiler_params=params(LIMITS[2]),
        cost_estimate=pl.CostEstimate(flops=3_200_000_000, bytes_accessed=11_534_336, transcendentals=0),
        name="grams_high",
    )(rhs, v1, v0, u3, u2, u1, caps, sent)


def middle_kernel(mine_ref, other_ref, ch_ref, cl_ref, keep_ref, come_ref, t_ref, part_ref):
    _, bit = position()
    first = half_of(bit) == 0
    p, g = [], []
    for m in range(4):
        mine, other = mine_ref[X_PLACES[m]], other_ref[X_PLACES[m]]
        p.append(jnp.where(first, mine, other))
        g.append(jnp.where(first, other, mine))
    t = []
    for pair in (0, 2):
        joined = jnp.concatenate([p[pair][:RHS], p[pair + 1][:RHS]], axis=1)
        both = product_of(joined, ch_ref[pair // 2], cl_ref[pair // 2])
        t += [both[:, :RANK], both[:, RANK:]]
    q2 = [p[m][RHS:] - product(t[m], g[m]) for m in range(4)]
    joined = jnp.concatenate([q2[0] + q2[1], q2[2] + q2[3]], axis=1)
    coeff = jnp.concatenate([t[0], product_of(joined, ch_ref[2, :, :RANK], cl_ref[2, :, :RANK])], axis=1)
    t_ref[...] = coeff
    sums = keep_ref[...] + come_ref[...]
    half = RHS // 2
    rows = jnp.where(half_of(bit) == 0, coeff[:half], coeff[half:])
    q = sums[:half] - product(rows, sums[G_AT:G10_AT])
    part_ref[:half] = q[:, :RANK]
    part_ref[half : 2 * half] = q[:, RANK:]
    quarter = RANK // 4
    part_ref[2 * half : 2 * half + quarter] = sums[G10_AT:, :RANK]
    part_ref[2 * half + quarter :] = sums[G10_AT:, RANK:]


def middle_step(mine, other, ch, cl, keep, come):
    return pl.pallas_call(
        middle_kernel,
        out_shape=(array(RHS, 2 * RANK), array(RANK, RANK)),
        in_specs=[VMEM] * 6,
        out_specs=(VMEM,) * 2,
        compiler_params=params(LIMITS[3]),
        cost_estimate=pl.CostEstimate(flops=120_000_000, bytes_accessed=1_500_000, transcendentals=0),
        name="coefficients_low",
    )(mine, other, ch, cl, keep, come)


def low_update_kernel(t_ref, rhs_ref, u3_ref, u2_ref, sent_ref, cur_ref, sent_out):
    sent_out[...] = sent_ref[...]
    th, tl = split(t_ref[...])
    left = jnp.concatenate([th, tl], axis=0)
    for cols in spans((2,) * 4, rhs_ref.shape[1]):
        gh, gl = split(jnp.concatenate([u3_ref[:, cols], u2_ref[:, cols]], axis=0))
        both = jnp.dot(left, gh, preferred_element_type=F32)
        update = both[:RHS] + both[RHS:] + jnp.dot(th, gl, preferred_element_type=F32)
        cur_ref[:, cols] = rhs_ref[:, cols] - update


def low_update(t, rhs, u3, u2, sent):
    return pl.pallas_call(
        low_update_kernel,
        out_shape=(array(*rhs.shape), array(*sent.shape)),
        in_specs=[VMEM] * 5,
        out_specs=(VMEM, VMEM),
        compiler_params=params(LIMITS[4]),
        cost_estimate=pl.CostEstimate(flops=402_653_184, bytes_accessed=6_291_456, transcendentals=0),
        name="update_low",
    )(t, rhs, u3, u2, sent)


def pairs_kernel(u1_ref, gen_ref, caps_ref, sent_ref, sent_out, high_ref, low_ref, ch_ref, cl_ref, u0_ref, sem):
    copy = pltpu.make_async_copy(gen_ref.at[0], u0_ref, sem)
    copy.start()
    sent_out[...] = sent_ref[...]
    _, bit = position()
    ordered(caps_ref, 3, bit[5], bit[6], ch_ref, cl_ref)
    high_ref[:RANK], low_ref[:RANK] = split(u1_ref[...])
    copy.wait()
    high_ref[RANK:], low_ref[RANK:] = split(u0_ref[...])


def pairs_step(u1, gen, caps, sent):
    pair, nodes = half_array(2 * RANK, u1.shape[1]), half_array(3, 2 * RANK, 2 * RANK)
    return pl.pallas_call(
        pairs_kernel,
        out_shape=(array(*sent.shape), pair, pair, nodes, nodes),
        in_specs=[VMEM, HBM, VMEM, VMEM],
        out_specs=(VMEM,) * 5,
        scratch_shapes=[pltpu.VMEM(u1.shape, F32), pltpu.SemaphoreType.DMA(())],
        compiler_params=params(LIMITS[5]),
        cost_estimate=pl.CostEstimate(flops=100_000_000, bytes_accessed=8_388_608, transcendentals=0),
        name="pairs_high",
    )(u1, gen, caps, sent)


def last_kernel(mine_ref, other_ref, ch_ref, cl_ref, cur_ref, high_ref, low_ref, out_ref,
                buf, sems):
    first = half_of(position()[1]) == 0
    half = RHS // 2
    q1, q0, g = [], [], []
    for m in range(4):
        mine, other = mine_ref[Y_PLACES[m]], other_ref[Y_PLACES[m]]
        low = jnp.where(first, mine, other)
        high = jnp.where(first, other, mine)
        q1.append(jnp.concatenate([low[:half], high[:half]], axis=0))
        q0.append(jnp.concatenate([low[half:RHS], high[half:RHS]], axis=0))
        g.append(jnp.concatenate([low[RHS:], high[RHS:]], axis=0))
    t = []
    for pair in (0, 2):
        joined = jnp.concatenate([q1[pair], q1[pair + 1]], axis=1)
        both = product_of(joined, ch_ref[pair // 2], cl_ref[pair // 2])
        t += [both[:, :RANK], both[:, RANK:]]
    r = [q0[m] - product(t[m], g[m]) for m in range(4)]
    joined = jnp.concatenate([r[0] + r[1], r[2] + r[3]], axis=1)
    th, tl = split(jnp.concatenate([t[0], product_of(joined, ch_ref[2, :, :RANK], cl_ref[2, :, :RANK])], axis=1))
    left = jnp.concatenate([th, tl], axis=0)
    copies = []
    for i, cols in enumerate(spans((2,) * 4, cur_ref.shape[1])):
        both = jnp.dot(left, high_ref[:, cols], preferred_element_type=F32)
        update = both[:RHS] + both[RHS:] + jnp.dot(th, low_ref[:, cols], preferred_element_type=F32)
        buf[:, cols] = cur_ref[:, cols] - update
        copy = pltpu.make_async_copy(buf.at[:, cols], out_ref.at[:, cols], sems.at[i])
        copy.start()
        copies.append(copy)
    for copy in copies:
        copy.wait()


def last_step(mine, other, ch, cl, cur, high, low):
    return pl.pallas_call(
        last_kernel,
        out_shape=array(*cur.shape),
        in_specs=[VMEM] * 7,
        out_specs=HBM,
        scratch_shapes=[pltpu.VMEM(cur.shape, F32), pltpu.SemaphoreType.DMA((4,))],
        compiler_params=params(LIMITS[6]),
        cost_estimate=pl.CostEstimate(flops=500_000_000, bytes_accessed=7_000_000, transcendentals=0),
        name="update_high",
    )(mine, other, ch, cl, cur, high, low)


def swap(value, mask):
    return lax.ppermute(value, "leaf", [(i, i ^ mask) for i in range(DEVICES)])


def parity(index):
    return bin(index).count("1") & 1


def crossed(value, even, odd):
    def partner(i):
        mask = odd if parity(i) else even
        return i ^ mask ^ parity(mask)

    return lax.ppermute(value, "leaf", [(i, partner(i)) for i in range(DEVICES)])


def neighbours(value, masks):
    three, two, one = (swap(value, m) for m in masks)
    return one, two, three


def crossed_neighbours(value, even, odd):
    three, two, one = (crossed(value, e, o) for e, o in zip(even, odd))
    return one, two, three


def body(rhs, basis, gen, cap):
    keep, send = first_step(rhs, basis, gen)
    other = swap(send, CORE)
    keep, caps = nodes_step(cap, keep)
    chip = keep + other
    b, c, d = crossed_neighbours(chip, Z_MASKS, Z_MASKS)
    chip, v1, v0, u3, u2, u1 = load_step(basis, gen, chip)
    line = chip + b + c + d
    b, c, d = crossed_neighbours(line, X_MASKS, X_MASKS)
    line, keep, send, ch, cl = grams_step(rhs, v1, v0, u3, u2, u1, caps, line)
    come = swap(send, CORE)
    lines = jnp.stack([b, c, d, line])
    other = swap(lines, CORE)
    t, chip = middle_step(lines, other, ch, cl, keep, come)
    b, c, d = crossed_neighbours(chip, X_MASKS, Z_MASKS)
    current, chip = low_update(t, rhs, u3, u2, chip)
    part = chip + b + c + d
    b, c, d = crossed_neighbours(part, Z_MASKS, X_MASKS)
    part, high, low, ch, cl = pairs_step(u1, gen, caps, part)
    plane = part + b + c + d
    b, c, d = crossed_neighbours(plane, Y_MASKS, Y_MASKS)
    planes = jnp.stack([b, d, c, plane])
    other = swap(planes, CORE)
    return last_step(planes, other, ch, cl, current, high, low)


def solution(mesh):
    in_specs = (P(None, "leaf"), P(None, None, "leaf"), P(None, None, "leaf"), P())
    return jax.shard_map(body, mesh=mesh, in_specs=in_specs, out_specs=P(None, "leaf"), check_vma=False)
```

```python
import functools

import jax
import jax.numpy as jnp
from jax import lax
from jax.experimental import pallas as pl
from jax.experimental.pallas import tpu as pltpu
from jax.sharding import PartitionSpec as P

F32 = jnp.float32
BF16 = jnp.bfloat16
RANK = 128
RHS = 64
DEVICES = 128
LIMITS = (53, 40, 38, 38, 40, 47, 44, 51, 47)
HBM = pl.BlockSpec(memory_space=pltpu.HBM)
VMEM = pl.BlockSpec(memory_space=pltpu.VMEM)

CORE = 1
Z_MASKS = (6, 4, 2)
X_MASKS = (24, 16, 8)
Y_MASKS = (96, 64, 32)
X_PLACES = (3, 0, 1, 2)
Y_PLACES = (3, 0, 2, 1)


def position():
    device = lax.axis_index("leaf").astype(jnp.int32)
    return device, [device >> k & 1 for k in range(7)]


def half_of(bit):
    return bit[0] ^ bit[1] ^ bit[2] ^ bit[3] ^ bit[4] ^ bit[5] ^ bit[6]


def split(value):
    high = value.astype(BF16)
    return high, (value - high.astype(F32)).astype(BF16)


def stacked(values):
    parts = [split(v) for v in values]
    return jnp.concatenate([h for h, _ in parts] + [l for _, l in parts], axis=0)


def product(left, right):
    lh, ll = split(left)
    rh, rl = split(right)
    rows = left.shape[0]
    both = jnp.dot(jnp.concatenate([lh, ll], axis=0), rh, preferred_element_type=F32)
    return both[:rows] + both[rows:] + jnp.dot(lh, rl, preferred_element_type=F32)


def product_of(left, high, low):
    lh, ll = split(left)
    rows = left.shape[0]
    both = jnp.dot(jnp.concatenate([lh, ll], axis=0), high, preferred_element_type=F32)
    return both[:rows] + both[rows:] + jnp.dot(lh, low, preferred_element_type=F32)


def contract(left, right):
    return lax.dot_general(left, right, (((1,), (1,)), ((), ())), preferred_element_type=F32)


def fold(total, rows):
    half = total.shape[1] // 2
    wide = total[:rows] + total[rows:]
    return wide[:, :half] + wide[:, half:]


def params(limit):
    return pltpu.CompilerParams(vmem_limit_bytes=limit << 20)


def spans(sizes, points):
    at = 0
    for size in sizes:
        yield pl.ds(at * points // 8, size * points // 8)
        at += size


def fetch(sources, sems, sizes, points):
    parts = []
    for i, cols in enumerate(spans(sizes, points)):
        row = []
        for j, (ref, level, buffer) in enumerate(sources):
            src = ref.at[:, cols] if level is None else ref.at[level, :, cols]
            row.append(pltpu.make_async_copy(src, buffer.at[:, cols], sems.at[i, j]))
        parts.append((cols, row))
    for _, row in parts:
        for copy in row:
            copy.start()
    return parts


def add_to(acc, value, first):
    if first:
        acc[...] = value
    else:
        acc[...] += value


PARTS = (2, 2, 2, 2)


def first_kernel(points, rhs_ref, basis_ref, gen_ref, keep_ref, send_ref,
                 rhs_buf, v3_buf, v2_buf, u3_buf, acc2, acc3, sems):
    sources = ((rhs_ref, None, rhs_buf), (basis_ref, 3, v3_buf), (basis_ref, 2, v2_buf), (gen_ref, 3, u3_buf))
    for i, (cols, row) in enumerate(fetch(sources, sems, PARTS, points)):
        for copy in row:
            copy.wait()
        rhs = stacked([rhs_buf[:, cols]])
        left = jnp.concatenate([rhs, stacked([u3_buf[:, cols]])], axis=0)
        add_to(acc2, contract(left, stacked([v2_buf[:, cols]])), i == 0)
        add_to(acc3, contract(rhs, stacked([v3_buf[:, cols]])), i == 0)
    p3 = fold(acc3[...], RHS)
    p2 = fold(acc2[: 2 * RHS], RHS)
    g32 = fold(acc2[2 * RHS :], RANK)
    first = half_of(position()[1]) == 0

    @pl.when(first)
    def _():
        keep_ref[:RHS] = p3
        keep_ref[RHS:] = p2
        send_ref[...] = g32

    @pl.when(jnp.logical_not(first))
    def _():
        send_ref[:RHS] = p3
        send_ref[RHS:] = p2
        keep_ref[...] = g32


def array(*shape):
    return jax.ShapeDtypeStruct(shape, F32)


def half_array(*shape):
    return jax.ShapeDtypeStruct(shape, BF16)


def first_step(rhs, basis, gen):
    points = rhs.shape[1]
    wide = pltpu.VMEM((RANK, points), F32)
    return pl.pallas_call(
        functools.partial(first_kernel, points),
        out_shape=(array(RANK, RANK), array(RANK, RANK)),
        in_specs=[HBM, HBM, HBM],
        out_specs=(VMEM,) * 2,
        scratch_shapes=[
            pltpu.VMEM((RHS, points), F32), wide, wide, wide,
            pltpu.VMEM((2 * (RHS + RANK), 2 * RANK), F32),
            pltpu.VMEM((2 * RHS, 2 * RANK), F32),
            pltpu.SemaphoreType.DMA((len(PARTS), 4)),
        ],
        compiler_params=params(LIMITS[0]),
        cost_estimate=pl.CostEstimate(flops=800_000_000, bytes_accessed=7_340_032, transcendentals=0),
        name="project_low",
    )(rhs, basis, gen)


def early_kernel(gen_ref, sent_ref, sent_out, u1_ref, sem):
    copy = pltpu.make_async_copy(gen_ref.at[1], u1_ref, sem)
    copy.start()
    sent_out[...] = sent_ref[...]
    copy.wait()


def early_step(gen, sent):
    return pl.pallas_call(
        early_kernel,
        out_shape=(array(*sent.shape), array(*gen.shape[1:])),
        in_specs=[HBM, VMEM],
        out_specs=(VMEM, VMEM),
        scratch_shapes=[pltpu.SemaphoreType.DMA(())],
        compiler_params=params(LIMITS[7]),
        cost_estimate=pl.CostEstimate(flops=1_000, bytes_accessed=2_097_152, transcendentals=0),
        name="load_early",
    )(gen, sent)


def load_kernel(basis_ref, gen_ref, sent_ref, sent_out, v1_ref, v0_ref, u3_ref, u2_ref, sems):
    sources = [
        (basis_ref, 1, v1_ref), (basis_ref, 0, v0_ref),
        (gen_ref, 3, u3_ref), (gen_ref, 2, u2_ref),
    ]
    copies = [pltpu.make_async_copy(ref.at[k], out, sems.at[i]) for i, (ref, k, out) in enumerate(sources)]
    for copy in copies:
        copy.start()
    sent_out[...] = sent_ref[...]
    for copy in copies:
        copy.wait()


def load_step(basis, gen, sent):
    wide = array(*basis.shape[1:])
    return pl.pallas_call(
        load_kernel,
        out_shape=(array(*sent.shape), wide, wide, wide, wide),
        in_specs=[HBM, HBM, VMEM],
        out_specs=(VMEM,) * 5,
        scratch_shapes=[pltpu.SemaphoreType.DMA((4,))],
        compiler_params=params(LIMITS[1]),
        cost_estimate=pl.CostEstimate(flops=1_000, bytes_accessed=8_388_608, transcendentals=0),
        name="load_high",
    )(basis, gen, sent)


G_AT = RHS // 2
G10_AT = G_AT + 2 * RANK
SUM_ROWS = G10_AT + RANK // 4


def ordered(caps_ref, s_high, s_low, high_ref, low_ref):
    for i, (s, columns) in enumerate(((s_high, 2), (s_high, 2), (s_low, 1))):
        for r, row in enumerate((1 - s, s)):
            for c, col in enumerate((s, 1 - s)[:columns]):
                high, low = split(
                    caps_ref[
                        i,
                        pl.ds(pl.multiple_of(row * RANK, RANK), RANK),
                        pl.ds(pl.multiple_of(col * RANK, RANK), RANK),
                    ]
                )
                high_ref[i, r * RANK : (r + 1) * RANK, c * RANK : (c + 1) * RANK] = high
                low_ref[i, r * RANK : (r + 1) * RANK, c * RANK : (c + 1) * RANK] = low


def grams_kernel(rhs_ref, v1_ref, v0_ref, u3_ref, u2_ref, u1_ref, sent_ref, sent_out,
                 keep_ref, send_ref):
    sent_out[...] = sent_ref[...]
    _, bit = position()
    low_half = half_of(bit) == 0
    left = stacked([rhs_ref[...], u3_ref[...]])
    u2 = stacked([u2_ref[...]])
    for k, ref in enumerate((v1_ref, v0_ref)):
        right = stacked([ref[...]])
        cols = slice(k * RANK, (k + 1) * RANK)
        both = fold(contract(left, right), RHS + RANK)
        g2 = fold(contract(u2, right), RANK)
        one, two = both[: RHS // 2], both[RHS // 2 : RHS]
        keep_ref[: RHS // 2, cols] = jnp.where(low_half, one, two)
        send_ref[: RHS // 2, cols] = jnp.where(low_half, two, one)
        for ref in (keep_ref, send_ref):
            ref[G_AT : G_AT + RANK, cols] = both[RHS:]
            ref[G_AT + RANK : G10_AT, cols] = g2
    g10 = fold(contract(stacked([u1_ref[...]]), right), RANK)
    quarter = RANK // 4
    parts = [jnp.concatenate([g10[i * quarter : (i + 1) * quarter] for i in pair], axis=1) for pair in ((0, 1), (2, 3))]
    keep_ref[G10_AT:] = jnp.where(low_half, parts[0], parts[1])
    send_ref[G10_AT:] = jnp.where(low_half, parts[1], parts[0])


def grams_step(rhs, v1, v0, u3, u2, u1, sent):
    return pl.pallas_call(
        grams_kernel,
        out_shape=(
            array(*sent.shape), array(SUM_ROWS, 2 * RANK), array(SUM_ROWS, 2 * RANK),
        ),
        in_specs=[VMEM] * 7,
        out_specs=(VMEM,) * 3,
        compiler_params=params(LIMITS[2]),
        cost_estimate=pl.CostEstimate(flops=3_200_000_000, bytes_accessed=11_534_336, transcendentals=0),
        name="grams_high",
    )(rhs, v1, v0, u3, u2, u1, sent)


def fetch_nodes(cap_ref, nodes, caps_ref, sems):
    copies = [pltpu.make_async_copy(cap_ref.at[n], caps_ref.at[i], sems.at[i]) for i, n in enumerate(nodes)]
    for copy in copies:
        copy.start()
    return copies


def nodes_kernel(cap_ref, sent_ref, sent_out, ch_ref, cl_ref, caps_ref, sems):
    device, bit = position()
    n3, n2 = device >> 4, device >> 5
    copies = fetch_nodes(cap_ref, (7 + n3, 7 + (n3 ^ 1), 3 + n2), caps_ref, sems)
    sent_out[...] = sent_ref[...]
    for copy in copies:
        copy.wait()
    ordered(caps_ref, bit[3], bit[4], ch_ref, cl_ref)


def nodes_step(cap, sent):
    nodes = half_array(3, 2 * RANK, 2 * RANK)
    return pl.pallas_call(
        nodes_kernel,
        out_shape=(array(*sent.shape), nodes, nodes),
        in_specs=[HBM, VMEM],
        out_specs=(VMEM,) * 3,
        scratch_shapes=[pltpu.VMEM((3, 2 * RANK, 2 * RANK), F32), pltpu.SemaphoreType.DMA((3,))],
        compiler_params=params(LIMITS[8]),
        cost_estimate=pl.CostEstimate(flops=1_000, bytes_accessed=786_432, transcendentals=0),
        name="nodes_low",
    )(cap, sent)


def upper(t, g, q, high, low):
    sides = (slice(0, RANK), slice(0, RANK), slice(RANK, 2 * RANK), slice(RANK, 2 * RANK))
    moved = jnp.concatenate([product_of(g[m], high[side], low[side]) for m, side in enumerate(sides)], axis=0)
    joined = jnp.concatenate([q[0] + q[1], q[2] + q[3]], axis=1)
    return product_of(joined, high, low) - product(jnp.concatenate(t, axis=1), moved)


def middle_kernel(mine_ref, other_ref, ch_ref, cl_ref, keep_ref, come_ref, t_ref, part_ref):
    _, bit = position()
    first = half_of(bit) == 0
    p, g = [], []
    for m in range(4):
        mine, other = mine_ref[X_PLACES[m]], other_ref[X_PLACES[m]]
        p.append(jnp.where(first, mine, other))
        g.append(jnp.where(first, other, mine))
    t = []
    for pair in (0, 2):
        joined = jnp.concatenate([p[pair][:RHS], p[pair + 1][:RHS]], axis=1)
        both = product_of(joined, ch_ref[pair // 2], cl_ref[pair // 2])
        t += [both[:, :RANK], both[:, RANK:]]
    above = upper(t, g, [p[m][RHS:] for m in range(4)], ch_ref[2, :, :RANK], cl_ref[2, :, :RANK])
    t_ref[:, :RANK] = t[0]
    t_ref[:, RANK:] = above
    sums = keep_ref[...] + come_ref[...]
    half = RHS // 2
    low_half = half_of(bit) == 0
    grams = sums[G_AT:G10_AT]
    q = sums[:half] - product(jnp.where(low_half, t[0][:half], t[0][half:]), grams[:RANK])
    q = q - product(jnp.where(low_half, above[:half], above[half:]), grams[RANK:])
    part_ref[:half] = q[:, :RANK]
    part_ref[half : 2 * half] = q[:, RANK:]
    quarter = RANK // 4
    part_ref[2 * half : 2 * half + quarter] = sums[G10_AT:, :RANK]
    part_ref[2 * half + quarter :] = sums[G10_AT:, RANK:]


def middle_step(mine, other, ch, cl, keep, come):
    return pl.pallas_call(
        middle_kernel,
        out_shape=(array(RHS, 2 * RANK), array(RANK, RANK)),
        in_specs=[VMEM] * 6,
        out_specs=(VMEM,) * 2,
        compiler_params=params(LIMITS[3]),
        cost_estimate=pl.CostEstimate(flops=120_000_000, bytes_accessed=1_500_000, transcendentals=0),
        name="coefficients_low",
    )(mine, other, ch, cl, keep, come)


def low_update_kernel(t_ref, rhs_ref, u3_ref, u2_ref, sent_ref, cur_ref, sent_out):
    sent_out[...] = sent_ref[...]
    th, tl = split(t_ref[...])
    left = jnp.concatenate([th, tl], axis=0)
    for cols in spans((2,) * 4, rhs_ref.shape[1]):
        gh, gl = split(jnp.concatenate([u3_ref[:, cols], u2_ref[:, cols]], axis=0))
        both = jnp.dot(left, gh, preferred_element_type=F32)
        update = both[:RHS] + both[RHS:] + jnp.dot(th, gl, preferred_element_type=F32)
        cur_ref[:, cols] = rhs_ref[:, cols] - update


def low_update(t, rhs, u3, u2, sent):
    return pl.pallas_call(
        low_update_kernel,
        out_shape=(array(*rhs.shape), array(*sent.shape)),
        in_specs=[VMEM] * 5,
        out_specs=(VMEM, VMEM),
        compiler_params=params(LIMITS[4]),
        cost_estimate=pl.CostEstimate(flops=402_653_184, bytes_accessed=6_291_456, transcendentals=0),
        name="update_low",
    )(t, rhs, u3, u2, sent)


def pairs_kernel(u1_ref, gen_ref, cap_ref, sent_ref, sent_out, high_ref, low_ref, ch_ref, cl_ref,
                 u0_ref, caps_ref, sem, sems):
    copy = pltpu.make_async_copy(gen_ref.at[0], u0_ref, sem)
    copy.start()
    sent_out[...] = sent_ref[...]
    device, bit = position()
    n1 = device >> 6
    copies = fetch_nodes(cap_ref, (1 + n1, 1 + (n1 ^ 1), 0), caps_ref, sems)
    high_ref[:RANK], low_ref[:RANK] = split(u1_ref[...])
    for node in copies:
        node.wait()
    ordered(caps_ref, bit[5], bit[6], ch_ref, cl_ref)
    copy.wait()
    high_ref[RANK:], low_ref[RANK:] = split(u0_ref[...])


def pairs_step(u1, gen, cap, sent):
    pair, nodes = half_array(2 * RANK, u1.shape[1]), half_array(3, 2 * RANK, 2 * RANK)
    return pl.pallas_call(
        pairs_kernel,
        out_shape=(array(*sent.shape), pair, pair, nodes, nodes),
        in_specs=[VMEM, HBM, HBM, VMEM],
        out_specs=(VMEM,) * 5,
        scratch_shapes=[
            pltpu.VMEM(u1.shape, F32), pltpu.VMEM((3, 2 * RANK, 2 * RANK), F32),
            pltpu.SemaphoreType.DMA(()), pltpu.SemaphoreType.DMA((3,)),
        ],
        compiler_params=params(LIMITS[5]),
        cost_estimate=pl.CostEstimate(flops=100_000_000, bytes_accessed=8_388_608, transcendentals=0),
        name="pairs_high",
    )(u1, gen, cap, sent)


def last_kernel(mine_ref, other_ref, ch_ref, cl_ref, cur_ref, high_ref, low_ref, out_ref,
                buf, sems):
    first = half_of(position()[1]) == 0
    half = RHS // 2
    q1, q0, g = [], [], []
    for m in range(4):
        mine, other = mine_ref[Y_PLACES[m]], other_ref[Y_PLACES[m]]
        low = jnp.where(first, mine, other)
        high = jnp.where(first, other, mine)
        q1.append(jnp.concatenate([low[:half], high[:half]], axis=0))
        q0.append(jnp.concatenate([low[half:RHS], high[half:RHS]], axis=0))
        g.append(jnp.concatenate([low[RHS:], high[RHS:]], axis=0))
    t = []
    for pair in (0, 2):
        joined = jnp.concatenate([q1[pair], q1[pair + 1]], axis=1)
        both = product_of(joined, ch_ref[pair // 2], cl_ref[pair // 2])
        t += [both[:, :RANK], both[:, RANK:]]
    above = upper(t, g, q0, ch_ref[2, :, :RANK], cl_ref[2, :, :RANK])
    th, tl = split(jnp.concatenate([t[0], above], axis=1))
    left = jnp.concatenate([th, tl], axis=0)
    copies = []
    for i, cols in enumerate(spans((2,) * 4, cur_ref.shape[1])):
        both = jnp.dot(left, high_ref[:, cols], preferred_element_type=F32)
        update = both[:RHS] + both[RHS:] + jnp.dot(th, low_ref[:, cols], preferred_element_type=F32)
        buf[:, cols] = cur_ref[:, cols] - update
        copy = pltpu.make_async_copy(buf.at[:, cols], out_ref.at[:, cols], sems.at[i])
        copy.start()
        copies.append(copy)
    for copy in copies:
        copy.wait()


def last_step(mine, other, ch, cl, cur, high, low):
    return pl.pallas_call(
        last_kernel,
        out_shape=array(*cur.shape),
        in_specs=[VMEM] * 7,
        out_specs=HBM,
        scratch_shapes=[pltpu.VMEM(cur.shape, F32), pltpu.SemaphoreType.DMA((4,))],
        compiler_params=params(LIMITS[6]),
        cost_estimate=pl.CostEstimate(flops=500_000_000, bytes_accessed=7_000_000, transcendentals=0),
        name="update_high",
    )(mine, other, ch, cl, cur, high, low)


def swap(value, mask):
    return lax.ppermute(value, "leaf", [(i, i ^ mask) for i in range(DEVICES)])


def parity(index):
    return bin(index).count("1") & 1


def crossed(value, even, odd):
    def partner(i):
        mask = odd if parity(i) else even
        return i ^ mask ^ parity(mask)

    return lax.ppermute(value, "leaf", [(i, partner(i)) for i in range(DEVICES)])


def neighbours(value, masks):
    three, two, one = (swap(value, m) for m in masks)
    return one, two, three


def crossed_neighbours(value, even, odd):
    three, two, one = (crossed(value, e, o) for e, o in zip(even, odd))
    return one, two, three


def body(rhs, basis, gen, cap):
    keep, send = first_step(rhs, basis, gen)
    other = swap(send, CORE)
    keep, u1 = early_step(gen, keep)
    chip = keep + other
    b, c, d = crossed_neighbours(chip, Z_MASKS, Z_MASKS)
    chip, v1, v0, u3, u2 = load_step(basis, gen, chip)
    line = chip + b + c + d
    b, c, d = crossed_neighbours(line, X_MASKS, X_MASKS)
    line, keep, send = grams_step(rhs, v1, v0, u3, u2, u1, line)
    come = swap(send, CORE)
    lines = jnp.stack([b, c, d, line])
    other = swap(lines, CORE)
    lines, ch, cl = nodes_step(cap, lines)
    t, chip = middle_step(lines, other, ch, cl, keep, come)
    b, c, d = crossed_neighbours(chip, X_MASKS, Z_MASKS)
    current, chip = low_update(t, rhs, u3, u2, chip)
    part = chip + b + c + d
    b, c, d = crossed_neighbours(part, Z_MASKS, X_MASKS)
    part, high, low, ch, cl = pairs_step(u1, gen, cap, part)
    plane = part + b + c + d
    b, c, d = crossed_neighbours(plane, Y_MASKS, Y_MASKS)
    planes = jnp.stack([b, d, c, plane])
    other = swap(planes, CORE)
    return last_step(planes, other, ch, cl, current, high, low)


def solution(mesh):
    in_specs = (P(None, "leaf"), P(None, None, "leaf"), P(None, None, "leaf"), P())
    return jax.shard_map(body, mesh=mesh, in_specs=in_specs, out_specs=P(None, "leaf"), check_vma=False)
```

```python
import functools

import jax
import jax.numpy as jnp
from jax import lax
from jax.experimental import pallas as pl
from jax.experimental.pallas import tpu as pltpu
from jax.sharding import PartitionSpec as P

F32 = jnp.float32
BF16 = jnp.bfloat16
RANK = 128
RHS = 64
DEVICES = 128
LIMITS = (53, 40, 38, 38, 40, 47, 44, 51, 47)
HBM = pl.BlockSpec(memory_space=pltpu.HBM)
VMEM = pl.BlockSpec(memory_space=pltpu.VMEM)

CORE = 1
Z_MASKS = (6, 4, 2)
X_MASKS = (24, 16, 8)
Y_MASKS = (96, 64, 32)
X_PLACES = (3, 0, 1, 2)
Y_PLACES = (3, 0, 2, 1)


def position():
    device = lax.axis_index("leaf").astype(jnp.int32)
    return device, [device >> k & 1 for k in range(7)]


def half_of(bit):
    return bit[0] ^ bit[1] ^ bit[2] ^ bit[3] ^ bit[4] ^ bit[5] ^ bit[6]


def split(value):
    high = value.astype(BF16)
    return high, (value - high.astype(F32)).astype(BF16)


def stacked(values):
    parts = [split(v) for v in values]
    return jnp.concatenate([h for h, _ in parts] + [l for _, l in parts], axis=0)


def product(left, right):
    lh, ll = split(left)
    rh, rl = split(right)
    rows = left.shape[0]
    both = jnp.dot(jnp.concatenate([lh, ll], axis=0), rh, preferred_element_type=F32)
    return both[:rows] + both[rows:] + jnp.dot(lh, rl, preferred_element_type=F32)


def product_of(left, high, low):
    lh, ll = split(left)
    rows = left.shape[0]
    both = jnp.dot(jnp.concatenate([lh, ll], axis=0), high, preferred_element_type=F32)
    return both[:rows] + both[rows:] + jnp.dot(lh, low, preferred_element_type=F32)


def contract(left, right):
    return lax.dot_general(left, right, (((1,), (1,)), ((), ())), preferred_element_type=F32)


def fold(total, rows):
    half = total.shape[1] // 2
    wide = total[:rows] + total[rows:]
    return wide[:, :half] + wide[:, half:]


def params(limit):
    return pltpu.CompilerParams(vmem_limit_bytes=limit << 20)


def spans(sizes, points):
    at = 0
    for size in sizes:
        yield pl.ds(at * points // 8, size * points // 8)
        at += size


def fetch(sources, sems, sizes, points):
    parts = []
    for i, cols in enumerate(spans(sizes, points)):
        row = []
        for j, (ref, level, buffer) in enumerate(sources):
            src = ref.at[:, cols] if level is None else ref.at[level, :, cols]
            row.append(pltpu.make_async_copy(src, buffer.at[:, cols], sems.at[i, j]))
        parts.append((cols, row))
    for _, row in parts:
        for copy in row:
            copy.start()
    return parts


def add_to(acc, value, first):
    if first:
        acc[...] = value
    else:
        acc[...] += value


PARTS = (2, 2, 2, 2)


def first_kernel(points, rhs_ref, basis_ref, gen_ref, keep_ref, send_ref,
                 rhs_buf, v3_buf, v2_buf, u3_buf, acc2, acc3, sems):
    sources = ((rhs_ref, None, rhs_buf), (basis_ref, 3, v3_buf), (basis_ref, 2, v2_buf), (gen_ref, 3, u3_buf))
    for i, (cols, row) in enumerate(fetch(sources, sems, PARTS, points)):
        for copy in row:
            copy.wait()
        rhs = stacked([rhs_buf[:, cols]])
        left = jnp.concatenate([rhs, stacked([u3_buf[:, cols]])], axis=0)
        add_to(acc2, contract(left, stacked([v2_buf[:, cols]])), i == 0)
        add_to(acc3, contract(rhs, stacked([v3_buf[:, cols]])), i == 0)
    p3 = fold(acc3[...], RHS)
    p2 = fold(acc2[: 2 * RHS], RHS)
    g32 = fold(acc2[2 * RHS :], RANK)
    first = half_of(position()[1]) == 0

    @pl.when(first)
    def _():
        keep_ref[:RHS] = p3
        keep_ref[RHS:] = p2
        send_ref[...] = g32

    @pl.when(jnp.logical_not(first))
    def _():
        send_ref[:RHS] = p3
        send_ref[RHS:] = p2
        keep_ref[...] = g32


def array(*shape):
    return jax.ShapeDtypeStruct(shape, F32)


def half_array(*shape):
    return jax.ShapeDtypeStruct(shape, BF16)


def first_step(rhs, basis, gen):
    points = rhs.shape[1]
    wide = pltpu.VMEM((RANK, points), F32)
    return pl.pallas_call(
        functools.partial(first_kernel, points),
        out_shape=(array(RANK, RANK), array(RANK, RANK)),
        in_specs=[HBM, HBM, HBM],
        out_specs=(VMEM,) * 2,
        scratch_shapes=[
            pltpu.VMEM((RHS, points), F32), wide, wide, wide,
            pltpu.VMEM((2 * (RHS + RANK), 2 * RANK), F32),
            pltpu.VMEM((2 * RHS, 2 * RANK), F32),
            pltpu.SemaphoreType.DMA((len(PARTS), 4)),
        ],
        compiler_params=params(LIMITS[0]),
        cost_estimate=pl.CostEstimate(flops=800_000_000, bytes_accessed=7_340_032, transcendentals=0),
        name="project_low",
    )(rhs, basis, gen)


def early_kernel(gen_ref, sent_ref, sent_out, u1_ref, sem):
    copy = pltpu.make_async_copy(gen_ref.at[1], u1_ref, sem)
    copy.start()
    sent_out[...] = sent_ref[...]
    copy.wait()


def early_step(gen, sent):
    return pl.pallas_call(
        early_kernel,
        out_shape=(array(*sent.shape), array(*gen.shape[1:])),
        in_specs=[HBM, VMEM],
        out_specs=(VMEM, VMEM),
        scratch_shapes=[pltpu.SemaphoreType.DMA(())],
        compiler_params=params(LIMITS[7]),
        cost_estimate=pl.CostEstimate(flops=1_000, bytes_accessed=2_097_152, transcendentals=0),
        name="load_early",
    )(gen, sent)


def load_kernel(basis_ref, gen_ref, sent_ref, sent_out, v1_ref, v0_ref, u3_ref, u2_ref, sems):
    sources = [
        (basis_ref, 1, v1_ref), (basis_ref, 0, v0_ref),
        (gen_ref, 3, u3_ref), (gen_ref, 2, u2_ref),
    ]
    copies = [pltpu.make_async_copy(ref.at[k], out, sems.at[i]) for i, (ref, k, out) in enumerate(sources)]
    for copy in copies:
        copy.start()
    sent_out[...] = sent_ref[...]
    for copy in copies:
        copy.wait()


def load_step(basis, gen, sent):
    wide = array(*basis.shape[1:])
    return pl.pallas_call(
        load_kernel,
        out_shape=(array(*sent.shape), wide, wide, wide, wide),
        in_specs=[HBM, HBM, VMEM],
        out_specs=(VMEM,) * 5,
        scratch_shapes=[pltpu.SemaphoreType.DMA((4,))],
        compiler_params=params(LIMITS[1]),
        cost_estimate=pl.CostEstimate(flops=1_000, bytes_accessed=8_388_608, transcendentals=0),
        name="load_high",
    )(basis, gen, sent)


G_AT = RHS // 2
G10_AT = G_AT + 2 * RANK
SUM_ROWS = G10_AT + RANK // 4


def ordered(caps_ref, s_high, s_low, high_ref, low_ref):
    for i, (s, columns) in enumerate(((s_high, 2), (s_high, 2), (s_low, 1))):
        for r, row in enumerate((1 - s, s)):
            for c, col in enumerate((s, 1 - s)[:columns]):
                high, low = split(
                    caps_ref[
                        i,
                        pl.ds(pl.multiple_of(row * RANK, RANK), RANK),
                        pl.ds(pl.multiple_of(col * RANK, RANK), RANK),
                    ]
                )
                high_ref[i, r * RANK : (r + 1) * RANK, c * RANK : (c + 1) * RANK] = high
                low_ref[i, r * RANK : (r + 1) * RANK, c * RANK : (c + 1) * RANK] = low


def grams_kernel(rhs_ref, v1_ref, v0_ref, u3_ref, u2_ref, u1_ref, sent_ref, sent_out,
                 keep_ref, send_ref):
    sent_out[...] = sent_ref[...]
    _, bit = position()
    low_half = half_of(bit) == 0
    left = stacked([rhs_ref[...], u3_ref[...]])
    u2 = stacked([u2_ref[...]])
    for k, ref in enumerate((v1_ref, v0_ref)):
        right = stacked([ref[...]])
        cols = slice(k * RANK, (k + 1) * RANK)
        both = fold(contract(left, right), RHS + RANK)
        g2 = fold(contract(u2, right), RANK)
        one, two = both[: RHS // 2], both[RHS // 2 : RHS]
        keep_ref[: RHS // 2, cols] = jnp.where(low_half, one, two)
        send_ref[: RHS // 2, cols] = jnp.where(low_half, two, one)
        for ref in (keep_ref, send_ref):
            ref[G_AT : G_AT + RANK, cols] = both[RHS:]
            ref[G_AT + RANK : G10_AT, cols] = g2
    g10 = fold(contract(stacked([u1_ref[...]]), right), RANK)
    quarter = RANK // 4
    parts = [jnp.concatenate([g10[i * quarter : (i + 1) * quarter] for i in pair], axis=1) for pair in ((0, 1), (2, 3))]
    keep_ref[G10_AT:] = jnp.where(low_half, parts[0], parts[1])
    send_ref[G10_AT:] = jnp.where(low_half, parts[1], parts[0])


def grams_step(rhs, v1, v0, u3, u2, u1, sent):
    return pl.pallas_call(
        grams_kernel,
        out_shape=(
            array(*sent.shape), array(SUM_ROWS, 2 * RANK), array(SUM_ROWS, 2 * RANK),
        ),
        in_specs=[VMEM] * 7,
        out_specs=(VMEM,) * 3,
        compiler_params=params(LIMITS[2]),
        cost_estimate=pl.CostEstimate(flops=3_200_000_000, bytes_accessed=11_534_336, transcendentals=0),
        name="grams_high",
    )(rhs, v1, v0, u3, u2, u1, sent)


def fetch_nodes(cap_ref, nodes, caps_ref, sems):
    copies = [pltpu.make_async_copy(cap_ref.at[n], caps_ref.at[i], sems.at[i]) for i, n in enumerate(nodes)]
    for copy in copies:
        copy.start()
    return copies


def nodes_kernel(cap_ref, sent_ref, sent_out, ch_ref, cl_ref, caps_ref, sems):
    device, bit = position()
    n3, n2 = device >> 4, device >> 5
    copies = fetch_nodes(cap_ref, (7 + n3, 7 + (n3 ^ 1), 3 + n2), caps_ref, sems)
    sent_out[...] = sent_ref[...]
    for copy in copies:
        copy.wait()
    ordered(caps_ref, bit[3], bit[4], ch_ref, cl_ref)


def nodes_step(cap, sent):
    nodes = half_array(3, 2 * RANK, 2 * RANK)
    return pl.pallas_call(
        nodes_kernel,
        out_shape=(array(*sent.shape), nodes, nodes),
        in_specs=[HBM, VMEM],
        out_specs=(VMEM,) * 3,
        scratch_shapes=[pltpu.VMEM((3, 2 * RANK, 2 * RANK), F32), pltpu.SemaphoreType.DMA((3,))],
        compiler_params=params(LIMITS[8]),
        cost_estimate=pl.CostEstimate(flops=1_000, bytes_accessed=786_432, transcendentals=0),
        name="nodes_low",
    )(cap, sent)


def upper(t, g, q, high, low):
    sides = (slice(0, RANK), slice(0, RANK), slice(RANK, 2 * RANK), slice(RANK, 2 * RANK))
    moved = jnp.concatenate([product_of(g[m], high[side], low[side]) for m, side in enumerate(sides)], axis=0)
    joined = jnp.concatenate([q[0] + q[1], q[2] + q[3]], axis=1)
    return product_of(joined, high, low) - product(jnp.concatenate(t, axis=1), moved)


def middle_kernel(mine_ref, other_ref, ch_ref, cl_ref, keep_ref, come_ref, t_ref, part_ref):
    _, bit = position()
    first = half_of(bit) == 0
    p, g = [], []
    for m in range(4):
        mine, other = mine_ref[X_PLACES[m]], other_ref[X_PLACES[m]]
        p.append(jnp.where(first, mine, other))
        g.append(jnp.where(first, other, mine))
    t = []
    for pair in (0, 2):
        joined = jnp.concatenate([p[pair][:RHS], p[pair + 1][:RHS]], axis=1)
        both = product_of(joined, ch_ref[pair // 2], cl_ref[pair // 2])
        t += [both[:, :RANK], both[:, RANK:]]
    above = upper(t, g, [p[m][RHS:] for m in range(4)], ch_ref[2, :, :RANK], cl_ref[2, :, :RANK])
    t_ref[:, :RANK] = t[0]
    t_ref[:, RANK:] = above
    sums = keep_ref[...] + come_ref[...]
    half = RHS // 2
    low_half = half_of(bit) == 0
    grams = sums[G_AT:G10_AT]
    q = sums[:half] - product(jnp.where(low_half, t[0][:half], t[0][half:]), grams[:RANK])
    q = q - product(jnp.where(low_half, above[:half], above[half:]), grams[RANK:])
    part_ref[:half] = q[:, :RANK]
    part_ref[half : 2 * half] = q[:, RANK:]
    quarter = RANK // 4
    part_ref[2 * half : 2 * half + quarter] = sums[G10_AT:, :RANK]
    part_ref[2 * half + quarter :] = sums[G10_AT:, RANK:]


def middle_step(mine, other, ch, cl, keep, come):
    return pl.pallas_call(
        middle_kernel,
        out_shape=(array(RHS, 2 * RANK), array(RANK, RANK)),
        in_specs=[VMEM] * 6,
        out_specs=(VMEM,) * 2,
        compiler_params=params(LIMITS[3]),
        cost_estimate=pl.CostEstimate(flops=120_000_000, bytes_accessed=1_500_000, transcendentals=0),
        name="coefficients_low",
    )(mine, other, ch, cl, keep, come)


def low_update_kernel(t_ref, rhs_ref, u3_ref, u2_ref, sent_ref, cur_ref, sent_out):
    sent_out[...] = sent_ref[...]
    th, tl = split(t_ref[...])
    left = jnp.concatenate([th, tl], axis=0)
    for cols in spans((2,) * 4, rhs_ref.shape[1]):
        gh, gl = split(jnp.concatenate([u3_ref[:, cols], u2_ref[:, cols]], axis=0))
        both = jnp.dot(left, gh, preferred_element_type=F32)
        update = both[:RHS] + both[RHS:] + jnp.dot(th, gl, preferred_element_type=F32)
        cur_ref[:, cols] = rhs_ref[:, cols] - update


def low_update(t, rhs, u3, u2, sent):
    return pl.pallas_call(
        low_update_kernel,
        out_shape=(array(*rhs.shape), array(*sent.shape)),
        in_specs=[VMEM] * 5,
        out_specs=(VMEM, VMEM),
        compiler_params=params(LIMITS[4]),
        cost_estimate=pl.CostEstimate(flops=402_653_184, bytes_accessed=6_291_456, transcendentals=0),
        name="update_low",
    )(t, rhs, u3, u2, sent)


def pairs_kernel(u1_ref, gen_ref, cap_ref, sent_ref, sent_out, high_ref, low_ref, ch_ref, cl_ref,
                 u0_ref, caps_ref, sem, sems):
    copy = pltpu.make_async_copy(gen_ref.at[0], u0_ref, sem)
    copy.start()
    sent_out[...] = sent_ref[...]
    device, bit = position()
    n1 = device >> 6
    copies = fetch_nodes(cap_ref, (1 + n1, 1 + (n1 ^ 1), 0), caps_ref, sems)
    high_ref[:RANK], low_ref[:RANK] = split(u1_ref[...])
    for node in copies:
        node.wait()
    ordered(caps_ref, bit[5], bit[6], ch_ref, cl_ref)
    copy.wait()
    high_ref[RANK:], low_ref[RANK:] = split(u0_ref[...])


def pairs_step(u1, gen, cap, sent):
    pair, nodes = half_array(2 * RANK, u1.shape[1]), half_array(3, 2 * RANK, 2 * RANK)
    return pl.pallas_call(
        pairs_kernel,
        out_shape=(array(*sent.shape), pair, pair, nodes, nodes),
        in_specs=[VMEM, HBM, HBM, VMEM],
        out_specs=(VMEM,) * 5,
        scratch_shapes=[
            pltpu.VMEM(u1.shape, F32), pltpu.VMEM((3, 2 * RANK, 2 * RANK), F32),
            pltpu.SemaphoreType.DMA(()), pltpu.SemaphoreType.DMA((3,)),
        ],
        compiler_params=params(LIMITS[5]),
        cost_estimate=pl.CostEstimate(flops=100_000_000, bytes_accessed=8_388_608, transcendentals=0),
        name="pairs_high",
    )(u1, gen, cap, sent)


def last_kernel(mine_ref, other_ref, ch_ref, cl_ref, cur_ref, high_ref, low_ref, out_ref,
                buf, sems):
    first = half_of(position()[1]) == 0
    half = RHS // 2
    q1, q0, g = [], [], []
    for m in range(4):
        mine, other = mine_ref[Y_PLACES[m]], other_ref[Y_PLACES[m]]
        low = jnp.where(first, mine, other)
        high = jnp.where(first, other, mine)
        q1.append(jnp.concatenate([low[:half], high[:half]], axis=0))
        q0.append(jnp.concatenate([low[half:RHS], high[half:RHS]], axis=0))
        g.append(jnp.concatenate([low[RHS:], high[RHS:]], axis=0))
    t = []
    for pair in (0, 2):
        joined = jnp.concatenate([q1[pair], q1[pair + 1]], axis=1)
        both = product_of(joined, ch_ref[pair // 2], cl_ref[pair // 2])
        t += [both[:, :RANK], both[:, RANK:]]
    above = upper(t, g, q0, ch_ref[2, :, :RANK], cl_ref[2, :, :RANK])
    th, tl = split(jnp.concatenate([t[0], above], axis=1))
    left = jnp.concatenate([th, tl], axis=0)
    copies = []
    for i, cols in enumerate(spans((2,) * 4, cur_ref.shape[1])):
        both = jnp.dot(left, high_ref[:, cols], preferred_element_type=F32)
        update = both[:RHS] + both[RHS:] + jnp.dot(th, low_ref[:, cols], preferred_element_type=F32)
        buf[:, cols] = cur_ref[:, cols] - update
        copy = pltpu.make_async_copy(buf.at[:, cols], out_ref.at[:, cols], sems.at[i])
        copy.start()
        copies.append(copy)
    for copy in copies:
        copy.wait()


def last_step(mine, other, ch, cl, cur, high, low):
    return pl.pallas_call(
        last_kernel,
        out_shape=array(*cur.shape),
        in_specs=[VMEM] * 7,
        out_specs=HBM,
        scratch_shapes=[pltpu.VMEM(cur.shape, F32), pltpu.SemaphoreType.DMA((4,))],
        compiler_params=params(LIMITS[6]),
        cost_estimate=pl.CostEstimate(flops=500_000_000, bytes_accessed=7_000_000, transcendentals=0),
        name="update_high",
    )(mine, other, ch, cl, cur, high, low)


def swap(value, mask):
    return lax.ppermute(value, "leaf", [(i, i ^ mask) for i in range(DEVICES)])


def parity(index):
    return bin(index).count("1") & 1


def crossed(value, even, odd):
    def partner(i):
        mask = odd if parity(i) else even
        return i ^ mask ^ parity(mask)

    return lax.ppermute(value, "leaf", [(i, partner(i)) for i in range(DEVICES)])


def neighbours(value, masks):
    three, two, one = (swap(value, m) for m in masks)
    return one, two, three


def crossed_neighbours(value, even, odd):
    three, two, one = (crossed(value, e, o) for e, o in zip(even, odd))
    return one, two, three


def body(rhs, basis, gen, cap):
    keep, send = first_step(rhs, basis, gen)
    other = swap(send, CORE)
    keep, u1 = early_step(gen, keep)
    chip = keep + other
    b, c, d = crossed_neighbours(chip, Z_MASKS, Z_MASKS)
    chip, v1, v0, u3, u2 = load_step(basis, gen, chip)
    line = chip + b + d + c
    b, c, d = crossed_neighbours(line, X_MASKS, X_MASKS)
    line, keep, send = grams_step(rhs, v1, v0, u3, u2, u1, line)
    come = swap(send, CORE)
    lines = jnp.stack([b, c, d, line])
    other = swap(lines, CORE)
    lines, ch, cl = nodes_step(cap, lines)
    t, chip = middle_step(lines, other, ch, cl, keep, come)
    b, c, d = crossed_neighbours(chip, X_MASKS, Z_MASKS)
    current, chip = low_update(t, rhs, u3, u2, chip)
    part = chip + b + c + d
    b, c, d = crossed_neighbours(part, Z_MASKS, X_MASKS)
    part, high, low, ch, cl = pairs_step(u1, gen, cap, part)
    plane = part + b + c + d
    b, c, d = crossed_neighbours(plane, Y_MASKS, Y_MASKS)
    planes = jnp.stack([b, d, c, plane])
    other = swap(planes, CORE)
    return last_step(planes, other, ch, cl, current, high, low)


def solution(mesh):
    in_specs = (P(None, "leaf"), P(None, None, "leaf"), P(None, None, "leaf"), P())
    return jax.shard_map(body, mesh=mesh, in_specs=in_specs, out_specs=P(None, "leaf"), check_vma=False)
```

```python
import functools

import jax
import jax.numpy as jnp
from jax import lax
from jax.experimental import pallas as pl
from jax.experimental.pallas import tpu as pltpu
from jax.sharding import PartitionSpec as P

F32 = jnp.float32
BF16 = jnp.bfloat16
RANK = 128
RHS = 64
DEVICES = 128
LIMITS = (53, 40, 38, 38, 40, 47, 44, 51, 47)
HBM = pl.BlockSpec(memory_space=pltpu.HBM)
VMEM = pl.BlockSpec(memory_space=pltpu.VMEM)

CORE = 1
Z_MASKS = (6, 4, 2)
X_MASKS = (24, 16, 8)
Y_MASKS = (96, 64, 32)
X_PLACES = (3, 0, 1, 2)
Y_PLACES = (3, 0, 2, 1)


def position():
    device = lax.axis_index("leaf").astype(jnp.int32)
    return device, [device >> k & 1 for k in range(7)]


def half_of(bit):
    return bit[0] ^ bit[1] ^ bit[2] ^ bit[3] ^ bit[4] ^ bit[5] ^ bit[6]


def split(value):
    high = value.astype(BF16)
    return high, (value - high.astype(F32)).astype(BF16)


def stacked(values):
    parts = [split(v) for v in values]
    return jnp.concatenate([h for h, _ in parts] + [l for _, l in parts], axis=0)


def product(left, right):
    lh, ll = split(left)
    rh, rl = split(right)
    rows = left.shape[0]
    both = jnp.dot(jnp.concatenate([lh, ll], axis=0), rh, preferred_element_type=F32)
    return both[:rows] + both[rows:] + jnp.dot(lh, rl, preferred_element_type=F32)


def product_of(left, high, low):
    lh, ll = split(left)
    rows = left.shape[0]
    both = jnp.dot(jnp.concatenate([lh, ll], axis=0), high, preferred_element_type=F32)
    return both[:rows] + both[rows:] + jnp.dot(lh, low, preferred_element_type=F32)


def contract(left, right):
    return lax.dot_general(left, right, (((1,), (1,)), ((), ())), preferred_element_type=F32)


def fold(total, rows):
    half = total.shape[1] // 2
    wide = total[:rows] + total[rows:]
    return wide[:, :half] + wide[:, half:]


def params(limit):
    return pltpu.CompilerParams(vmem_limit_bytes=limit << 20)


def spans(sizes, points):
    at = 0
    for size in sizes:
        yield pl.ds(at * points // 8, size * points // 8)
        at += size


def fetch(sources, sems, sizes, points):
    parts = []
    for i, cols in enumerate(spans(sizes, points)):
        row = []
        for j, (ref, level, buffer) in enumerate(sources):
            src = ref.at[:, cols] if level is None else ref.at[level, :, cols]
            row.append(pltpu.make_async_copy(src, buffer.at[:, cols], sems.at[i, j]))
        parts.append((cols, row))
    for _, row in parts:
        for copy in row:
            copy.start()
    return parts


def add_to(acc, value, first):
    if first:
        acc[...] = value
    else:
        acc[...] += value


PARTS = (2, 2, 2, 2)


def first_kernel(points, rhs_ref, basis_ref, gen_ref, keep_ref, send_ref,
                 rhs_buf, v3_buf, v2_buf, u3_buf, acc2, acc3, sems):
    sources = ((rhs_ref, None, rhs_buf), (basis_ref, 3, v3_buf), (basis_ref, 2, v2_buf), (gen_ref, 3, u3_buf))
    for i, (cols, row) in enumerate(fetch(sources, sems, PARTS, points)):
        for copy in row:
            copy.wait()
        rhs = stacked([rhs_buf[:, cols]])
        left = jnp.concatenate([rhs, stacked([u3_buf[:, cols]])], axis=0)
        add_to(acc2, contract(left, stacked([v2_buf[:, cols]])), i == 0)
        add_to(acc3, contract(rhs, stacked([v3_buf[:, cols]])), i == 0)
    p3 = fold(acc3[...], RHS)
    p2 = fold(acc2[: 2 * RHS], RHS)
    g32 = fold(acc2[2 * RHS :], RANK)
    first = half_of(position()[1]) == 0

    @pl.when(first)
    def _():
        keep_ref[:RHS] = p3
        keep_ref[RHS:] = p2
        send_ref[...] = g32

    @pl.when(jnp.logical_not(first))
    def _():
        send_ref[:RHS] = p3
        send_ref[RHS:] = p2
        keep_ref[...] = g32


def array(*shape):
    return jax.ShapeDtypeStruct(shape, F32)


def half_array(*shape):
    return jax.ShapeDtypeStruct(shape, BF16)


def first_step(rhs, basis, gen):
    points = rhs.shape[1]
    wide = pltpu.VMEM((RANK, points), F32)
    return pl.pallas_call(
        functools.partial(first_kernel, points),
        out_shape=(array(RANK, RANK), array(RANK, RANK)),
        in_specs=[HBM, HBM, HBM],
        out_specs=(VMEM,) * 2,
        scratch_shapes=[
            pltpu.VMEM((RHS, points), F32), wide, wide, wide,
            pltpu.VMEM((2 * (RHS + RANK), 2 * RANK), F32),
            pltpu.VMEM((2 * RHS, 2 * RANK), F32),
            pltpu.SemaphoreType.DMA((len(PARTS), 4)),
        ],
        compiler_params=params(LIMITS[0]),
        cost_estimate=pl.CostEstimate(flops=800_000_000, bytes_accessed=7_340_032, transcendentals=0),
        name="project_low",
    )(rhs, basis, gen)


def early_kernel(gen_ref, sent_ref, sent_out, u1_ref, sem):
    copy = pltpu.make_async_copy(gen_ref.at[1, :RHS], u1_ref, sem)
    copy.start()
    sent_out[...] = sent_ref[...]
    copy.wait()


def early_step(gen, sent):
    return pl.pallas_call(
        early_kernel,
        out_shape=(array(*sent.shape), array(RHS, gen.shape[2])),
        in_specs=[HBM, VMEM],
        out_specs=(VMEM, VMEM),
        scratch_shapes=[pltpu.SemaphoreType.DMA(())],
        compiler_params=params(LIMITS[7]),
        cost_estimate=pl.CostEstimate(flops=1_000, bytes_accessed=1_048_576, transcendentals=0),
        name="load_early",
    )(gen, sent)


def load_kernel(basis_ref, gen_ref, sent_ref, sent_out, v1_ref, v0_ref, u3_ref, u2_ref, rest_ref, sems):
    sources = [
        (basis_ref, 1, v1_ref), (basis_ref, 0, v0_ref),
        (gen_ref, 3, u3_ref), (gen_ref, 2, u2_ref),
    ]
    copies = [pltpu.make_async_copy(ref.at[k], out, sems.at[i]) for i, (ref, k, out) in enumerate(sources)]
    copies.append(pltpu.make_async_copy(gen_ref.at[1, RHS:], rest_ref, sems.at[4]))
    for copy in copies:
        copy.start()
    sent_out[...] = sent_ref[...]
    for copy in copies:
        copy.wait()


def load_step(basis, gen, sent):
    wide = array(*basis.shape[1:])
    return pl.pallas_call(
        load_kernel,
        out_shape=(array(*sent.shape), wide, wide, wide, wide, array(RHS, basis.shape[2])),
        in_specs=[HBM, HBM, VMEM],
        out_specs=(VMEM,) * 6,
        scratch_shapes=[pltpu.SemaphoreType.DMA((5,))],
        compiler_params=params(LIMITS[1]),
        cost_estimate=pl.CostEstimate(flops=1_000, bytes_accessed=8_388_608, transcendentals=0),
        name="load_high",
    )(basis, gen, sent)


G_AT = RHS // 2
G10_AT = G_AT + 2 * RANK
SUM_ROWS = G10_AT + RANK // 4


def ordered(caps_ref, s_high, s_low, high_ref, low_ref):
    for i, (s, columns) in enumerate(((s_high, 2), (s_high, 2), (s_low, 1))):
        for r, row in enumerate((1 - s, s)):
            for c, col in enumerate((s, 1 - s)[:columns]):
                high, low = split(
                    caps_ref[
                        i,
                        pl.ds(pl.multiple_of(row * RANK, RANK), RANK),
                        pl.ds(pl.multiple_of(col * RANK, RANK), RANK),
                    ]
                )
                high_ref[i, r * RANK : (r + 1) * RANK, c * RANK : (c + 1) * RANK] = high
                low_ref[i, r * RANK : (r + 1) * RANK, c * RANK : (c + 1) * RANK] = low


def grams_kernel(rhs_ref, v1_ref, v0_ref, u3_ref, u2_ref, u1_ref, rest_ref, sent_ref, sent_out,
                 keep_ref, send_ref):
    sent_out[...] = sent_ref[...]
    _, bit = position()
    low_half = half_of(bit) == 0
    left = stacked([rhs_ref[...], u3_ref[...]])
    u2 = stacked([u2_ref[...]])
    for k, ref in enumerate((v1_ref, v0_ref)):
        right = stacked([ref[...]])
        cols = slice(k * RANK, (k + 1) * RANK)
        both = fold(contract(left, right), RHS + RANK)
        g2 = fold(contract(u2, right), RANK)
        one, two = both[: RHS // 2], both[RHS // 2 : RHS]
        keep_ref[: RHS // 2, cols] = jnp.where(low_half, one, two)
        send_ref[: RHS // 2, cols] = jnp.where(low_half, two, one)
        for ref in (keep_ref, send_ref):
            ref[G_AT : G_AT + RANK, cols] = both[RHS:]
            ref[G_AT + RANK : G10_AT, cols] = g2
    g10 = fold(contract(stacked([u1_ref[...], rest_ref[...]]), right), RANK)
    quarter = RANK // 4
    parts = [jnp.concatenate([g10[i * quarter : (i + 1) * quarter] for i in pair], axis=1) for pair in ((0, 1), (2, 3))]
    keep_ref[G10_AT:] = jnp.where(low_half, parts[0], parts[1])
    send_ref[G10_AT:] = jnp.where(low_half, parts[1], parts[0])


def grams_step(rhs, v1, v0, u3, u2, u1, rest, sent):
    return pl.pallas_call(
        grams_kernel,
        out_shape=(
            array(*sent.shape), array(SUM_ROWS, 2 * RANK), array(SUM_ROWS, 2 * RANK),
        ),
        in_specs=[VMEM] * 8,
        out_specs=(VMEM,) * 3,
        compiler_params=params(LIMITS[2]),
        cost_estimate=pl.CostEstimate(flops=3_200_000_000, bytes_accessed=11_534_336, transcendentals=0),
        name="grams_high",
    )(rhs, v1, v0, u3, u2, u1, rest, sent)


def fetch_nodes(cap_ref, nodes, caps_ref, sems):
    copies = [pltpu.make_async_copy(cap_ref.at[n], caps_ref.at[i], sems.at[i]) for i, n in enumerate(nodes)]
    for copy in copies:
        copy.start()
    return copies


def nodes_kernel(cap_ref, sent_ref, sent_out, ch_ref, cl_ref, caps_ref, sems):
    device, bit = position()
    n3, n2 = device >> 4, device >> 5
    copies = fetch_nodes(cap_ref, (7 + n3, 7 + (n3 ^ 1), 3 + n2), caps_ref, sems)
    sent_out[...] = sent_ref[...]
    for copy in copies:
        copy.wait()
    ordered(caps_ref, bit[3], bit[4], ch_ref, cl_ref)


def nodes_step(cap, sent):
    nodes = half_array(3, 2 * RANK, 2 * RANK)
    return pl.pallas_call(
        nodes_kernel,
        out_shape=(array(*sent.shape), nodes, nodes),
        in_specs=[HBM, VMEM],
        out_specs=(VMEM,) * 3,
        scratch_shapes=[pltpu.VMEM((3, 2 * RANK, 2 * RANK), F32), pltpu.SemaphoreType.DMA((3,))],
        compiler_params=params(LIMITS[8]),
        cost_estimate=pl.CostEstimate(flops=1_000, bytes_accessed=786_432, transcendentals=0),
        name="nodes_low",
    )(cap, sent)


def upper(t, g, q, high, low):
    sides = (slice(0, RANK), slice(0, RANK), slice(RANK, 2 * RANK), slice(RANK, 2 * RANK))
    moved = jnp.concatenate([product_of(g[m], high[side], low[side]) for m, side in enumerate(sides)], axis=0)
    joined = jnp.concatenate([q[0] + q[1], q[2] + q[3]], axis=1)
    return product_of(joined, high, low) - product(jnp.concatenate(t, axis=1), moved)


def middle_kernel(mine_ref, other_ref, ch_ref, cl_ref, keep_ref, come_ref, t_ref, part_ref):
    _, bit = position()
    first = half_of(bit) == 0
    p, g = [], []
    for m in range(4):
        mine, other = mine_ref[X_PLACES[m]], other_ref[X_PLACES[m]]
        p.append(jnp.where(first, mine, other))
        g.append(jnp.where(first, other, mine))
    t = []
    for pair in (0, 2):
        joined = jnp.concatenate([p[pair][:RHS], p[pair + 1][:RHS]], axis=1)
        both = product_of(joined, ch_ref[pair // 2], cl_ref[pair // 2])
        t += [both[:, :RANK], both[:, RANK:]]
    above = upper(t, g, [p[m][RHS:] for m in range(4)], ch_ref[2, :, :RANK], cl_ref[2, :, :RANK])
    t_ref[:, :RANK] = t[0]
    t_ref[:, RANK:] = above
    sums = keep_ref[...] + come_ref[...]
    half = RHS // 2
    low_half = half_of(bit) == 0
    grams = sums[G_AT:G10_AT]
    q = sums[:half] - product(jnp.where(low_half, t[0][:half], t[0][half:]), grams[:RANK])
    q = q - product(jnp.where(low_half, above[:half], above[half:]), grams[RANK:])
    part_ref[:half] = q[:, :RANK]
    part_ref[half : 2 * half] = q[:, RANK:]
    quarter = RANK // 4
    part_ref[2 * half : 2 * half + quarter] = sums[G10_AT:, :RANK]
    part_ref[2 * half + quarter :] = sums[G10_AT:, RANK:]


def middle_step(mine, other, ch, cl, keep, come):
    return pl.pallas_call(
        middle_kernel,
        out_shape=(array(RHS, 2 * RANK), array(RANK, RANK)),
        in_specs=[VMEM] * 6,
        out_specs=(VMEM,) * 2,
        compiler_params=params(LIMITS[3]),
        cost_estimate=pl.CostEstimate(flops=120_000_000, bytes_accessed=1_500_000, transcendentals=0),
        name="coefficients_low",
    )(mine, other, ch, cl, keep, come)


def low_update_kernel(t_ref, rhs_ref, u3_ref, u2_ref, sent_ref, cur_ref, sent_out):
    sent_out[...] = sent_ref[...]
    th, tl = split(t_ref[...])
    left = jnp.concatenate([th, tl], axis=0)
    for cols in spans((2,) * 4, rhs_ref.shape[1]):
        gh, gl = split(jnp.concatenate([u3_ref[:, cols], u2_ref[:, cols]], axis=0))
        both = jnp.dot(left, gh, preferred_element_type=F32)
        update = both[:RHS] + both[RHS:] + jnp.dot(th, gl, preferred_element_type=F32)
        cur_ref[:, cols] = rhs_ref[:, cols] - update


def low_update(t, rhs, u3, u2, sent):
    return pl.pallas_call(
        low_update_kernel,
        out_shape=(array(*rhs.shape), array(*sent.shape)),
        in_specs=[VMEM] * 5,
        out_specs=(VMEM, VMEM),
        compiler_params=params(LIMITS[4]),
        cost_estimate=pl.CostEstimate(flops=402_653_184, bytes_accessed=6_291_456, transcendentals=0),
        name="update_low",
    )(t, rhs, u3, u2, sent)


def pairs_kernel(u1_ref, rest_ref, gen_ref, cap_ref, sent_ref, sent_out, high_ref, low_ref, ch_ref, cl_ref,
                 u0_ref, caps_ref, sem, sems):
    copy = pltpu.make_async_copy(gen_ref.at[0], u0_ref, sem)
    copy.start()
    sent_out[...] = sent_ref[...]
    device, bit = position()
    n1 = device >> 6
    copies = fetch_nodes(cap_ref, (1 + n1, 1 + (n1 ^ 1), 0), caps_ref, sems)
    high_ref[:RHS], low_ref[:RHS] = split(u1_ref[...])
    high_ref[RHS:RANK], low_ref[RHS:RANK] = split(rest_ref[...])
    for node in copies:
        node.wait()
    ordered(caps_ref, bit[5], bit[6], ch_ref, cl_ref)
    copy.wait()
    high_ref[RANK:], low_ref[RANK:] = split(u0_ref[...])


def pairs_step(u1, rest, gen, cap, sent):
    pair, nodes = half_array(2 * RANK, u1.shape[1]), half_array(3, 2 * RANK, 2 * RANK)
    return pl.pallas_call(
        pairs_kernel,
        out_shape=(array(*sent.shape), pair, pair, nodes, nodes),
        in_specs=[VMEM, VMEM, HBM, HBM, VMEM],
        out_specs=(VMEM,) * 5,
        scratch_shapes=[
            pltpu.VMEM((RANK, u1.shape[1]), F32), pltpu.VMEM((3, 2 * RANK, 2 * RANK), F32),
            pltpu.SemaphoreType.DMA(()), pltpu.SemaphoreType.DMA((3,)),
        ],
        compiler_params=params(LIMITS[5]),
        cost_estimate=pl.CostEstimate(flops=100_000_000, bytes_accessed=8_388_608, transcendentals=0),
        name="pairs_high",
    )(u1, rest, gen, cap, sent)


def last_kernel(mine_ref, other_ref, ch_ref, cl_ref, cur_ref, high_ref, low_ref, out_ref,
                buf, sems):
    first = half_of(position()[1]) == 0
    half = RHS // 2
    q1, q0, g = [], [], []
    for m in range(4):
        mine, other = mine_ref[Y_PLACES[m]], other_ref[Y_PLACES[m]]
        low = jnp.where(first, mine, other)
        high = jnp.where(first, other, mine)
        q1.append(jnp.concatenate([low[:half], high[:half]], axis=0))
        q0.append(jnp.concatenate([low[half:RHS], high[half:RHS]], axis=0))
        g.append(jnp.concatenate([low[RHS:], high[RHS:]], axis=0))
    t = []
    for pair in (0, 2):
        joined = jnp.concatenate([q1[pair], q1[pair + 1]], axis=1)
        both = product_of(joined, ch_ref[pair // 2], cl_ref[pair // 2])
        t += [both[:, :RANK], both[:, RANK:]]
    above = upper(t, g, q0, ch_ref[2, :, :RANK], cl_ref[2, :, :RANK])
    th, tl = split(jnp.concatenate([t[0], above], axis=1))
    left = jnp.concatenate([th, tl], axis=0)
    copies = []
    for i, cols in enumerate(spans((2,) * 4, cur_ref.shape[1])):
        both = jnp.dot(left, high_ref[:, cols], preferred_element_type=F32)
        update = both[:RHS] + both[RHS:] + jnp.dot(th, low_ref[:, cols], preferred_element_type=F32)
        buf[:, cols] = cur_ref[:, cols] - update
        copy = pltpu.make_async_copy(buf.at[:, cols], out_ref.at[:, cols], sems.at[i])
        copy.start()
        copies.append(copy)
    for copy in copies:
        copy.wait()


def last_step(mine, other, ch, cl, cur, high, low):
    return pl.pallas_call(
        last_kernel,
        out_shape=array(*cur.shape),
        in_specs=[VMEM] * 7,
        out_specs=HBM,
        scratch_shapes=[pltpu.VMEM(cur.shape, F32), pltpu.SemaphoreType.DMA((4,))],
        compiler_params=params(LIMITS[6]),
        cost_estimate=pl.CostEstimate(flops=500_000_000, bytes_accessed=7_000_000, transcendentals=0),
        name="update_high",
    )(mine, other, ch, cl, cur, high, low)


def swap(value, mask):
    return lax.ppermute(value, "leaf", [(i, i ^ mask) for i in range(DEVICES)])


def parity(index):
    return bin(index).count("1") & 1


def crossed(value, even, odd):
    def partner(i):
        mask = odd if parity(i) else even
        return i ^ mask ^ parity(mask)

    return lax.ppermute(value, "leaf", [(i, partner(i)) for i in range(DEVICES)])


def neighbours(value, masks):
    three, two, one = (swap(value, m) for m in masks)
    return one, two, three


def crossed_neighbours(value, even, odd):
    three, two, one = (crossed(value, e, o) for e, o in zip(even, odd))
    return one, two, three


def body(rhs, basis, gen, cap):
    keep, send = first_step(rhs, basis, gen)
    other = swap(send, CORE)
    keep, u1 = early_step(gen, keep)
    chip = keep + other
    b, c, d = crossed_neighbours(chip, Z_MASKS, Z_MASKS)
    chip, v1, v0, u3, u2, rest = load_step(basis, gen, chip)
    line = chip + b + d + c
    b, c, d = crossed_neighbours(line, X_MASKS, X_MASKS)
    line, keep, send = grams_step(rhs, v1, v0, u3, u2, u1, rest, line)
    come = swap(send, CORE)
    lines = jnp.stack([b, c, d, line])
    other = swap(lines, CORE)
    lines, ch, cl = nodes_step(cap, lines)
    t, chip = middle_step(lines, other, ch, cl, keep, come)
    b, c, d = crossed_neighbours(chip, X_MASKS, Z_MASKS)
    current, chip = low_update(t, rhs, u3, u2, chip)
    part = chip + b + c + d
    b, c, d = crossed_neighbours(part, Z_MASKS, X_MASKS)
    part, high, low, ch, cl = pairs_step(u1, rest, gen, cap, part)
    plane = part + b + c + d
    b, c, d = crossed_neighbours(plane, Y_MASKS, Y_MASKS)
    planes = jnp.stack([b, d, c, plane])
    other = swap(planes, CORE)
    return last_step(planes, other, ch, cl, current, high, low)


def solution(mesh):
    in_specs = (P(None, "leaf"), P(None, None, "leaf"), P(None, None, "leaf"), P())
    return jax.shard_map(body, mesh=mesh, in_specs=in_specs, out_specs=P(None, "leaf"), check_vma=False)
```
